32 devices in a mesh: freq: 4 (over x, core), vis: 8 (over z, y).
Axes of the slice: x: 2, y: 2, z: 4, core: 2. Of those that a mesh axis runs over, the one named last changes fastest.
Arguments:
- model_input: bfloat16 [2, 16, 512, 512], P(None, 'freq', 'vis'), parts along dimension 1, may hold values from -6 to 6
- w_kernels: bfloat16 [64, 2, 128, 128], P('freq'), parts along dimension 0, may hold values from -0.375 to 0.375
- visibilities: bfloat16 [1024, 2, 128, 128], P(('freq', 'vis')), parts along dimension 0, may hold values from -6 to 6
- tile_facet: int32 [1024], P(('freq', 'vis')), parts along dimension 0, may hold values from 0 to 3
- tile_patch: int32 [1024], P(('freq', 'vis')), parts along dimension 0, may hold values from 0 to 15
- tile_wplane: int32 [1024], P(('freq', 'vis')), parts along dimension 0, may hold values from 0 to 15
- tile_count: int32 [32], P(('freq', 'vis')), parts along dimension 0, may hold values from 16 to 32, as said below
Outputs:
- residual_image: float32 [16, 512, 512], P('freq', 'vis'), parts along dimension 0
The draws below stay inside these ranges and needn't reach their ends.
There are 4 independent parts, one for each index of `freq`. The reference program is written for one: setup_inputs(seed, part) draws one part's arguments, and reference() takes and returns one part's arrays. A program takes and returns all parts, laid end to end along the dimension named above; each array names one. Nothing has to cross between parts.
Inputs may be any that keep to these rules, and one draw needn't show every extreme that they name: `tile_count`: each device's live tiles fill its first slots; some device holds exactly 32.
All inputs are finite; a program needn't handle non-finite values.
Results may differ from the reference program's by a relative error of at most 0.02.
Values may be sent and summed in bfloat16 or wider, within the bound.
No kernel may reach another device: no remote copies, remote signals or barrier semaphores. Data moves between devices by JAX's collectives and lax.ppermute only.
A program may use at most 128 MiB of HBM per device.

```python
import math
import jax
import jax.numpy as jnp
from jax import lax

P_SIZE = 512
S = 128
F = 4
WPLANES = 16
CYCLES = 2
TILE_CAP = 32
NP = 16
TILES = 256


def draw_tile_count(key, part):
    devices = TILES // TILE_CAP
    draw_one, draw_two = jax.random.split(key)
    counts = jax.random.randint(draw_one, (devices,), TILE_CAP // 2, TILE_CAP + 1)
    busiest = jax.random.randint(draw_two, (), 0, devices)
    return jnp.where(jnp.arange(devices) == busiest, TILE_CAP, counts).astype(jnp.int32)


def place_ends(array, rng, smallest, largest):
    longest = array.shape.index(max(array.shape))
    spots = []
    for shift in (0, 1):
        where = [jax.random.randint(jax.random.fold_in(rng, axis), (), 0, length) for axis, length in enumerate(array.shape)]
        where[longest] = (where[longest] + shift) % array.shape[longest]
        spots.append(tuple(where))
    return array.at[spots[0]].set(smallest).at[spots[1]].set(largest)


def level_of(own_key, shape, pieces, low, high):
    def one(axis_at, parts):
        heights = jax.random.uniform(jax.random.fold_in(jax.random.fold_in(own_key, 6), axis_at), (parts,), jnp.float32, low / len(pieces), high / len(pieces))
        return jnp.repeat(jnp.exp(heights), shape[axis_at] // parts).reshape((-1,) + (1,) * (len(shape) - axis_at - 1))

    loudness = one(*pieces[0])
    for cut in pieces[1:]:
        loudness = loudness * one(*cut)
    return loudness


def centred(own_key, extent, scale, bound, pieces=(), kind=jnp.bfloat16):
    level = level_of(own_key, extent, pieces, -0.22, 0.18) if pieces else 1.0
    result = jax.random.normal(own_key, extent, jnp.float32) * scale * level
    return jnp.minimum(jnp.maximum(result, -bound), bound).astype(kind)


def setup_inputs(seed: int = 0, part: int = 0) -> dict:
    keys = jax.random.split(jax.random.key(seed), 8)
    part_splits = jax.random.split(jax.random.fold_in(keys[7], part), 8)
    model_input = centred(part_splits[0], (CYCLES, F, P_SIZE, P_SIZE), 1.0, 6.0, ((2, 8),))
    w_kernels = centred(part_splits[1], (WPLANES, 2, S, S), (2 * S) ** -0.5, 0.375)
    visibilities = centred(part_splits[2], (TILES, 2, S, S), 1.0, 6.0, ((0, 8),))
    tile_facet = place_ends(jax.random.randint(part_splits[3], (TILES,), 0, F), jax.random.fold_in(part_splits[3], 1), 0, F - 1).astype(jnp.int32)
    tile_patch = place_ends(jax.random.randint(part_splits[4], (TILES,), 0, NP), jax.random.fold_in(part_splits[4], 1), 0, NP - 1).astype(jnp.int32)
    tile_wplane = place_ends(jax.random.randint(part_splits[5], (TILES,), 0, WPLANES), jax.random.fold_in(part_splits[5], 1), 0, WPLANES - 1).astype(jnp.int32)
    tile_count = draw_tile_count(jax.random.fold_in(jax.random.fold_in(keys[7], part), 71), part)
    return dict(model_input=model_input, w_kernels=w_kernels, visibilities=visibilities, tile_facet=tile_facet, tile_patch=tile_patch, tile_wplane=tile_wplane, tile_count=tile_count)


loop_gain = 0.5

def dft_tables(first_row, row_count, length):
    row_ids = first_row + jnp.arange(row_count, dtype=jnp.int32)
    col_ids = jnp.arange(length, dtype=jnp.int32)
    phases = row_ids[:, None] * col_ids[None, :] % length
    angles = phases.astype(jnp.float32) * (2.0 * math.pi / length)
    scaling = 1.0 / math.sqrt(length)
    return (jnp.cos(angles) * scaling, jnp.sin(angles) * scaling)

def product(pattern, first_op, second_op):
    return jnp.einsum(pattern, first_op, second_op, precision=lax.Precision.HIGHEST)

def to_half(value):
    return lax.optimization_barrier(value.astype(jnp.bfloat16)).astype(jnp.float32)

def tile_terms(patches, kernel, observed, alive):
    patch_real, patch_imag = (patches[:, 0], patches[:, 1])
    kern_real, kern_imag = (kernel[:, 0], kernel[:, 1])
    mid_real = to_half(product('tij,tjk->tik', kern_real, patch_real) - product('tij,tjk->tik', kern_imag, patch_imag))
    mid_imag = to_half(product('tij,tjk->tik', kern_real, patch_imag) + product('tij,tjk->tik', kern_imag, patch_real))
    model_real = product('tij,tkj->tik', mid_real, kern_real) - product('tij,tkj->tik', mid_imag, kern_imag)
    model_imag = product('tij,tkj->tik', mid_real, kern_imag) + product('tij,tkj->tik', mid_imag, kern_real)
    resid_real = to_half((observed[:, 0] - model_real) * alive[:, None, None])
    resid_imag = to_half((observed[:, 1] - model_imag) * alive[:, None, None])
    back_real = to_half(product('tji,tjk->tik', kern_real, resid_real) + product('tji,tjk->tik', kern_imag, resid_imag))
    back_imag = to_half(product('tji,tjk->tik', kern_real, resid_imag) - product('tji,tjk->tik', kern_imag, resid_real))
    out_real = product('tij,tjk->tik', back_real, kern_real) + product('tij,tjk->tik', back_imag, kern_imag)
    out_imag = product('tij,tjk->tik', back_imag, kern_real) - product('tij,tjk->tik', back_real, kern_imag)
    return jnp.stack([out_real, out_imag], axis=1)

def reference(model_input, w_kernels, visibilities, tile_facet, tile_patch, tile_wplane, tile_count):
    devices = TILES // TILE_CAP
    cosine, sine = dft_tables(0, P_SIZE, P_SIZE)
    cosine_half = cosine.astype(jnp.bfloat16).astype(jnp.float32)
    sine_half = sine.astype(jnp.bfloat16).astype(jnp.float32)
    slots = (tile_facet * NP + tile_patch).astype(jnp.int32)
    alive = (jnp.arange(TILE_CAP, dtype=jnp.int32)[None, :] < tile_count[:, None]).astype(jnp.float32).reshape(TILES)
    weight = math.sqrt(F * NP / TILES)
    kernels = w_kernels.astype(jnp.float32)
    residual_image = jnp.zeros((F, P_SIZE, P_SIZE), jnp.float32)
    for cycle_index in range(CYCLES):
        if cycle_index == 0:
            sky_model = model_input[0].astype(jnp.float32)
        else:
            sky_model = to_half(model_input[cycle_index].astype(jnp.float32) + loop_gain * residual_image)
        half_real = to_half(product('fij,jk->fik', sky_model, cosine_half))
        half_imag = to_half(-product('fij,jk->fik', sky_model, sine_half))
        grid_real = to_half(product('ij,fjk->fik', cosine_half, half_real) + product('ij,fjk->fik', sine_half, half_imag))
        grid_imag = to_half(product('ij,fjk->fik', cosine_half, half_imag) - product('ij,fjk->fik', sine_half, half_real))
        full_grid = jnp.stack([grid_real, grid_imag], axis=1)
        patch_table = full_grid.reshape(F, 2, P_SIZE // S, S, P_SIZE // S, S).transpose(0, 2, 4, 1, 3, 5).reshape(F * NP, 2, S, S)

        def accumulate(running, tile_block):
            slot_ids, plane_ids, observed, live_block = tile_block
            tile_sums = tile_terms(patch_table[slot_ids], kernels[plane_ids], observed.astype(jnp.float32), live_block)
            return (running.at[slot_ids].add(tile_sums), None)
        blocks = (slots.reshape(devices, TILE_CAP), tile_wplane.reshape(devices, TILE_CAP), visibilities.reshape(devices, TILE_CAP, 2, S, S), alive.reshape(devices, TILE_CAP))
        summed, unused = lax.scan(accumulate, jnp.zeros((F * NP, 2, S, S), jnp.float32), blocks)
        resid_grid = summed.reshape(F, P_SIZE // S, P_SIZE // S, 2, S, S).transpose(0, 3, 1, 4, 2, 5).reshape(F, 2, P_SIZE, P_SIZE)
        spec_real = product('ij,fjk->fik', cosine, resid_grid[:, 0]) - product('ij,fjk->fik', sine, resid_grid[:, 1])
        spec_imag = product('ij,fjk->fik', cosine, resid_grid[:, 1]) + product('ij,fjk->fik', sine, resid_grid[:, 0])
        residual_image = (product('fij,jk->fik', spec_real, cosine) - product('fij,jk->fik', spec_imag, sine)) * weight
    return residual_image
```

```python
import functools
import math

import jax
import jax.numpy as jnp
import ml_dtypes
import numpy as np
from jax import lax
from jax.experimental import pallas as pl
from jax.experimental.pallas import tpu as pltpu
from jax.sharding import PartitionSpec as P

P_SIZE = 512
S = 128
F = 4
WPLANES = 16
TILE_CAP = 32
NP = 16
SIDE = P_SIZE // S
PAIR = 2 * S
UNROLL = 2
GAIN = 0.5
VMEM_BYTES = 48 * 1024 * 1024

BF16 = jnp.bfloat16
F32 = jnp.float32


def angle_tables():
    index = np.arange(P_SIZE)
    angles = (index[:, None] * index[None, :] % P_SIZE) * (2.0 * np.pi / P_SIZE)
    return np.cos(angles) / np.sqrt(P_SIZE), np.sin(angles) / np.sqrt(P_SIZE)


def half(array):
    return np.asarray(array, np.float32).astype(ml_dtypes.bfloat16)


def complex_block(real, imag):
    return np.block([[real, -imag], [imag, real]])


def row_table():
    cosine, sine = angle_tables()
    parts = [cosine.reshape(P_SIZE, SIDE, 1, S), -sine.reshape(P_SIZE, SIDE, 1, S)]
    return half(np.concatenate(parts, axis=2).reshape(P_SIZE, 2 * P_SIZE))


def column_tables(devices):
    cosine, sine = angle_tables()
    rows = P_SIZE // devices
    parts = [t.reshape(P_SIZE, devices, rows).transpose(1, 0, 2) for t in (cosine, sine)]
    return half(np.concatenate(parts, axis=2))


def flip_tables():
    small = np.zeros((S, S))
    for k in range(1, S):
        small[S - k, k] = 1.0
    zero = np.zeros((S, S))
    lanes = np.block([[small, zero], [zero, -small]])
    rows = np.zeros((PAIR, PAIR))
    for i in range(1, PAIR):
        rows[i, PAIR - i] = 1.0
    return half(lanes), half(rows)


def inverse_row_tables():
    a, i = np.arange(S)[:, None], np.arange(S)[None, :]
    blocks = []
    for q in range(SIDE):
        angles = ((SIDE * a + q) * i % P_SIZE) * (2.0 * np.pi / P_SIZE)
        blocks.append(complex_block(np.cos(angles), np.sin(angles)) / np.sqrt(P_SIZE))
    return half(np.stack(blocks))


def inverse_column_table(weight):
    cosine, sine = angle_tables()
    parts = [cosine.reshape(SIDE, 1, S, P_SIZE), -sine.reshape(SIDE, 1, S, P_SIZE)]
    return half(np.concatenate(parts, axis=1).reshape(2 * P_SIZE, P_SIZE) * weight)


def dot(a, b):
    return jnp.dot(a, b, preferred_element_type=F32)


def restack(pair):
    top = jnp.concatenate([pair[:S, :S], pair[S:, :S]], axis=1)
    bottom = jnp.concatenate([pair[:S, S:], pair[S:, S:]], axis=1)
    return jnp.concatenate([top, bottom], axis=0)


def prep_kernel(slot_ref, plane_ref, count_ref, wk_ref, vis_ref, sky_ref, row_ref, gram_ref, back_ref, half_ref, kern, kern_t, acc):
    for w in range(WPLANES):
        real, imag = wk_ref[w, 0], wk_ref[w, 1]
        block = jnp.concatenate(
            [jnp.concatenate([real, -imag], axis=1), jnp.concatenate([imag, real], axis=1)], axis=0
        )
        real_t = real.astype(F32).T.astype(BF16)
        imag_t = imag.astype(F32).T.astype(BF16)
        block_t = jnp.concatenate(
            [jnp.concatenate([real_t, imag_t], axis=1), jnp.concatenate([-imag_t, real_t], axis=1)], axis=0
        )
        kern[w] = block
        kern_t[w] = block_t
        gram_ref[w] = dot(block_t, block).astype(BF16)

    half_ref[...] = dot(sky_ref[...], row_ref[...]).astype(BF16)

    acc[...] = jnp.zeros_like(acc)
    count = count_ref[0]

    def tiles(step, carry):
        for lane in range(4):
            t = step * 4 + lane
            slot, w = slot_ref[t], plane_ref[t]
            alive = jnp.where(t < count, 1.0, 0.0).astype(F32)
            observed = jnp.concatenate([vis_ref[t, 0], vis_ref[t, 1]], axis=1)
            right = (dot(observed, kern[w]) * alive).astype(BF16)
            stacked = jnp.concatenate([right[:, :S], right[:, S:]], axis=0)
            both = dot(kern_t[w], stacked)
            term = jnp.concatenate([both[:S], both[S:]], axis=1)
            facet, patch = slot >> 4, slot & (NP - 1)
            row = pl.multiple_of((patch >> 2) * S, S)
            place = (facet, patch & 3, pl.ds(row, S))
            acc[place] = acc[place] + term
        return carry

    lax.fori_loop(0, (count + 3) // 4, tiles, 0)
    for f in range(F):
        back_ref[f] = acc[f].astype(BF16)


def degrid_grid(items_ref, base, count, gram_ref, grid_ref, acc):
    def step(n, carry):
        for lane in range(UNROLL):
            code = items_ref[base + n * UNROLL + lane]
            w = code & (WPLANES - 1)
            first, second = (code >> 4) & 31, (code >> 9) & 31

            def read(slot):
                row = pl.multiple_of(((slot >> 2) & 3) * S, S)
                return grid_ref[slot & 3, pl.ds(row, S)]

            gram = gram_ref[w]
            pair = jnp.concatenate([read(first), read(second)], axis=0)
            right = dot(pair, gram).astype(BF16)
            both = dot(gram, restack(right))
            for k, slot in enumerate((first, second)):
                cols = slice(k * S, (k + 1) * S)
                term = jnp.concatenate([both[:S, cols], both[S:, cols]], axis=1)
                place = (slot & 3, pl.ds(pl.multiple_of((slot >> 2) * S, S), S))
                acc[place] = acc[place] - term
        return carry

    lax.fori_loop(0, (count + UNROLL - 1) // UNROLL, step, 0)


def facet_kernel(
    facet,
    coef,
    stride,
    pos_ref,
    items_ref,
    count_ref,
    gram_ref,
    back_ref,
    half_ref,
    column_ref,
    lanes_ref,
    rows_ref,
    inv_row_ref,
    inv_col_ref,
    out_ref,
    grid,
    acc,
    flip,
):
    count = count_ref[facet]

    def column_pass(cycle, pc):
        part = half_ref[cycle, 0, :, pc * PAIR : (pc + 1) * PAIR]
        turned = jnp.concatenate([part[:, S:], -part[:, :S]], axis=1)
        return dot(column_ref[0], jnp.concatenate([part, turned], axis=0))

    for pc in range(SIDE):
        grid[pc] = column_pass(0, pc).astype(BF16)
        acc[pc, :P_SIZE] = back_ref[0, pc].astype(F32)
    degrid_grid(items_ref, facet * stride, count, gram_ref, grid, acc)

    lane = lax.broadcasted_iota(jnp.int32, (1, PAIR), 1)
    row = lax.broadcasted_iota(jnp.int32, (PAIR, 1), 0)
    sign = jnp.where(lane < S, 1.0, -1.0).astype(F32)
    for pc in range(SIDE):
        flip[pc] = acc[pc, :P_SIZE].astype(BF16)
    for pc in range(SIDE):
        turned = dot(flip[SIDE - 1 - pc], lanes_ref[...])
        edge = flip[(SIDE - pc) % SIDE].astype(F32) * sign
        mirrored = jnp.where(lane % S == 0, edge, turned)
        mirrored_half = mirrored.astype(BF16)
        fresh = column_pass(1, pc)
        for b in range(2):
            mine = slice(b * PAIR, (b + 1) * PAIR)
            other = slice((1 - b) * PAIR, (2 - b) * PAIR)
            swapped = dot(rows_ref[...], mirrored_half[other])
            swapped = jnp.where(row == 0, mirrored[mine], swapped)
            grid[pc, mine] = (fresh[mine] + coef * (acc[pc, mine] + swapped)).astype(BF16)
    for pc in range(SIDE):
        acc[pc, :P_SIZE] = back_ref[0, pc].astype(F32)
    degrid_grid(items_ref, facet * stride, count, gram_ref, grid, acc)

    mixed = [[] for _ in range(SIDE)]
    for pc in range(SIDE):
        r0, r1, r2, r3 = (acc[pc, p * S : (p + 1) * S] for p in range(SIDE))
        even, odd = r0 + r2, r0 - r2
        even_b, odd_b = r1 + r3, r1 - r3
        turned = jnp.concatenate([-odd_b[:, S:], odd_b[:, :S]], axis=1)
        for q, value in enumerate((even + even_b, odd + turned, even - even_b, odd - turned)):
            value = value.astype(BF16)
            mixed[q].append(jnp.concatenate([value[:, :S], value[:, S:]], axis=0))
    for q in range(SIDE):
        spec = dot(inv_row_ref[q], jnp.concatenate(mixed[q], axis=1)).astype(BF16)
        parts = []
        for pc in range(SIDE):
            cols = slice(pc * S, (pc + 1) * S)
            parts += [spec[:S, cols], spec[S:, cols]]
        out_ref[q] = dot(jnp.concatenate(parts, axis=1), inv_col_ref[...]).astype(BF16)


def tile_lists(codes, stride):
    total = codes.shape[0]
    group = codes >> 4
    ids = jnp.arange(total, dtype=jnp.int32)
    same = (group[:, None] == group[None, :]) & (ids[None, :] < ids[:, None])
    rank = jnp.sum(same.astype(jnp.int32), axis=1)
    pairs = (jnp.sum((group[None, :] == jnp.arange(F * WPLANES)[:, None]).astype(jnp.int32), axis=1) + 1) >> 1
    by_facet = pairs.reshape(F, WPLANES)
    count = jnp.sum(by_facet, axis=1)
    facet = codes >> 8
    planes = jnp.arange(F * WPLANES, dtype=jnp.int32)
    earlier = (planes[None, :] < group[:, None]) & ((planes[None, :] >> 4) == facet[:, None])
    base = jnp.sum(jnp.where(earlier, pairs[None, :], 0), axis=1)
    where = facet * stride + base + (rank >> 1)
    patch, plane = codes & (NP - 1), (codes >> 4) & (WPLANES - 1)
    delta = jnp.where((rank & 1) == 0, plane + ((patch - NP) << 4), (patch - NP) << 9)
    places = jnp.arange(F * stride, dtype=jnp.int32)
    hit = (places[:, None] == where[None, :]) & (facet < F)[None, :]
    items = (NP << 4) + (NP << 9) + jnp.sum(jnp.where(hit, delta[None, :], 0), axis=1)
    return items, count


def local(model_input, w_kernels, visibilities, tile_facet, tile_patch, tile_wplane, tile_count):
    devices = lax.axis_size("vis")
    position = lax.axis_index("vis").astype(jnp.int32)
    rows = P_SIZE // devices
    weight = math.sqrt(F * NP / (TILE_CAP * devices))
    total = TILE_CAP * devices
    stride = total // 2 + WPLANES + UNROLL

    slots = tile_facet * NP + tile_patch
    live = jnp.arange(TILE_CAP, dtype=jnp.int32) < tile_count[0]
    codes = jnp.where(live, (tile_facet << 8) + (tile_wplane << 4) + tile_patch, 1 << 12)
    all_codes = lax.all_gather(codes, "vis", axis=0, tiled=True)

    smem = pl.BlockSpec(memory_space=pltpu.SMEM)
    vmem = pl.BlockSpec(memory_space=pltpu.VMEM)
    gram, back, halves = pl.pallas_call(
        prep_kernel,
        out_shape=(
            jax.ShapeDtypeStruct((WPLANES, PAIR, PAIR), BF16),
            jax.ShapeDtypeStruct((F, SIDE, P_SIZE, PAIR), BF16),
            jax.ShapeDtypeStruct((2 * F * rows, 2 * P_SIZE), BF16),
        ),
        in_specs=[smem, smem, smem, vmem, vmem, vmem, vmem],
        out_specs=(vmem, vmem, vmem),
        scratch_shapes=[
            pltpu.VMEM((WPLANES, PAIR, PAIR), BF16),
            pltpu.VMEM((WPLANES, PAIR, PAIR), BF16),
            pltpu.VMEM((F, SIDE, P_SIZE, PAIR), F32),
        ],
        compiler_params=pltpu.CompilerParams(vmem_limit_bytes=VMEM_BYTES),
        cost_estimate=pl.CostEstimate(flops=8 * 10**9, bytes_accessed=12 * 2**20, transcendentals=0),
        name="prep",
    )(
        slots,
        tile_wplane,
        tile_count,
        w_kernels,
        visibilities,
        model_input.reshape(2 * F * rows, P_SIZE),
        jnp.asarray(row_table()),
    )
    halves = halves.reshape(2, F, rows, 2 * P_SIZE)
    items, counts = tile_lists(all_codes, stride)

    lanes, row_flip = flip_tables()
    columns = jnp.asarray(column_tables(devices))
    inv_rows = jnp.asarray(inverse_row_tables())
    inv_cols = jnp.asarray(inverse_column_table(weight))
    here = position.reshape(1)
    outs = []
    for facet in range(F):
        image = pl.pallas_call(
            functools.partial(facet_kernel, facet, GAIN * weight / 2, stride),
            out_shape=jax.ShapeDtypeStruct((SIDE, S, P_SIZE), BF16),
            grid_spec=pltpu.PrefetchScalarGridSpec(
                num_scalar_prefetch=3,
                grid=(1,),
                in_specs=[
                    vmem,
                    pl.BlockSpec((1, SIDE, P_SIZE, PAIR), lambda i, p, a, b, f=facet: (f, 0, 0, 0)),
                    pl.BlockSpec((2, 1, rows, 2 * P_SIZE), lambda i, p, a, b, f=facet: (0, f, 0, 0)),
                    pl.BlockSpec((1, P_SIZE, 2 * rows), lambda i, p, a, b: (p[0], 0, 0)),
                    vmem,
                    vmem,
                    vmem,
                    vmem,
                ],
                out_specs=vmem,
                scratch_shapes=[
                    pltpu.VMEM((SIDE, P_SIZE, PAIR), BF16),
                    pltpu.VMEM((SIDE, P_SIZE + S, PAIR), F32),
                    pltpu.VMEM((SIDE, P_SIZE, PAIR), BF16),
                ],
            ),
            compiler_params=pltpu.CompilerParams(vmem_limit_bytes=VMEM_BYTES),
            cost_estimate=pl.CostEstimate(flops=8 * 10**9, bytes_accessed=6 * 2**20, transcendentals=0),
            name="facet",
        )(here, items, counts, gram, back, halves, columns, jnp.asarray(lanes), jnp.asarray(row_flip), inv_rows, inv_cols)
        share = image.reshape(SIDE, devices, rows // SIDE, P_SIZE).transpose(1, 0, 2, 3)
        share = lax.psum_scatter(share, "vis", scatter_dimension=0, tiled=True)
        outs.append(share.reshape(SIDE, rows // SIDE, P_SIZE))
    full = jnp.stack(outs).astype(F32)
    return full.transpose(0, 2, 1, 3).reshape(F, rows, P_SIZE)


def solution(mesh):
    return jax.shard_map(
        local,
        mesh=mesh,
        in_specs=(
            P(None, "freq", "vis", None),
            P("freq", None, None, None),
            P(("freq", "vis"), None, None, None),
            P(("freq", "vis")),
            P(("freq", "vis")),
            P(("freq", "vis")),
            P(("freq", "vis")),
        ),
        out_specs=P("freq", "vis", None),
        check_vma=False,
    )
```

```python
import functools
import math

import jax
import jax.numpy as jnp
import ml_dtypes
import numpy as np
from jax import lax
from jax.experimental import pallas as pl
from jax.experimental.pallas import tpu as pltpu
from jax.sharding import PartitionSpec as P

P_SIZE = 512
S = 128
F = 4
WPLANES = 16
TILE_CAP = 32
NP = 16
SIDE = P_SIZE // S
PAIR = 2 * S
UNROLL = 4
GAIN = 0.5
PREP_VMEM = 32 * 1024 * 1024
FACET_VMEM = 24 * 1024 * 1024

BF16 = jnp.bfloat16
F32 = jnp.float32


def angle_tables():
    index = np.arange(P_SIZE)
    angles = (index[:, None] * index[None, :] % P_SIZE) * (2.0 * np.pi / P_SIZE)
    return np.cos(angles) / np.sqrt(P_SIZE), np.sin(angles) / np.sqrt(P_SIZE)


def half(array):
    return np.asarray(array, np.float32).astype(ml_dtypes.bfloat16)


def complex_block(real, imag):
    return np.block([[real, -imag], [imag, real]])


def by_columns(table):
    rows, columns = table.shape
    return table.reshape(rows, columns // S, S).transpose(1, 0, 2)


def wide(ref, chunk):
    return jnp.concatenate([ref[chunk], ref[chunk + 1]], axis=1)


def row_table():
    cosine, sine = angle_tables()
    parts = [cosine.reshape(P_SIZE, SIDE, 1, S), -sine.reshape(P_SIZE, SIDE, 1, S)]
    return half(by_columns(np.concatenate(parts, axis=2).reshape(P_SIZE, 2 * P_SIZE)))


def column_tables(devices):
    cosine, sine = angle_tables()
    rows = P_SIZE // devices
    parts = [t.reshape(P_SIZE, devices, rows).transpose(1, 0, 2) for t in (cosine, sine)]
    return half(np.concatenate(parts, axis=2))


def flip_tables():
    small = np.zeros((S, S))
    for k in range(1, S):
        small[S - k, k] = 1.0
    zero = np.zeros((S, S))
    lanes = np.block([[small, zero], [zero, -small]])
    rows = np.zeros((PAIR, PAIR))
    for i in range(1, PAIR):
        rows[i, PAIR - i] = 1.0
    return half(by_columns(lanes)), half(by_columns(rows))


def inverse_row_tables():
    a, i = np.arange(S)[:, None], np.arange(S)[None, :]
    blocks = []
    for q in range(SIDE):
        angles = ((SIDE * a + q) * i % P_SIZE) * (2.0 * np.pi / P_SIZE)
        blocks.append(by_columns(complex_block(np.cos(angles), np.sin(angles)) / np.sqrt(P_SIZE)))
    return half(np.concatenate(blocks))


def inverse_column_table(weight):
    cosine, sine = angle_tables()
    parts = [cosine.reshape(SIDE, 1, S, P_SIZE), -sine.reshape(SIDE, 1, S, P_SIZE)]
    return half(by_columns(np.concatenate(parts, axis=1).reshape(2 * P_SIZE, P_SIZE) * weight))


def dot(a, b):
    return jnp.dot(a, b, preferred_element_type=F32)


def restack(pair):
    top = jnp.concatenate([pair[:S, :S], pair[S:, :S]], axis=1)
    bottom = jnp.concatenate([pair[:S, S:], pair[S:, S:]], axis=1)
    return jnp.concatenate([top, bottom], axis=0)


def prep_kernel(slot_ref, plane_ref, count_ref, wk_ref, vis_ref, sky_ref, row_ref, tie_ref, gram_ref, back_ref, half_ref, kern, kern_t, acc):
    for w in range(WPLANES):
        real, imag = wk_ref[w, 0], wk_ref[w, 1]
        block = jnp.concatenate(
            [jnp.concatenate([real, -imag], axis=1), jnp.concatenate([imag, real], axis=1)], axis=0
        )
        real_t = real.astype(F32).T.astype(BF16)
        imag_t = imag.astype(F32).T.astype(BF16)
        block_t = jnp.concatenate(
            [jnp.concatenate([real_t, imag_t], axis=1), jnp.concatenate([-imag_t, real_t], axis=1)], axis=0
        )
        kern[w] = block
        kern_t[w] = block_t
        gram_ref[w] = dot(block_t, block).astype(BF16)

    for pc in range(SIDE):
        half_ref[:, pc * PAIR : (pc + 1) * PAIR] = dot(sky_ref[...], wide(row_ref, 2 * pc)).astype(BF16)

    acc[...] = jnp.zeros_like(acc)
    count = count_ref[0]

    def tiles(step, carry):
        for lane in range(4):
            t = step * 4 + lane
            slot, w = slot_ref[t], plane_ref[t]
            alive = jnp.where(t < count, 1.0, 0.0).astype(F32)
            observed = jnp.concatenate([vis_ref[t, 0], vis_ref[t, 1]], axis=1)
            right = (dot(observed, kern[w]) * alive).astype(BF16)
            stacked = jnp.concatenate([right[:, :S], right[:, S:]], axis=0)
            both = dot(kern_t[w], stacked)
            term = jnp.concatenate([both[:S], both[S:]], axis=1)
            facet, patch = slot >> 4, slot & (NP - 1)
            row = pl.multiple_of((patch >> 2) * S, S)
            place = (facet, patch & 3, pl.ds(row, S))
            acc[place] = acc[place] + term
        return carry

    lax.fori_loop(0, (count + 3) // 4, tiles, 0)
    for f in range(F):
        back_ref[f] = acc[f].astype(BF16)


def degrid_grid(items_ref, base, count, gram_ref, grid_ref, acc, held):
    def step(n, carry):
        for lane in range(UNROLL):
            code = items_ref[base + n * UNROLL + lane]
            both = dot(gram_ref[code & (WPLANES - 1)], held[lane])
            for k, slot in enumerate(((code >> 4) & 31, (code >> 9) & 31)):
                cols = slice(k * S, (k + 1) * S)
                term = jnp.concatenate([both[:S, cols], both[S:, cols]], axis=1)
                place = (slot & 3, pl.ds(pl.multiple_of((slot >> 2) * S, S), S))
                acc[place] = acc[place] - term
        for lane in range(UNROLL):
            code = items_ref[base + (n + 1) * UNROLL + lane]

            def read(slot):
                row = pl.multiple_of(((slot >> 2) & 3) * S, S)
                return grid_ref[slot & 3, pl.ds(row, S)]

            pair = jnp.concatenate([read((code >> 4) & 31), read((code >> 9) & 31)], axis=0)
            held[lane] = restack(dot(pair, gram_ref[code & (WPLANES - 1)]).astype(BF16))
        return carry

    lax.fori_loop(0, (count + UNROLL - 1) // UNROLL + 1, step, 0)


def facet_kernel(
    facet,
    coef,
    stride,
    devices,
    ties,
    pos_ref,
    items_ref,
    count_ref,
    gram_ref,
    back_ref,
    half_ref,
    column_ref,
    lanes_ref,
    rows_ref,
    inv_row_ref,
    inv_col_ref,
    *rest,
):
    rest = rest[ties:]
    *out_refs, grid, acc, flip, held = rest
    count = count_ref[facet]

    def column_pass(cycle, pc):
        part = half_ref[cycle, 0, :, pc * PAIR : (pc + 1) * PAIR]
        turned = jnp.concatenate([part[:, S:], -part[:, :S]], axis=1)
        return dot(column_ref[0], jnp.concatenate([part, turned], axis=0))

    for pc in range(SIDE):
        grid[pc] = column_pass(0, pc).astype(BF16)
        acc[pc, :P_SIZE] = back_ref[0, pc].astype(F32)
    degrid_grid(items_ref, facet * stride, count, gram_ref, grid, acc, held)

    lane = lax.broadcasted_iota(jnp.int32, (1, PAIR), 1)
    row = lax.broadcasted_iota(jnp.int32, (PAIR, 1), 0)
    sign = jnp.where(lane < S, 1.0, -1.0).astype(F32)
    for pc in range(SIDE):
        flip[pc] = acc[pc, :P_SIZE].astype(BF16)
    for pc in range(SIDE):
        turned = dot(flip[SIDE - 1 - pc], wide(lanes_ref, 0))
        edge = flip[(SIDE - pc) % SIDE].astype(F32) * sign
        mirrored = jnp.where(lane % S == 0, edge, turned)
        mirrored_half = mirrored.astype(BF16)
        fresh = column_pass(1, pc)
        for b in range(2):
            mine = slice(b * PAIR, (b + 1) * PAIR)
            other = slice((1 - b) * PAIR, (2 - b) * PAIR)
            swapped = dot(wide(rows_ref, 0), mirrored_half[other])
            swapped = jnp.where(row == 0, mirrored[mine], swapped)
            grid[pc, mine] = (fresh[mine] + coef * (acc[pc, mine] + swapped)).astype(BF16)
    for pc in range(SIDE):
        acc[pc, :P_SIZE] = back_ref[0, pc].astype(F32)
    degrid_grid(items_ref, facet * stride, count, gram_ref, grid, acc, held)

    mixed = [[] for _ in range(SIDE)]
    for pc in range(SIDE):
        r0, r1, r2, r3 = (acc[pc, p * S : (p + 1) * S] for p in range(SIDE))
        even, odd = r0 + r2, r0 - r2
        even_b, odd_b = r1 + r3, r1 - r3
        turned = jnp.concatenate([-odd_b[:, S:], odd_b[:, :S]], axis=1)
        for q, value in enumerate((even + even_b, odd + turned, even - even_b, odd - turned)):
            value = value.astype(BF16)
            mixed[q].append(jnp.concatenate([value[:, :S], value[:, S:]], axis=0))
    for q in range(SIDE):
        spec = dot(wide(inv_row_ref, 2 * q), jnp.concatenate(mixed[q], axis=1)).astype(BF16)
        parts = []
        for pc in range(SIDE):
            cols = slice(pc * S, (pc + 1) * S)
            parts += [spec[:S, cols], spec[S:, cols]]
        spec = jnp.concatenate(parts, axis=1)
        image = jnp.concatenate([dot(spec, wide(inv_col_ref, j)) for j in range(0, SIDE, 2)], axis=1)
        if len(out_refs) == 1:
            out_refs[0][q] = image.astype(BF16)
            continue
        keep_ref, send_ref = out_refs
        share, far = S // devices, devices // 2
        odd, mine = pos_ref[0] & 1, pos_ref[0] >> 1
        for there in range(far):
            zero = image[2 * there * share : (2 * there + 1) * share].astype(BF16)
            one = image[(2 * there + 1) * share : (2 * there + 2) * share].astype(BF16)
            place = (there - mine + far) % far
            keep_ref[place, q] = jnp.where(odd == 0, zero, one)
            send_ref[place, q] = jnp.where(odd == 0, one, zero)


def tile_lists(codes, stride):
    total = codes.shape[0]
    group = codes >> 4
    ids = jnp.arange(total, dtype=jnp.int32)
    same = (group[:, None] == group[None, :]) & (ids[None, :] < ids[:, None])
    rank = jnp.sum(same.astype(jnp.int32), axis=1)
    pairs = (jnp.sum((group[None, :] == jnp.arange(F * WPLANES)[:, None]).astype(jnp.int32), axis=1) + 1) >> 1
    by_facet = pairs.reshape(F, WPLANES)
    count = jnp.sum(by_facet, axis=1)
    facet = codes >> 8
    planes = jnp.arange(F * WPLANES, dtype=jnp.int32)
    earlier = (planes[None, :] < group[:, None]) & ((planes[None, :] >> 4) == facet[:, None])
    base = jnp.sum(jnp.where(earlier, pairs[None, :], 0), axis=1)
    where = facet * stride + base + (rank >> 1)
    patch, plane = codes & (NP - 1), (codes >> 4) & (WPLANES - 1)
    delta = jnp.where((rank & 1) == 0, plane + ((patch - NP) << 4), (patch - NP) << 9)
    places = jnp.arange(F * stride, dtype=jnp.int32)
    where = where + UNROLL
    hit = (places[:, None] == where[None, :]) & (facet < F)[None, :]
    items = (NP << 4) + (NP << 9) + jnp.sum(jnp.where(hit, delta[None, :], 0), axis=1)
    return items, count


def shift(value, offset, devices):
    return lax.ppermute(value, "vis", [(i, (i + offset) % devices) for i in range(devices)])


def split_image(image, position, devices):
    share, far = S // devices, devices // 2
    parts = jnp.roll(image.reshape(SIDE, far, 2, share, P_SIZE), -(position >> 1), axis=1).transpose(2, 1, 0, 3, 4)
    odd = position & 1
    return lax.dynamic_index_in_dim(parts, odd, 0, False), lax.dynamic_index_in_dim(parts, 1 - odd, 0, False)


def merge_pair(keep, taken):
    return [(keep[k].astype(F32) + taken[k].astype(F32)).astype(BF16) for k in range(1, keep.shape[0])]


def final_kernel(parts, *refs):
    *in_refs, out_ref, mixed = refs
    for f in range(F):
        keep_ref, taken_ref, *others = in_refs[f * parts : (f + 1) * parts]
        for q in range(SIDE):
            total = keep_ref[0, q].astype(F32) + taken_ref[0, q].astype(F32)
            for other in others:
                total = total + other[q].astype(F32)
            for c in range(SIDE):
                mixed[c, pl.ds(q, total.shape[0], stride=SIDE), :] = total[:, c * S : (c + 1) * S]
        for c in range(SIDE):
            out_ref[f, :, c * S : (c + 1) * S] = mixed[c]


def local(model_input, w_kernels, visibilities, tile_facet, tile_patch, tile_wplane, tile_count):
    devices = lax.axis_size("vis")
    position = lax.axis_index("vis").astype(jnp.int32)
    rows = P_SIZE // devices
    weight = math.sqrt(F * NP / (TILE_CAP * devices))
    total = TILE_CAP * devices
    stride = total // 2 + WPLANES // 2 + 3 * UNROLL

    slots = tile_facet * NP + tile_patch
    live = jnp.arange(TILE_CAP, dtype=jnp.int32) < tile_count[0]
    codes = jnp.where(live, (tile_facet << 8) + (tile_wplane << 4) + tile_patch, 1 << 12)
    neighbour = [(i, i ^ 1) for i in range(devices)]
    codes = jnp.concatenate([codes, lax.ppermute(codes, "vis", neighbour)])
    all_codes = jnp.concatenate([codes] + [shift(codes, 2 * k, devices) for k in range(1, devices // 2)])

    smem = pl.BlockSpec(memory_space=pltpu.SMEM)
    vmem = pl.BlockSpec(memory_space=pltpu.VMEM)
    gram, back, halves = pl.pallas_call(
        prep_kernel,
        out_shape=(
            jax.ShapeDtypeStruct((WPLANES, PAIR, PAIR), BF16),
            jax.ShapeDtypeStruct((F, SIDE, P_SIZE, PAIR), BF16),
            jax.ShapeDtypeStruct((2 * F * rows, 2 * P_SIZE), BF16),
        ),
        in_specs=[smem, smem, smem, vmem, vmem, vmem, vmem, pl.BlockSpec(memory_space=pl.ANY)],
        out_specs=(vmem, vmem, vmem),
        scratch_shapes=[
            pltpu.VMEM((WPLANES, PAIR, PAIR), BF16),
            pltpu.VMEM((WPLANES, PAIR, PAIR), BF16),
            pltpu.VMEM((F, SIDE, P_SIZE, PAIR), F32),
        ],
        compiler_params=pltpu.CompilerParams(vmem_limit_bytes=PREP_VMEM),
        cost_estimate=pl.CostEstimate(flops=8 * 10**9, bytes_accessed=12 * 2**20, transcendentals=0),
        name="prep",
    )(
        slots,
        tile_wplane,
        tile_count,
        w_kernels,
        visibilities,
        model_input.reshape(2 * F * rows, P_SIZE),
        jnp.asarray(row_table()),
        codes,
    )
    halves = halves.reshape(2, F, rows, 2 * P_SIZE)
    items, counts = tile_lists(all_codes, stride)

    lanes, row_flip = flip_tables()
    columns = jnp.asarray(column_tables(devices))
    inv_rows = jnp.asarray(inverse_row_tables())
    inv_cols = jnp.asarray(inverse_column_table(weight))
    here = position.reshape(1)
    share, far = S // devices, devices // 2
    split = share % 16 == 0
    if split:
        out_shape = [jax.ShapeDtypeStruct((far, SIDE, share, P_SIZE), BF16)] * 2
    else:
        out_shape = [jax.ShapeDtypeStruct((SIDE, S, P_SIZE), BF16)]
    pairs, merged, others = [], [], []
    for facet in range(F):
        ties = []
        if facet >= 2:
            merged.append(merge_pair(*pairs[facet - 2]))
            others.append([shift(part, 2 * k, devices) for k, part in enumerate(merged[-1], 1)])
            ties += merged[-1][:1]
        if facet >= 3:
            ties += others[facet - 3]
        image = pl.pallas_call(
            functools.partial(facet_kernel, facet, GAIN * weight / 2, stride, devices, len(ties)),
            out_shape=out_shape,
            grid_spec=pltpu.PrefetchScalarGridSpec(
                num_scalar_prefetch=3,
                grid=(1,),
                in_specs=[
                    vmem,
                    pl.BlockSpec((1, SIDE, P_SIZE, PAIR), lambda i, p, a, b, f=facet: (f, 0, 0, 0)),
                    pl.BlockSpec((2, 1, rows, 2 * P_SIZE), lambda i, p, a, b, f=facet: (0, f, 0, 0)),
                    pl.BlockSpec((1, P_SIZE, 2 * rows), lambda i, p, a, b: (p[0], 0, 0)),
                    vmem,
                    vmem,
                    vmem,
                    vmem,
                ]
                + [pl.BlockSpec(memory_space=pl.ANY)] * len(ties),
                out_specs=[vmem] * len(out_shape),
                scratch_shapes=[
                    pltpu.VMEM((SIDE, P_SIZE, PAIR), BF16),
                    pltpu.VMEM((SIDE, P_SIZE + S, PAIR), F32),
                    pltpu.VMEM((SIDE, P_SIZE, PAIR), BF16),
                    pltpu.VMEM((UNROLL, PAIR, PAIR), BF16),
                ],
            ),
            compiler_params=pltpu.CompilerParams(vmem_limit_bytes=FACET_VMEM),
            cost_estimate=pl.CostEstimate(flops=12 * 10**9, bytes_accessed=6 * 2**20, transcendentals=0),
            name="facet",
        )(here, items, counts, gram, back, halves, columns, jnp.asarray(lanes), jnp.asarray(row_flip), inv_rows, inv_cols, *ties)
        keep, send = image if split else split_image(image[0], position, devices)
        pairs.append((keep, lax.ppermute(send, "vis", neighbour)))
    for facet in range(F - 2, F):
        merged.append(merge_pair(*pairs[facet]))
        others.append([shift(part, 2 * k, devices) for k, part in enumerate(merged[-1], 1)])

    first = pl.BlockSpec((1, SIDE, share, P_SIZE), lambda i: (0, 0, 0, 0))
    operands = [a for pair, other in zip(pairs, others) for a in (*pair, *other)]
    parts = len(operands) // F
    return pl.pallas_call(
        functools.partial(final_kernel, parts),
        out_shape=jax.ShapeDtypeStruct((F, rows, P_SIZE), F32),
        grid=(1,),
        in_specs=([first, first] + [vmem] * (parts - 2)) * F,
        out_specs=vmem,
        scratch_shapes=[pltpu.VMEM((SIDE, rows, S), F32)],
        cost_estimate=pl.CostEstimate(flops=10**6, bytes_accessed=2**20, transcendentals=0),
        name="final",
    )(*operands)


def solution(mesh):
    return jax.shard_map(
        local,
        mesh=mesh,
        in_specs=(
            P(None, "freq", "vis", None),
            P("freq", None, None, None),
            P(("freq", "vis"), None, None, None),
            P(("freq", "vis")),
            P(("freq", "vis")),
            P(("freq", "vis")),
            P(("freq", "vis")),
        ),
        out_specs=P("freq", "vis", None),
        check_vma=False,
    )
```

```python
import functools
import math

import jax
import jax.numpy as jnp
import ml_dtypes
import numpy as np
from jax import lax
from jax.experimental import pallas as pl
from jax.experimental.pallas import tpu as pltpu
from jax.sharding import PartitionSpec as P

P_SIZE = 512
S = 128
F = 4
WPLANES = 16
TILE_CAP = 32
NP = 16
SIDE = P_SIZE // S
PAIR = 2 * S
UNROLL = 4
GAIN = 0.5
VMEM_BYTES = 60 * 1024 * 1024

BF16 = jnp.bfloat16
F32 = jnp.float32


def angle_tables():
    index = np.arange(P_SIZE)
    angles = (index[:, None] * index[None, :] % P_SIZE) * (2.0 * np.pi / P_SIZE)
    return np.cos(angles) / np.sqrt(P_SIZE), np.sin(angles) / np.sqrt(P_SIZE)


def half(array):
    return np.asarray(array, np.float32).astype(ml_dtypes.bfloat16)


def complex_block(real, imag):
    return np.block([[real, -imag], [imag, real]])


def by_columns(table):
    rows, columns = table.shape
    return table.reshape(rows, columns // S, S).transpose(1, 0, 2)


def wide(ref, chunk):
    return jnp.concatenate([ref[chunk], ref[chunk + 1]], axis=1)


def row_table():
    cosine, sine = angle_tables()
    parts = [cosine.reshape(P_SIZE, SIDE, 1, S), -sine.reshape(P_SIZE, SIDE, 1, S)]
    return half(by_columns(np.concatenate(parts, axis=2).reshape(P_SIZE, 2 * P_SIZE)))


def column_tables(devices):
    cosine, sine = angle_tables()
    rows = P_SIZE // devices
    parts = [t.reshape(P_SIZE, devices, rows).transpose(1, 0, 2) for t in (cosine, sine)]
    return half(np.concatenate(parts, axis=2))


def flip_tables():
    small = np.zeros((S, S))
    for k in range(1, S):
        small[S - k, k] = 1.0
    zero = np.zeros((S, S))
    lanes = np.block([[small, zero], [zero, -small]])
    rows = np.zeros((PAIR, PAIR))
    for i in range(1, PAIR):
        rows[i, PAIR - i] = 1.0
    return half(by_columns(lanes)), half(by_columns(rows))


def inverse_row_tables():
    a, i = np.arange(S)[:, None], np.arange(S)[None, :]
    blocks = []
    for q in range(SIDE):
        angles = ((SIDE * a + q) * i % P_SIZE) * (2.0 * np.pi / P_SIZE)
        blocks.append(by_columns(complex_block(np.cos(angles), np.sin(angles)) / np.sqrt(P_SIZE)))
    return half(np.concatenate(blocks))


def inverse_column_table(weight):
    cosine, sine = angle_tables()
    parts = [cosine.reshape(SIDE, 1, S, P_SIZE), -sine.reshape(SIDE, 1, S, P_SIZE)]
    return half(by_columns(np.concatenate(parts, axis=1).reshape(2 * P_SIZE, P_SIZE) * weight))


def dot(a, b):
    return jnp.dot(a, b, preferred_element_type=F32)


def restack(pair):
    top = jnp.concatenate([pair[:S, :S], pair[S:, :S]], axis=1)
    bottom = jnp.concatenate([pair[:S, S:], pair[S:, S:]], axis=1)
    return jnp.concatenate([top, bottom], axis=0)


def prep_kernel(
    slot_ref,
    plane_ref,
    count_ref,
    wk_hbm,
    vis_hbm,
    sky_hbm,
    row_hbm,
    gram_hbm,
    back_hbm,
    half_hbm,
    wk_ref,
    vis_ref,
    sky_ref,
    row_ref,
    gram_ref,
    back_ref,
    half_ref,
    kern,
    kern_t,
    acc,
    sems,
):
    loads = [
        pltpu.make_async_copy(src, dst, sems.at[k])
        for k, (src, dst) in enumerate(
            ((wk_hbm, wk_ref), (sky_hbm, sky_ref), (row_hbm, row_ref), (vis_hbm, vis_ref))
        )
    ]
    for load in loads:
        load.start()
    acc[...] = jnp.zeros_like(acc)

    loads[0].wait()
    for w in range(WPLANES):
        real, imag = wk_ref[w, 0], wk_ref[w, 1]
        block = jnp.concatenate(
            [jnp.concatenate([real, -imag], axis=1), jnp.concatenate([imag, real], axis=1)], axis=0
        )
        real_t = real.astype(F32).T.astype(BF16)
        imag_t = imag.astype(F32).T.astype(BF16)
        block_t = jnp.concatenate(
            [jnp.concatenate([real_t, imag_t], axis=1), jnp.concatenate([-imag_t, real_t], axis=1)], axis=0
        )
        kern[w] = block
        kern_t[w] = block_t
        gram_ref[w] = dot(block_t, block).astype(BF16)
    gram_out = pltpu.make_async_copy(gram_ref, gram_hbm, sems.at[4])
    gram_out.start()

    loads[1].wait()
    loads[2].wait()
    for pc in range(SIDE):
        half_ref[:, pc * PAIR : (pc + 1) * PAIR] = dot(sky_ref[...], wide(row_ref, 2 * pc)).astype(BF16)
    half_out = pltpu.make_async_copy(half_ref, half_hbm, sems.at[5])
    half_out.start()

    loads[3].wait()
    count = count_ref[0]

    def tiles(step, carry):
        for lane in range(4):
            t = step * 4 + lane
            slot, w = slot_ref[t], plane_ref[t]
            alive = jnp.where(t < count, 1.0, 0.0).astype(F32)
            observed = jnp.concatenate([vis_ref[t, 0], vis_ref[t, 1]], axis=1)
            right = (dot(observed, kern[w]) * alive).astype(BF16)
            stacked = jnp.concatenate([right[:, :S], right[:, S:]], axis=0)
            both = dot(kern_t[w], stacked)
            term = jnp.concatenate([both[:S], both[S:]], axis=1)
            facet, patch = slot >> 4, slot & (NP - 1)
            row = pl.multiple_of((patch >> 2) * S, S)
            place = (facet, patch & 3, pl.ds(row, S))
            acc[place] = acc[place] + term
        return carry

    lax.fori_loop(0, (count + 3) // 4, tiles, 0)
    outs = []
    for f in range(F):
        back_ref[f] = acc[f].astype(BF16)
        outs.append(pltpu.make_async_copy(back_ref.at[f], back_hbm.at[f], sems.at[6 + f]))
        outs[-1].start()
    for out in (gram_out, half_out, *outs):
        out.wait()


def degrid_grid(items_ref, base, count, gram_ref, grid_ref, acc, held):
    def step(n, carry):
        for lane in range(UNROLL):
            code = items_ref[base + n * UNROLL + lane]
            both = dot(gram_ref[code & (WPLANES - 1)], held[lane])
            for k, slot in enumerate(((code >> 4) & 31, (code >> 9) & 31)):
                cols = slice(k * S, (k + 1) * S)
                term = jnp.concatenate([both[:S, cols], both[S:, cols]], axis=1)
                place = (slot & 3, pl.ds(pl.multiple_of((slot >> 2) * S, S), S))
                acc[place] = acc[place] - term
        for lane in range(UNROLL):
            code = items_ref[base + (n + 1) * UNROLL + lane]

            def read(slot):
                row = pl.multiple_of(((slot >> 2) & 3) * S, S)
                return grid_ref[slot & 3, pl.ds(row, S)]

            pair = jnp.concatenate([read((code >> 4) & 31), read((code >> 9) & 31)], axis=0)
            held[lane] = restack(dot(pair, gram_ref[code & (WPLANES - 1)]).astype(BF16))
        return carry

    lax.fori_loop(0, (count + UNROLL - 1) // UNROLL + 1, step, 0)


def facet_kernel(
    facet,
    coef,
    stride,
    devices,
    ties,
    pos_ref,
    items_ref,
    count_ref,
    gram_hbm,
    back_hbm,
    half_hbm,
    column_hbm,
    lanes_hbm,
    rows_hbm,
    inv_row_hbm,
    inv_col_hbm,
    *rest,
):
    out_ref, gram_ref, back_ref, half_ref, column_ref, lanes_ref, rows_ref, inv_row_ref, inv_col_ref, *rest = rest[ties:]
    grid, acc, flip, held, sems = rest
    moves = (
        (half_hbm.at[0, facet], half_ref.at[0]),
        (half_hbm.at[1, facet], half_ref.at[1]),
        (column_hbm.at[pos_ref[0]], column_ref),
        (gram_hbm, gram_ref),
        (back_hbm.at[facet], back_ref),
        (lanes_hbm, lanes_ref),
        (rows_hbm, rows_ref),
        (inv_row_hbm, inv_row_ref),
        (inv_col_hbm, inv_col_ref),
    )
    loads = [pltpu.make_async_copy(src, dst, sems.at[k]) for k, (src, dst) in enumerate(moves)]
    for load in loads:
        load.start()
    for load in loads[:3]:
        load.wait()
    count = count_ref[facet]

    def column_pass(cycle, pc):
        part = half_ref[cycle, :, pc * PAIR : (pc + 1) * PAIR]
        turned = jnp.concatenate([part[:, S:], -part[:, :S]], axis=1)
        return dot(column_ref[...], jnp.concatenate([part, turned], axis=0))

    for pc in range(SIDE):
        grid[pc] = column_pass(0, pc).astype(BF16)
    loads[3].wait()
    loads[4].wait()
    for pc in range(SIDE):
        acc[pc, :P_SIZE] = back_ref[pc].astype(F32)
    degrid_grid(items_ref, facet * stride, count, gram_ref, grid, acc, held)

    loads[5].wait()
    loads[6].wait()
    lane = lax.broadcasted_iota(jnp.int32, (1, PAIR), 1)
    row = lax.broadcasted_iota(jnp.int32, (PAIR, 1), 0)
    sign = jnp.where(lane < S, 1.0, -1.0).astype(F32)
    for pc in range(SIDE):
        flip[pc] = acc[pc, :P_SIZE].astype(BF16)
    for pc in range(SIDE):
        turned = dot(flip[SIDE - 1 - pc], wide(lanes_ref, 0))
        edge = flip[(SIDE - pc) % SIDE].astype(F32) * sign
        mirrored = jnp.where(lane % S == 0, edge, turned)
        mirrored_half = mirrored.astype(BF16)
        fresh = column_pass(1, pc)
        for b in range(2):
            mine = slice(b * PAIR, (b + 1) * PAIR)
            other = slice((1 - b) * PAIR, (2 - b) * PAIR)
            swapped = dot(wide(rows_ref, 0), mirrored_half[other])
            swapped = jnp.where(row == 0, mirrored[mine], swapped)
            grid[pc, mine] = (fresh[mine] + coef * (acc[pc, mine] + swapped)).astype(BF16)
    for pc in range(SIDE):
        acc[pc, :P_SIZE] = back_ref[pc].astype(F32)
    degrid_grid(items_ref, facet * stride, count, gram_ref, grid, acc, held)

    loads[7].wait()
    loads[8].wait()
    mixed = [[] for _ in range(SIDE)]
    for pc in range(SIDE):
        r0, r1, r2, r3 = (acc[pc, p * S : (p + 1) * S] for p in range(SIDE))
        even, odd = r0 + r2, r0 - r2
        even_b, odd_b = r1 + r3, r1 - r3
        turned = jnp.concatenate([-odd_b[:, S:], odd_b[:, :S]], axis=1)
        for q, value in enumerate((even + even_b, odd + turned, even - even_b, odd - turned)):
            value = value.astype(BF16)
            mixed[q].append(jnp.concatenate([value[:, :S], value[:, S:]], axis=0))
    for q in range(SIDE):
        spec = dot(wide(inv_row_ref, 2 * q), jnp.concatenate(mixed[q], axis=1)).astype(BF16)
        parts = []
        for pc in range(SIDE):
            cols = slice(pc * S, (pc + 1) * S)
            parts += [spec[:S, cols], spec[S:, cols]]
        spec = jnp.concatenate(parts, axis=1)
        image = jnp.concatenate([dot(spec, wide(inv_col_ref, j)) for j in range(0, SIDE, 2)], axis=1)
        if len(out_ref.shape) == 3:
            out_ref[q] = image.astype(BF16)
            continue
        share = S // devices
        for there in range(devices):
            out_ref[there, q] = image[there * share : (there + 1) * share].astype(BF16)


def tile_lists(codes, stride):
    total = codes.shape[0]
    group = codes >> 4
    ids = jnp.arange(total, dtype=jnp.int32)
    same = (group[:, None] == group[None, :]) & (ids[None, :] < ids[:, None])
    rank = jnp.sum(same.astype(jnp.int32), axis=1)
    pairs = (jnp.sum((group[None, :] == jnp.arange(F * WPLANES)[:, None]).astype(jnp.int32), axis=1) + 1) >> 1
    by_facet = pairs.reshape(F, WPLANES)
    count = jnp.sum(by_facet, axis=1)
    facet = codes >> 8
    planes = jnp.arange(F * WPLANES, dtype=jnp.int32)
    earlier = (planes[None, :] < group[:, None]) & ((planes[None, :] >> 4) == facet[:, None])
    base = jnp.sum(jnp.where(earlier, pairs[None, :], 0), axis=1)
    where = facet * stride + base + (rank >> 1)
    patch, plane = codes & (NP - 1), (codes >> 4) & (WPLANES - 1)
    delta = jnp.where((rank & 1) == 0, plane + ((patch - NP) << 4), (patch - NP) << 9)
    places = jnp.arange(F * stride, dtype=jnp.int32)
    where = where + UNROLL
    hit = (places[:, None] == where[None, :]) & (facet < F)[None, :]
    items = (NP << 4) + (NP << 9) + jnp.sum(jnp.where(hit, delta[None, :], 0), axis=1)
    return items, count


def final_kernel(*refs):
    *in_refs, out_ref, mixed = refs
    for f, in_ref in enumerate(in_refs):
        for q in range(SIDE):
            value = in_ref[0, q].astype(F32)
            for c in range(SIDE):
                mixed[c, pl.ds(q, value.shape[0], stride=SIDE), :] = value[:, c * S : (c + 1) * S]
        for c in range(SIDE):
            out_ref[f, :, c * S : (c + 1) * S] = mixed[c]


def local(model_input, w_kernels, visibilities, tile_facet, tile_patch, tile_wplane, tile_count):
    devices = lax.axis_size("vis")
    position = lax.axis_index("vis").astype(jnp.int32)
    rows = P_SIZE // devices
    weight = math.sqrt(F * NP / (TILE_CAP * devices))
    total = TILE_CAP * devices
    stride = total // 2 + WPLANES // 2 + 3 * UNROLL

    slots = tile_facet * NP + tile_patch
    live = jnp.arange(TILE_CAP, dtype=jnp.int32) < tile_count[0]
    codes = jnp.where(live, (tile_facet << 8) + (tile_wplane << 4) + tile_patch, 1 << 12)
    sent = jnp.broadcast_to(jnp.pad(codes, (0, S - TILE_CAP))[None, :], (8, S))
    all_codes = lax.all_gather(sent, "vis", axis=0, tiled=True).reshape(devices, 8, S)[:, 0, :TILE_CAP].reshape(total)

    smem = pl.BlockSpec(memory_space=pltpu.SMEM)
    vmem = pl.BlockSpec(memory_space=pltpu.VMEM)
    hbm = pl.BlockSpec(memory_space=pl.ANY)
    half_shape = (2 * F * rows, 2 * P_SIZE)
    gram, back, halves = pl.pallas_call(
        prep_kernel,
        out_shape=(
            jax.ShapeDtypeStruct((WPLANES, PAIR, PAIR), BF16),
            jax.ShapeDtypeStruct((F, SIDE, P_SIZE, PAIR), BF16),
            jax.ShapeDtypeStruct(half_shape, BF16),
        ),
        in_specs=[smem, smem, smem, hbm, hbm, hbm, hbm],
        out_specs=(hbm, hbm, hbm),
        scratch_shapes=[
            pltpu.VMEM(w_kernels.shape, BF16),
            pltpu.VMEM(visibilities.shape, BF16),
            pltpu.VMEM((2 * F * rows, P_SIZE), BF16),
            pltpu.VMEM((2 * SIDE, P_SIZE, S), BF16),
            pltpu.VMEM((WPLANES, PAIR, PAIR), BF16),
            pltpu.VMEM((F, SIDE, P_SIZE, PAIR), BF16),
            pltpu.VMEM(half_shape, BF16),
            pltpu.VMEM((WPLANES, PAIR, PAIR), BF16),
            pltpu.VMEM((WPLANES, PAIR, PAIR), BF16),
            pltpu.VMEM((F, SIDE, P_SIZE, PAIR), F32),
            pltpu.SemaphoreType.DMA((6 + F,)),
        ],
        compiler_params=pltpu.CompilerParams(vmem_limit_bytes=VMEM_BYTES),
        cost_estimate=pl.CostEstimate(flops=8 * 10**9, bytes_accessed=12 * 2**20, transcendentals=0),
        name="prep",
    )(
        slots,
        tile_wplane,
        tile_count,
        w_kernels,
        visibilities,
        model_input.reshape(2 * F * rows, P_SIZE),
        jnp.asarray(row_table()),
    )
    halves = halves.reshape(2, F, rows, 2 * P_SIZE)
    items, counts = tile_lists(all_codes, stride)

    lanes, row_flip = flip_tables()
    tables = [column_tables(devices), lanes, row_flip, inverse_row_tables(), inverse_column_table(weight)]
    columns, lanes, row_flip, inv_rows, inv_cols = (jnp.asarray(t) for t in tables)
    here = position.reshape(1)
    share = S // devices
    split = share % 16 == 0
    image_shape = (devices, SIDE, share, P_SIZE) if split else (SIDE, S, P_SIZE)
    sums = []
    for facet in range(F):
        ties = sums[facet - 2 : facet - 1] if facet >= 2 else []
        image = pl.pallas_call(
            functools.partial(facet_kernel, facet, GAIN * weight / 2, stride, devices, len(ties)),
            out_shape=jax.ShapeDtypeStruct(image_shape, BF16),
            in_specs=[smem] * 3 + [hbm] * (8 + len(ties)),
            out_specs=vmem,
            scratch_shapes=[
                pltpu.VMEM((WPLANES, PAIR, PAIR), BF16),
                pltpu.VMEM((SIDE, P_SIZE, PAIR), BF16),
                pltpu.VMEM((2, rows, 2 * P_SIZE), BF16),
                pltpu.VMEM((P_SIZE, 2 * rows), BF16),
                pltpu.VMEM(lanes.shape, BF16),
                pltpu.VMEM(row_flip.shape, BF16),
                pltpu.VMEM(inv_rows.shape, BF16),
                pltpu.VMEM(inv_cols.shape, BF16),
                pltpu.VMEM((SIDE, P_SIZE, PAIR), BF16),
                pltpu.VMEM((SIDE, P_SIZE + S, PAIR), F32),
                pltpu.VMEM((SIDE, P_SIZE, PAIR), BF16),
                pltpu.VMEM((UNROLL, PAIR, PAIR), BF16),
                pltpu.SemaphoreType.DMA((9,)),
            ],
            compiler_params=pltpu.CompilerParams(vmem_limit_bytes=VMEM_BYTES),
            cost_estimate=pl.CostEstimate(flops=12 * 10**9, bytes_accessed=6 * 2**20, transcendentals=0),
            name="facet",
        )(here, items, counts, gram, back, halves, columns, lanes, row_flip, inv_rows, inv_cols, *ties)
        if not split:
            image = image.reshape(SIDE, devices, share, P_SIZE).transpose(1, 0, 2, 3)
        if facet == F - 1:
            image, _ = lax.optimization_barrier((image, sums[-1]))
        sums.append(lax.psum_scatter(image, "vis", scatter_dimension=0, tiled=True))

    return pl.pallas_call(
        final_kernel,
        out_shape=jax.ShapeDtypeStruct((F, rows, P_SIZE), F32),
        in_specs=[vmem] * F,
        out_specs=vmem,
        scratch_shapes=[pltpu.VMEM((SIDE, rows, S), F32)],
        cost_estimate=pl.CostEstimate(flops=10**6, bytes_accessed=2**20, transcendentals=0),
        name="final",
    )(*sums)


def solution(mesh):
    return jax.shard_map(
        local,
        mesh=mesh,
        in_specs=(
            P(None, "freq", "vis", None),
            P("freq", None, None, None),
            P(("freq", "vis"), None, None, None),
            P(("freq", "vis")),
            P(("freq", "vis")),
            P(("freq", "vis")),
            P(("freq", "vis")),
        ),
        out_specs=P("freq", "vis", None),
        check_vma=False,
    )
```

```python
import functools
import math

import jax
import jax.numpy as jnp
import ml_dtypes
import numpy as np
from jax import lax
from jax.experimental import pallas as pl
from jax.experimental.pallas import tpu as pltpu
from jax.sharding import PartitionSpec as P

P_SIZE = 512
S = 128
F = 4
WPLANES = 16
TILE_CAP = 32
NP = 16
SIDE = P_SIZE // S
PAIR = 2 * S
UNROLL = 4
FIRST = 2
LISTS = F - FIRST + 1
SPARE = FIRST * NP
GAIN = 0.5
VMEM_BYTES = 60 * 1024 * 1024

BF16 = jnp.bfloat16
F32 = jnp.float32


def angle_tables():
    index = np.arange(P_SIZE)
    angles = (index[:, None] * index[None, :] % P_SIZE) * (2.0 * np.pi / P_SIZE)
    return np.cos(angles) / np.sqrt(P_SIZE), np.sin(angles) / np.sqrt(P_SIZE)


def half(array):
    return np.asarray(array, np.float32).astype(ml_dtypes.bfloat16)


def complex_block(real, imag):
    return np.block([[real, -imag], [imag, real]])


def by_columns(table):
    rows, columns = table.shape
    return table.reshape(rows, columns // S, S).transpose(1, 0, 2)


def wide(ref, chunk):
    return jnp.concatenate([ref[chunk], ref[chunk + 1]], axis=1)


def row_table():
    cosine, sine = angle_tables()
    parts = [cosine.reshape(P_SIZE, SIDE, 1, S), -sine.reshape(P_SIZE, SIDE, 1, S)]
    return half(by_columns(np.concatenate(parts, axis=2).reshape(P_SIZE, 2 * P_SIZE)))


def column_tables(devices):
    cosine, sine = angle_tables()
    rows = P_SIZE // devices
    parts = [t.reshape(P_SIZE, devices, rows).transpose(1, 0, 2) for t in (cosine, sine)]
    return half(np.concatenate(parts, axis=2))


def flip_tables():
    small = np.zeros((S, S))
    for k in range(1, S):
        small[S - k, k] = 1.0
    zero = np.zeros((S, S))
    lanes = np.block([[small, zero], [zero, -small]])
    rows = np.zeros((PAIR, PAIR))
    for i in range(1, PAIR):
        rows[i, PAIR - i] = 1.0
    return half(by_columns(lanes)), half(by_columns(rows))


def inverse_row_tables():
    a, i = np.arange(S)[:, None], np.arange(S)[None, :]
    blocks = []
    for q in range(SIDE):
        angles = ((SIDE * a + q) * i % P_SIZE) * (2.0 * np.pi / P_SIZE)
        blocks.append(by_columns(complex_block(np.cos(angles), np.sin(angles)) / np.sqrt(P_SIZE)))
    return half(np.concatenate(blocks))


def inverse_column_table(weight):
    cosine, sine = angle_tables()
    parts = [cosine.reshape(SIDE, 1, S, P_SIZE), -sine.reshape(SIDE, 1, S, P_SIZE)]
    return half(by_columns(np.concatenate(parts, axis=1).reshape(2 * P_SIZE, P_SIZE) * weight))


def dot(a, b):
    return jnp.dot(a, b, preferred_element_type=F32)


def restack(pair):
    top = jnp.concatenate([pair[:S, :S], pair[S:, :S]], axis=1)
    bottom = jnp.concatenate([pair[:S, S:], pair[S:, S:]], axis=1)
    return jnp.concatenate([top, bottom], axis=0)


def turn_pair(pair):
    return jnp.concatenate([pair[:, :S], pair[:, S:]], axis=0)


def prepare(slot_ref, plane_ref, count_ref, wk_ref, vis_ref, sky_ref, row_ref, gram_ref, half_ref, kern, kern_t, acc, held, loads, leave):
    acc[...] = jnp.zeros_like(acc)
    loads[0].wait()
    for w in range(WPLANES):
        real, imag = wk_ref[w, 0], wk_ref[w, 1]
        block = jnp.concatenate(
            [jnp.concatenate([real, -imag], axis=1), jnp.concatenate([imag, real], axis=1)], axis=0
        )
        real_t, imag_t = real.T, imag.T
        block_t = jnp.concatenate(
            [jnp.concatenate([real_t, imag_t], axis=1), jnp.concatenate([-imag_t, real_t], axis=1)], axis=0
        )
        kern[w] = block
        kern_t[w] = block_t
        gram_ref[w] = dot(block_t, block).astype(BF16)
    leave[0].start()

    loads[1].wait()
    loads[2].wait()
    for pc in range(SIDE):
        half_ref[:, pc * PAIR : (pc + 1) * PAIR] = dot(sky_ref[...], wide(row_ref, 2 * pc)).astype(BF16)
    leave[1].start()

    loads[3].wait()
    count = count_ref[0]

    def step(n, carry):
        for lane in range(UNROLL):
            t = jnp.maximum((n - 1) * UNROLL + lane, 0)
            slot = jnp.where(n > 0, slot_ref[t], F * NP)
            both = dot(kern_t[plane_ref[t]], held[lane, :, :S])
            acc[slot] = acc[slot] + jnp.concatenate([both[:S], both[S:]], axis=1)
        for lane in range(UNROLL):
            t = jnp.minimum(n * UNROLL + lane, TILE_CAP - 1)
            alive = jnp.where(n * UNROLL + lane < count, 1.0, 0.0).astype(F32)
            observed = jnp.concatenate([vis_ref[t, 0], vis_ref[t, 1]], axis=1)
            right = (dot(observed, kern[plane_ref[t]]) * alive).astype(BF16)
            held[lane, :, :S] = turn_pair(right)
        return carry

    lax.fori_loop(0, (count + UNROLL - 1) // UNROLL + 1, step, 0)


def degrid_grid(items_ref, base, count, gram_ref, grid_ref, acc, held):
    def step(n, carry):
        for lane in range(UNROLL):
            code = items_ref[base + n * UNROLL + lane]
            both = dot(gram_ref[code & (WPLANES - 1)], held[lane])
            for k, slot in enumerate(((code >> 4) & 63, (code >> 10) & 63)):
                cols = slice(k * S, (k + 1) * S)
                acc[slot] = acc[slot] - jnp.concatenate([both[:S, cols], both[S:, cols]], axis=1)
        for lane in range(UNROLL):
            code = items_ref[base + (n + 1) * UNROLL + lane]
            first, second = (code >> 4) & (SPARE - 1), (code >> 10) & (SPARE - 1)
            pair = jnp.concatenate([grid_ref[first], grid_ref[second]], axis=0)
            held[lane] = restack(dot(pair, gram_ref[code & (WPLANES - 1)]).astype(BF16))
        return carry

    lax.fori_loop(0, (count + UNROLL - 1) // UNROLL + 1, step, 0)


def both_cycles(
    facets, coef, base, count, pos, devices, items_ref, gram_ref, back_ref, half_of, tables, grid, acc, flip, held, keep_ref, send_ref
):
    column_ref, lanes_ref, rows_ref, inv_row_ref, inv_col_ref = tables[:5]
    loads = tables[5]

    def block(ref, facet, pc):
        first = facet * NP + pc * SIDE
        return ref[first : first + SIDE].reshape(P_SIZE, PAIR)

    def column_pass(cycle, facet, pc):
        part = half_of(cycle, facet, pc)
        turned = jnp.concatenate([part[:, S:], -part[:, :S]], axis=1)
        return dot(column_ref[...], jnp.concatenate([part, turned], axis=0))

    def place(ref, facet, pc, value):
        first = facet * NP + pc * SIDE
        ref[first : first + SIDE] = value.reshape(SIDE, S, PAIR)

    loads[0].wait()
    for facet in range(facets):
        for pc in range(SIDE):
            place(grid, facet, pc, column_pass(0, facet, pc).astype(BF16))
    degrid_grid(items_ref, base, count, gram_ref, grid, acc, held)

    loads[1].wait()
    loads[2].wait()
    lane = lax.broadcasted_iota(jnp.int32, (1, PAIR), 1)
    row = lax.broadcasted_iota(jnp.int32, (PAIR, 1), 0)
    sign = jnp.where(lane < S, 1.0, -1.0).astype(F32)
    for facet in range(facets):
        for pc in range(SIDE):
            place(flip, facet, pc, block(acc, facet, pc).astype(BF16))
        for pc in range(SIDE):
            turned = dot(block(flip, facet, SIDE - 1 - pc), wide(lanes_ref, 0))
            edge = block(flip, facet, (SIDE - pc) % SIDE).astype(F32) * sign
            mirrored = jnp.where(lane % S == 0, edge, turned)
            mirrored_half = mirrored.astype(BF16)
            fresh = column_pass(1, facet, pc)
            own = block(acc, facet, pc)
            parts = []
            for b in range(2):
                mine = slice(b * PAIR, (b + 1) * PAIR)
                other = slice((1 - b) * PAIR, (2 - b) * PAIR)
                swapped = dot(wide(rows_ref, 0), mirrored_half[other])
                swapped = jnp.where(row == 0, mirrored[mine], swapped)
                parts.append((fresh[mine] + coef * (own[mine] + swapped)).astype(BF16))
            place(grid, facet, pc, jnp.concatenate(parts, axis=0))
    for facet in range(facets):
        for pc in range(SIDE):
            place(acc, facet, pc, block(back_ref, facet, pc).astype(F32))
    degrid_grid(items_ref, base, count, gram_ref, grid, acc, held)

    loads[3].wait()
    loads[4].wait()
    share, far = S // devices, devices // 2
    for facet in range(facets):
        mixed = [[] for _ in range(SIDE)]
        for pc in range(SIDE):
            r0, r1, r2, r3 = (acc[facet * NP + pc * SIDE + p] for p in range(SIDE))
            even, odd = r0 + r2, r0 - r2
            even_b, odd_b = r1 + r3, r1 - r3
            turned = jnp.concatenate([-odd_b[:, S:], odd_b[:, :S]], axis=1)
            for q, value in enumerate((even + even_b, odd + turned, even - even_b, odd - turned)):
                mixed[q].append(turn_pair(value.astype(BF16)))
        for q in range(SIDE):
            spec = dot(wide(inv_row_ref, 2 * q), jnp.concatenate(mixed[q], axis=1)).astype(BF16)
            parts = []
            for pc in range(SIDE):
                cols = slice(pc * S, (pc + 1) * S)
                parts += [spec[:S, cols], spec[S:, cols]]
            spec = jnp.concatenate(parts, axis=1)
            image = jnp.concatenate([dot(spec, wide(inv_col_ref, j)) for j in range(0, SIDE, 2)], axis=1)
            if send_ref is None:
                keep_ref[facet, q] = image.astype(BF16)
                continue
            odd, mine = pos & 1, pos >> 1
            for there in range(far):
                zero = image[2 * there * share : (2 * there + 1) * share].astype(BF16)
                one = image[(2 * there + 1) * share : (2 * there + 2) * share].astype(BF16)
                offset = (there - mine + far) % far
                keep_ref[offset, facet, q] = jnp.where(odd == 0, zero, one)
                send_ref[offset, facet, q] = jnp.where(odd == 0, one, zero)


def copies(moves, sems, first=0):
    return [pltpu.make_async_copy(src, dst, sems.at[first + k]) for k, (src, dst) in enumerate(moves)]


def first_kernel(facets, rows, coef, devices, outs, *refs):
    pos_ref, items_ref, count_ref, slot_ref, plane_ref, live_ref = refs[:6]
    wk_hbm, vis_hbm, sky_hbm, row_hbm, column_hbm, *table_hbm = refs[6:15]
    gram_hbm, back_hbm, half_hbm, *images = refs[15 : 18 + outs]
    wk_ref, vis_ref, sky_ref, row_ref, column_ref, *table_refs = refs[18 + outs : 27 + outs]
    gram_ref, half_ref, back_ref, kern, kern_t, acc, grid, flip, held, sems = refs[27 + outs :]
    moves = [(wk_hbm, wk_ref), (sky_hbm, sky_ref), (row_hbm, row_ref), (vis_hbm, vis_ref), (column_hbm.at[pos_ref[0]], column_ref)]
    loads = copies(moves + list(zip(table_hbm, table_refs)), sems)
    for load in loads:
        load.start()
    later = facets * NP
    leave = copies(
        [(gram_ref, gram_hbm), (half_ref, half_hbm), (back_ref.at[pl.ds(later, F * NP - later)], back_hbm)], sems, len(loads)
    )
    prepare(
        slot_ref, plane_ref, live_ref, wk_ref, vis_ref, sky_ref, row_ref, gram_ref, half_ref, kern, kern_t, acc, held, loads, leave
    )
    for slot in range(0, F * NP, NP):
        back_ref[slot : slot + NP] = acc[slot : slot + NP].astype(BF16)
    leave[2].start()

    def half_of(cycle, facet, pc):
        first = (cycle * F + facet) * rows
        return half_ref[first : first + rows, pc * PAIR : (pc + 1) * PAIR]

    tables = (column_ref, *table_refs, loads[4:])
    keep_ref, send_ref = images if outs == 2 else (images[0], None)
    both_cycles(
        facets, coef, 0, count_ref[0], pos_ref[0], devices, items_ref, gram_ref, back_ref, half_of, tables, grid, acc, flip, held, keep_ref, send_ref
    )
    for out in leave:
        out.wait()


def later_kernel(facet, offset, base, part, rows, coef, devices, outs, *refs):
    pos_ref, items_ref, count_ref = refs[:3]
    gram_hbm, back_hbm, half_hbm, column_hbm, *table_hbm = refs[3:11]
    images = refs[11 : 11 + outs]
    gram_ref, back_ref, half_ref, column_ref, *table_refs = refs[11 + outs : 19 + outs]
    acc, grid, flip, held, sems = refs[19 + outs :]
    moves = [
        (half_hbm.at[pl.ds(facet * rows, rows)], half_ref.at[0]),
        (column_hbm.at[pos_ref[0]], column_ref),
        (back_hbm.at[pl.ds(offset, NP)], back_ref),
        (gram_hbm, gram_ref),
        (half_hbm.at[pl.ds((F + facet) * rows, rows)], half_ref.at[1]),
    ]
    loads = copies(moves + list(zip(table_hbm, table_refs)), sems)
    for load in loads:
        load.start()
    loads[2].wait()
    acc[:NP] = back_ref[...].astype(F32)
    for k in (0, 3, 4):
        loads[k].wait()

    def half_of(cycle, _, pc):
        return half_ref[cycle, :, pc * PAIR : (pc + 1) * PAIR]

    tables = (column_ref, *table_refs, [loads[1], *loads[5:]])
    keep_ref, send_ref = images if outs == 2 else (images[0], None)
    both_cycles(
        1, coef, base, count_ref[part], pos_ref[0], devices, items_ref, gram_ref, back_ref, half_of, tables, grid, acc, flip, held, keep_ref, send_ref
    )


def tile_lists(codes, stride):
    total = codes.shape[0]
    group = codes >> 6
    ids = jnp.arange(total, dtype=jnp.int32)
    same = (group[:, None] == group[None, :]) & (ids[None, :] < ids[:, None])
    rank = jnp.sum(same.astype(jnp.int32), axis=1)
    planes = jnp.arange(LISTS * WPLANES, dtype=jnp.int32)
    pairs = (jnp.sum((group[None, :] == planes[:, None]).astype(jnp.int32), axis=1) + 1) >> 1
    count = jnp.sum(pairs.reshape(LISTS, WPLANES), axis=1)
    which = codes >> 10
    earlier = (planes[None, :] < group[:, None]) & ((planes[None, :] >> 4) == which[:, None])
    base = jnp.sum(jnp.where(earlier, pairs[None, :], 0), axis=1)
    where = which * stride + UNROLL + base + (rank >> 1)
    slot, plane = codes & 63, (codes >> 6) & (WPLANES - 1)
    delta = jnp.where((rank & 1) == 0, plane + ((slot - SPARE) << 4), (slot - SPARE) << 10)
    places = jnp.arange(LISTS * stride, dtype=jnp.int32)
    hit = (places[:, None] == where[None, :]) & (which < LISTS)[None, :]
    items = (SPARE << 4) + (SPARE << 10) + jnp.sum(jnp.where(hit, delta[None, :], 0), axis=1)
    return items, count


def shift(value, offset, devices):
    return lax.ppermute(value, "vis", [(i, (i + offset) % devices) for i in range(devices)])


def split_image(image, position, devices):
    share, far = S // devices, devices // 2
    parts = image.reshape(-1, SIDE, far, 2, share, P_SIZE).transpose(3, 2, 0, 1, 4, 5)
    parts = jnp.roll(parts, -(position >> 1), axis=1)
    odd = position & 1
    return lax.dynamic_index_in_dim(parts, odd, 0, False), lax.dynamic_index_in_dim(parts, 1 - odd, 0, False)


def merge_pair(keep, taken):
    return [(keep[k].astype(F32) + taken[k].astype(F32)).astype(BF16) for k in range(1, keep.shape[0])]


def final_kernel(parts, *refs):
    *in_refs, out_ref, mixed = refs
    f = 0
    for group in range(len(in_refs) // parts):
        keep_ref, taken_ref, *others = in_refs[group * parts : (group + 1) * parts]
        for k in range(keep_ref.shape[1]):
            for q in range(SIDE):
                total = keep_ref[0, k, q].astype(F32) + taken_ref[0, k, q].astype(F32)
                for other in others:
                    total = total + other[k, q].astype(F32)
                for c in range(SIDE):
                    mixed[f, c, pl.ds(q, total.shape[0], stride=SIDE), :] = total[:, c * S : (c + 1) * S]
            for c in range(SIDE):
                out_ref[f, :, c * S : (c + 1) * S] = mixed[f, c]
            f += 1


def local(model_input, w_kernels, visibilities, tile_facet, tile_patch, tile_wplane, tile_count):
    devices = lax.axis_size("vis")
    position = lax.axis_index("vis").astype(jnp.int32)
    rows = P_SIZE // devices
    weight = math.sqrt(F * NP / (TILE_CAP * devices))
    total = TILE_CAP * devices
    stride = total // 2 + WPLANES // 2 + 3 * UNROLL
    coef = GAIN * weight / 2

    slots = tile_facet * NP + (tile_patch & 3) * SIDE + (tile_patch >> 2)
    live = jnp.arange(TILE_CAP, dtype=jnp.int32) < tile_count[0]
    which = jnp.maximum(tile_facet - (FIRST - 1), 0)
    near = jnp.where(tile_facet < FIRST, slots, slots & (NP - 1))
    codes = jnp.where(live, (which << 10) + (tile_wplane << 6) + near, LISTS << 10)
    all_codes = jnp.concatenate([codes] + [shift(codes, k, devices) for k in range(1, devices)])
    items, counts = tile_lists(all_codes, stride)

    lanes, row_flip = flip_tables()
    tables = [column_tables(devices), lanes, row_flip, inverse_row_tables(), inverse_column_table(weight)]
    tables = [jnp.asarray(t) for t in tables]
    here = position.reshape(1)
    smem = pl.BlockSpec(memory_space=pltpu.SMEM)
    vmem = pl.BlockSpec(memory_space=pltpu.VMEM)
    hbm = pl.BlockSpec(memory_space=pl.ANY)
    share, far = S // devices, devices // 2
    split = share % 16 == 0

    def image_shapes(facets):
        if split:
            return [jax.ShapeDtypeStruct((far, facets, SIDE, share, P_SIZE), BF16)] * 2
        return [jax.ShapeDtypeStruct((facets, SIDE, S, P_SIZE), BF16)]

    def halves_of(images):
        return images if split else split_image(images[0], position, devices)

    params = pltpu.CompilerParams(vmem_limit_bytes=VMEM_BYTES)
    outs = 2 if split else 1
    half_shape = (2 * F * rows, 2 * P_SIZE)
    gram_shape = (WPLANES, PAIR, PAIR)
    table_scratch = [pltpu.VMEM((P_SIZE, 2 * rows), BF16)] + [pltpu.VMEM(t.shape, BF16) for t in tables[1:]]

    gram, back, half_rows, *images = pl.pallas_call(
        functools.partial(first_kernel, FIRST, rows, coef, devices, outs),
        out_shape=[
            jax.ShapeDtypeStruct(gram_shape, BF16),
            jax.ShapeDtypeStruct(((F - FIRST) * NP, S, PAIR), BF16),
            jax.ShapeDtypeStruct(half_shape, BF16),
            *image_shapes(FIRST),
        ],
        in_specs=[smem] * 6 + [hbm] * 9,
        out_specs=[hbm] * 3 + [vmem] * outs,
        scratch_shapes=[
            pltpu.VMEM(w_kernels.shape, BF16),
            pltpu.VMEM(visibilities.shape, BF16),
            pltpu.VMEM((2 * F * rows, P_SIZE), BF16),
            pltpu.VMEM((2 * SIDE, P_SIZE, S), BF16),
            *table_scratch,
            pltpu.VMEM(gram_shape, BF16),
            pltpu.VMEM(half_shape, BF16),
            pltpu.VMEM((F * NP, S, PAIR), BF16),
            pltpu.VMEM(gram_shape, BF16),
            pltpu.VMEM(gram_shape, BF16),
            pltpu.VMEM((F * NP + 1, S, PAIR), F32),
            pltpu.VMEM((FIRST * NP, S, PAIR), BF16),
            pltpu.VMEM((FIRST * NP, S, PAIR), BF16),
            pltpu.VMEM((UNROLL, PAIR, PAIR), BF16),
            pltpu.SemaphoreType.DMA((12,)),
        ],
        compiler_params=params,
        cost_estimate=pl.CostEstimate(flops=30 * 10**9, bytes_accessed=12 * 2**20, transcendentals=0),
        name="first",
    )(
        here,
        items,
        counts,
        slots,
        tile_wplane,
        tile_count,
        w_kernels,
        visibilities,
        model_input.reshape(2 * F * rows, P_SIZE),
        jnp.asarray(row_table()),
        *tables,
    )

    neighbour = [(i, i ^ 1) for i in range(devices)]
    keep, send = halves_of(images)
    pairs = [(keep, lax.ppermute(send, "vis", neighbour))]
    merged, others = [], []

    def to_each_z(group):
        merged.append(merge_pair(*pairs[group]))
        others.append([shift(part, 2 * k, devices) for k, part in enumerate(merged[-1], 1)])

    for facet in range(FIRST, F):
        part = facet - FIRST + 1
        if part == 2:
            to_each_z(0)
            here, _ = lax.optimization_barrier((here, merged[0]))
        images = pl.pallas_call(
            functools.partial(
                later_kernel, facet, (facet - FIRST) * NP, part * stride, part, rows, coef, devices, outs
            ),
            out_shape=image_shapes(1),
            in_specs=[smem] * 3 + [hbm] * 8,
            out_specs=[vmem] * outs,
            scratch_shapes=[
                pltpu.VMEM(gram_shape, BF16),
                pltpu.VMEM((NP, S, PAIR), BF16),
                pltpu.VMEM((2, rows, 2 * P_SIZE), BF16),
                *table_scratch,
                pltpu.VMEM((SPARE + 1, S, PAIR), F32),
                pltpu.VMEM((NP, S, PAIR), BF16),
                pltpu.VMEM((NP, S, PAIR), BF16),
                pltpu.VMEM((UNROLL, PAIR, PAIR), BF16),
                pltpu.SemaphoreType.DMA((9,)),
            ],
            compiler_params=params,
            cost_estimate=pl.CostEstimate(flops=14 * 10**9, bytes_accessed=6 * 2**20, transcendentals=0),
            name="facet",
        )(here, items, counts, gram, back, half_rows, *tables)
        keep, send = halves_of(images)
        if part == 2:
            send, others[0] = lax.optimization_barrier((send, others[0]))
        pairs.append((keep, lax.ppermute(send, "vis", neighbour)))
    for group in range(1, LISTS):
        to_each_z(group)

    in_specs, operands = [], []
    for pair, other in zip(pairs, others):
        block = (1,) + pair[0].shape[1:]
        in_specs += [pl.BlockSpec(block, lambda i: (0, 0, 0, 0, 0))] * 2 + [vmem] * len(other)
        operands += [*pair, *other]
    return pl.pallas_call(
        functools.partial(final_kernel, len(operands) // LISTS),
        out_shape=jax.ShapeDtypeStruct((F, rows, P_SIZE), F32),
        grid=(1,),
        in_specs=in_specs,
        out_specs=vmem,
        scratch_shapes=[pltpu.VMEM((F, SIDE, rows, S), F32)],
        cost_estimate=pl.CostEstimate(flops=10**6, bytes_accessed=2**20, transcendentals=0),
        name="final",
    )(*operands)


def solution(mesh):
    return jax.shard_map(
        local,
        mesh=mesh,
        in_specs=(
            P(None, "freq", "vis", None),
            P("freq", None, None, None),
            P(("freq", "vis"), None, None, None),
            P(("freq", "vis")),
            P(("freq", "vis")),
            P(("freq", "vis")),
            P(("freq", "vis")),
        ),
        out_specs=P("freq", "vis", None),
        check_vma=False,
    )
```

```python
import functools
import math

import jax
import jax.numpy as jnp
import ml_dtypes
import numpy as np
from jax import lax
from jax.experimental import pallas as pl
from jax.experimental.pallas import tpu as pltpu
from jax.sharding import PartitionSpec as P

P_SIZE = 512
S = 128
F = 4
WPLANES = 16
TILE_CAP = 32
NP = 16
SIDE = P_SIZE // S
PAIR = 2 * S
UNROLL = 4
FIRST = 2
LISTS = F - FIRST + 1
SPARE = FIRST * NP
GAIN = 0.5
VMEM_BYTES = 60 * 1024 * 1024

BF16 = jnp.bfloat16
F32 = jnp.float32


def angle_tables():
    index = np.arange(P_SIZE)
    angles = (index[:, None] * index[None, :] % P_SIZE) * (2.0 * np.pi / P_SIZE)
    return np.cos(angles) / np.sqrt(P_SIZE), np.sin(angles) / np.sqrt(P_SIZE)


def half(array):
    return np.asarray(array, np.float32).astype(ml_dtypes.bfloat16)


def complex_block(real, imag):
    return np.block([[real, -imag], [imag, real]])


def by_columns(table):
    rows, columns = table.shape
    return table.reshape(rows, columns // S, S).transpose(1, 0, 2)


def wide(ref, chunk):
    return jnp.concatenate([ref[chunk], ref[chunk + 1]], axis=1)


def row_table():
    cosine, sine = angle_tables()
    parts = [cosine.reshape(P_SIZE, SIDE, 1, S), -sine.reshape(P_SIZE, SIDE, 1, S)]
    return half(by_columns(np.concatenate(parts, axis=2).reshape(P_SIZE, 2 * P_SIZE)))


def column_tables(devices):
    cosine, sine = angle_tables()
    rows = P_SIZE // devices
    parts = [t.reshape(P_SIZE, devices, rows).transpose(1, 0, 2) for t in (cosine, sine)]
    return half(np.concatenate(parts, axis=2))


def flip_tables():
    small = np.zeros((S, S))
    for k in range(1, S):
        small[S - k, k] = 1.0
    zero = np.zeros((S, S))
    lanes = np.block([[small, zero], [zero, -small]])
    rows = np.zeros((PAIR, PAIR))
    for i in range(1, PAIR):
        rows[i, PAIR - i] = 1.0
    return half(by_columns(lanes)), half(by_columns(rows))


def inverse_row_tables():
    a, i = np.arange(S)[:, None], np.arange(S)[None, :]
    blocks = []
    for q in range(SIDE):
        angles = ((SIDE * a + q) * i % P_SIZE) * (2.0 * np.pi / P_SIZE)
        blocks.append(by_columns(complex_block(np.cos(angles), np.sin(angles)) / np.sqrt(P_SIZE)))
    return half(np.concatenate(blocks))


def inverse_column_table(weight):
    cosine, sine = angle_tables()
    parts = [cosine.reshape(SIDE, 1, S, P_SIZE), -sine.reshape(SIDE, 1, S, P_SIZE)]
    return half(by_columns(np.concatenate(parts, axis=1).reshape(2 * P_SIZE, P_SIZE) * weight))


def dot(a, b):
    return jnp.dot(a, b, preferred_element_type=F32)


def restack(pair):
    top = jnp.concatenate([pair[:S, :S], pair[S:, :S]], axis=1)
    bottom = jnp.concatenate([pair[:S, S:], pair[S:, S:]], axis=1)
    return jnp.concatenate([top, bottom], axis=0)


def turn_pair(pair):
    return jnp.concatenate([pair[:, :S], pair[:, S:]], axis=0)


def prepare(slot_ref, plane_ref, count_ref, wk_ref, vis_ref, sky_ref, row_ref, gram_ref, half_ref, kern, kern_t, acc, held, loads, leave):
    acc[...] = jnp.zeros_like(acc)
    loads[0].wait()
    for load in loads[4:]:
        load.start()
    for w in range(WPLANES):
        real, imag = wk_ref[w, 0], wk_ref[w, 1]
        block = jnp.concatenate(
            [jnp.concatenate([real, -imag], axis=1), jnp.concatenate([imag, real], axis=1)], axis=0
        )
        real_t, imag_t = real.T, imag.T
        block_t = jnp.concatenate(
            [jnp.concatenate([real_t, imag_t], axis=1), jnp.concatenate([-imag_t, real_t], axis=1)], axis=0
        )
        kern[w] = block
        kern_t[w] = block_t
        gram_ref[w] = dot(block_t, block).astype(BF16)
    leave[0].start()

    loads[1].wait()
    loads[2].wait()
    for pc in range(SIDE):
        half_ref[:, pc * PAIR : (pc + 1) * PAIR] = dot(sky_ref[...], wide(row_ref, 2 * pc)).astype(BF16)
    leave[1].start()

    loads[3].wait()
    count = count_ref[0]

    def step(n, carry):
        for lane in range(UNROLL):
            t = jnp.maximum((n - 1) * UNROLL + lane, 0)
            slot = jnp.where(n > 0, slot_ref[t], F * NP)
            both = dot(kern_t[plane_ref[t]], held[lane, :, :S])
            acc[slot] = acc[slot] + jnp.concatenate([both[:S], both[S:]], axis=1)
        for lane in range(UNROLL):
            t = jnp.minimum(n * UNROLL + lane, TILE_CAP - 1)
            alive = jnp.where(n * UNROLL + lane < count, 1.0, 0.0).astype(F32)
            observed = jnp.concatenate([vis_ref[t, 0], vis_ref[t, 1]], axis=1)
            right = (dot(observed, kern[plane_ref[t]]) * alive).astype(BF16)
            held[lane, :, :S] = turn_pair(right)
        return carry

    lax.fori_loop(0, (count + UNROLL - 1) // UNROLL + 1, step, 0)


def degrid_grid(items_ref, base, times, count, gram_ref, grid_ref, acc, held):
    def step(n, carry):
        for lane in range(UNROLL):
            code = items_ref[base + n * UNROLL + lane]
            both = dot(gram_ref[code & (WPLANES - 1)], held[lane])
            for k, slot in enumerate(((code >> 4) & 63, (code >> 10) & 63)):
                cols = slice(k * S, (k + 1) * S)
                acc[slot] = acc[slot] - jnp.concatenate([both[:S, cols], both[S:, cols]], axis=1)
        for lane in range(UNROLL):
            code = items_ref[base + (n + 1) * UNROLL + lane]
            first, second = (code >> 4) & (SPARE - 1), (code >> 10) & (SPARE - 1)
            pair = jnp.concatenate([grid_ref[first], grid_ref[second]], axis=0)
            right = dot(pair, gram_ref[code & (WPLANES - 1)])
            equal = items_ref[times + base + (n + 1) * UNROLL + lane]
            right = [right[:S] * (equal & 0xFFFF).astype(F32), right[S:] * (equal >> 16).astype(F32)]
            held[lane] = restack(jnp.concatenate(right, axis=0).astype(BF16))
        return carry

    lax.fori_loop(0, (count + UNROLL - 1) // UNROLL + 1, step, 0)


def both_cycles(
    facets, coef, base, times, count, pos, devices, items_ref, gram_ref, back_ref, half_of, tables, grid, acc, flip, held, keep_ref, send_ref
):
    column_ref, lanes_ref, rows_ref, inv_row_ref, inv_col_ref = tables[:5]
    loads = tables[5]

    def block(ref, facet, pc):
        first = facet * NP + pc * SIDE
        return ref[first : first + SIDE].reshape(P_SIZE, PAIR)

    def column_pass(cycle, facet, pc):
        part = half_of(cycle, facet, pc)
        turned = jnp.concatenate([part[:, S:], -part[:, :S]], axis=1)
        return dot(column_ref[...], jnp.concatenate([part, turned], axis=0))

    def place(ref, facet, pc, value):
        first = facet * NP + pc * SIDE
        ref[first : first + SIDE] = value.reshape(SIDE, S, PAIR)

    loads[1].wait()
    for facet in range(facets):
        for pc in range(SIDE):
            place(grid, facet, pc, column_pass(0, facet, pc).astype(BF16))
    if loads[0] is not None:
        loads[0].wait()
    degrid_grid(items_ref, base, times, count, gram_ref, grid, acc, held)

    for load in loads[2:5]:
        if load is not None:
            load.wait()
    lane = lax.broadcasted_iota(jnp.int32, (1, PAIR), 1)
    row = lax.broadcasted_iota(jnp.int32, (PAIR, 1), 0)
    sign = jnp.where(lane < S, 1.0, -1.0).astype(F32)
    for facet in range(facets):
        for pc in range(SIDE):
            place(flip, facet, pc, block(acc, facet, pc).astype(BF16))
        for pc in range(SIDE):
            turned = dot(block(flip, facet, SIDE - 1 - pc), wide(lanes_ref, 0))
            edge = block(flip, facet, (SIDE - pc) % SIDE).astype(F32) * sign
            mirrored = jnp.where(lane % S == 0, edge, turned)
            mirrored_half = mirrored.astype(BF16)
            fresh = column_pass(1, facet, pc)
            own = block(acc, facet, pc)
            parts = []
            for b in range(2):
                mine = slice(b * PAIR, (b + 1) * PAIR)
                other = slice((1 - b) * PAIR, (2 - b) * PAIR)
                swapped = dot(wide(rows_ref, 0), mirrored_half[other])
                swapped = jnp.where(row == 0, mirrored[mine], swapped)
                parts.append((fresh[mine] + coef * (own[mine] + swapped)).astype(BF16))
            place(grid, facet, pc, jnp.concatenate(parts, axis=0))
    for facet in range(facets):
        for pc in range(SIDE):
            place(acc, facet, pc, block(back_ref, facet, pc).astype(F32))
    degrid_grid(items_ref, base, times, count, gram_ref, grid, acc, held)

    loads[5].wait()
    loads[6].wait()
    share, far = S // devices, devices // 2
    for facet in range(facets):
        mixed = [[] for _ in range(SIDE)]
        for pc in range(SIDE):
            r0, r1, r2, r3 = (acc[facet * NP + pc * SIDE + p] for p in range(SIDE))
            even, odd = r0 + r2, r0 - r2
            even_b, odd_b = r1 + r3, r1 - r3
            turned = jnp.concatenate([-odd_b[:, S:], odd_b[:, :S]], axis=1)
            for q, value in enumerate((even + even_b, odd + turned, even - even_b, odd - turned)):
                mixed[q].append(turn_pair(value.astype(BF16)))
        for q in range(SIDE):
            spec = dot(wide(inv_row_ref, 2 * q), jnp.concatenate(mixed[q], axis=1)).astype(BF16)
            parts = []
            for pc in range(SIDE):
                cols = slice(pc * S, (pc + 1) * S)
                parts += [spec[:S, cols], spec[S:, cols]]
            spec = jnp.concatenate(parts, axis=1)
            image = jnp.concatenate([dot(spec, wide(inv_col_ref, j)) for j in range(0, SIDE, 2)], axis=1)
            if send_ref is None:
                keep_ref[facet, q] = image.astype(BF16)
                continue
            odd, mine = pos & 1, pos >> 1
            for there in range(far):
                zero = image[2 * there * share : (2 * there + 1) * share].astype(BF16)
                one = image[(2 * there + 1) * share : (2 * there + 2) * share].astype(BF16)
                offset = (there - mine + far) % far
                keep_ref[offset, facet, q] = jnp.where(odd == 0, zero, one)
                send_ref[offset, facet, q] = jnp.where(odd == 0, one, zero)


def copies(moves, sems, first=0):
    return [pltpu.make_async_copy(src, dst, sems.at[first + k]) for k, (src, dst) in enumerate(moves)]


def first_kernel(facets, times, rows, coef, devices, outs, *refs):
    pos_ref, items_ref, slot_ref, plane_ref, live_ref = refs[:5]
    wk_hbm, vis_hbm, sky_hbm, row_hbm, column_hbm, *table_hbm = refs[5:14]
    gram_hbm, back_hbm, half_hbm, *images = refs[14 : 17 + outs]
    wk_ref, vis_ref, sky_ref, row_ref, column_ref, *table_refs = refs[17 + outs : 26 + outs]
    gram_ref, half_ref, back_ref, kern, kern_t, acc, grid, flip, held, sems = refs[26 + outs :]
    moves = [(wk_hbm, wk_ref), (sky_hbm, sky_ref), (row_hbm, row_ref), (vis_hbm, vis_ref), (column_hbm.at[pos_ref[0]], column_ref)]
    loads = copies(moves + list(zip(table_hbm, table_refs)), sems)
    for load in loads[:4]:
        load.start()
    later = facets * NP
    leave = copies(
        [(gram_ref, gram_hbm), (half_ref, half_hbm), (back_ref.at[pl.ds(later, F * NP - later)], back_hbm)], sems, len(loads)
    )
    prepare(
        slot_ref, plane_ref, live_ref, wk_ref, vis_ref, sky_ref, row_ref, gram_ref, half_ref, kern, kern_t, acc, held, loads, leave
    )
    for slot in range(0, F * NP, NP):
        back_ref[slot : slot + NP] = acc[slot : slot + NP].astype(BF16)
    leave[2].start()

    def half_of(cycle, facet, pc):
        first = (cycle * F + facet) * rows
        return half_ref[first : first + rows, pc * PAIR : (pc + 1) * PAIR]

    tables = (column_ref, *table_refs, [None, loads[4], None, *loads[5:]])
    keep_ref, send_ref = images if outs == 2 else (images[0], None)
    both_cycles(
        facets, coef, 0, times, items_ref[2 * times], pos_ref[0], devices, items_ref, gram_ref, back_ref, half_of, tables, grid, acc, flip, held, keep_ref, send_ref
    )
    for out in leave:
        out.wait()


def later_kernel(facet, offset, base, times, part, rows, coef, devices, outs, *refs):
    pos_ref, items_ref = refs[:2]
    gram_hbm, back_hbm, half_hbm, column_hbm, *table_hbm = refs[2:10]
    images = refs[10 : 10 + outs]
    gram_ref, back_ref, half_ref, column_ref, *table_refs = refs[10 + outs : 18 + outs]
    acc, grid, flip, held, sems = refs[18 + outs :]
    moves = [
        (half_hbm.at[pl.ds(facet * rows, rows)], half_ref.at[0]),
        (column_hbm.at[pos_ref[0]], column_ref),
        (back_hbm.at[pl.ds(offset, NP)], back_ref),
        (gram_hbm, gram_ref),
        (half_hbm.at[pl.ds((F + facet) * rows, rows)], half_ref.at[1]),
    ]
    loads = copies(moves + list(zip(table_hbm, table_refs)), sems)
    for load in loads[:4]:
        load.start()
    loads[2].wait()
    acc[:NP] = back_ref[...].astype(F32)
    for load in loads[4:]:
        load.start()
    loads[0].wait()

    def half_of(cycle, _, pc):
        return half_ref[cycle, :, pc * PAIR : (pc + 1) * PAIR]

    tables = (column_ref, *table_refs, [loads[3], loads[1], *loads[4:]])
    keep_ref, send_ref = images if outs == 2 else (images[0], None)
    both_cycles(
        1, coef, base, times, items_ref[2 * times + part], pos_ref[0], devices, items_ref, gram_ref, back_ref, half_of, tables, grid, acc, flip, held, keep_ref, send_ref
    )


def tile_lists(codes, stride):
    total = codes.shape[0]
    ids = jnp.arange(total, dtype=jnp.int32)
    before = ids[None, :] < ids[:, None]
    equal = codes[:, None] == codes[None, :]
    again = jnp.sum((equal & before).astype(jnp.int32), axis=1) > 0
    times = jnp.sum(equal.astype(jnp.int32), axis=1)
    group = jnp.where(again, LISTS * WPLANES, codes >> 6)
    rank = jnp.sum(((group[:, None] == group[None, :]) & before).astype(jnp.int32), axis=1)
    planes = jnp.arange(LISTS * WPLANES, dtype=jnp.int32)
    pairs = (jnp.sum((group[None, :] == planes[:, None]).astype(jnp.int32), axis=1) + 1) >> 1
    which = group >> 4
    earlier = (planes[None, :] < group[:, None]) & ((planes[None, :] >> 4) == which[:, None])
    base = jnp.sum(jnp.where(earlier, pairs[None, :], 0), axis=1)
    where = which * stride + UNROLL + base + (rank >> 1)
    slot, plane = codes & 63, (codes >> 6) & (WPLANES - 1)
    even = (rank & 1) == 0
    delta = jnp.where(even, plane + ((slot - SPARE) << 4), (slot - SPARE) << 10)
    places = jnp.arange(LISTS * stride, dtype=jnp.int32)
    hit = (places[:, None] == where[None, :]) & (which < LISTS)[None, :]
    items = (SPARE << 4) + (SPARE << 10) + jnp.sum(jnp.where(hit, delta[None, :], 0), axis=1)
    times = jnp.sum(jnp.where(hit, jnp.where(even, times, times << 16)[None, :], 0), axis=1)
    counts = jnp.sum(pairs.reshape(LISTS, WPLANES), axis=1)
    return jnp.concatenate([items, times, counts])


def shift(value, offset, devices):
    return lax.ppermute(value, "vis", [(i, (i + offset) % devices) for i in range(devices)])


def split_image(image, position, devices):
    share, far = S // devices, devices // 2
    parts = image.reshape(-1, SIDE, far, 2, share, P_SIZE).transpose(3, 2, 0, 1, 4, 5)
    parts = jnp.roll(parts, -(position >> 1), axis=1)
    odd = position & 1
    return lax.dynamic_index_in_dim(parts, odd, 0, False), lax.dynamic_index_in_dim(parts, 1 - odd, 0, False)


def merge_pair(keep, taken):
    return [(keep[k].astype(F32) + taken[k].astype(F32)).astype(BF16) for k in range(1, keep.shape[0])]


def final_kernel(parts, groups, *refs):
    out_ref, mixed = refs[-2:]
    f = 0
    for group in range(groups):
        keep_ref, taken_ref, *others = refs[group * parts : (group + 1) * parts]
        for k in range(keep_ref.shape[1]):
            for q in range(SIDE):
                total = keep_ref[0, k, q].astype(F32) + taken_ref[0, k, q].astype(F32)
                for other in others:
                    total = total + other[k, q].astype(F32)
                for c in range(SIDE):
                    mixed[f, c, pl.ds(q, total.shape[0], stride=SIDE), :] = total[:, c * S : (c + 1) * S]
            for c in range(SIDE):
                out_ref[f, :, c * S : (c + 1) * S] = mixed[f, c]
            f += 1


def local(model_input, w_kernels, visibilities, tile_facet, tile_patch, tile_wplane, tile_count):
    devices = lax.axis_size("vis")
    position = lax.axis_index("vis").astype(jnp.int32)
    rows = P_SIZE // devices
    weight = math.sqrt(F * NP / (TILE_CAP * devices))
    total = TILE_CAP * devices
    stride = total // 2 + WPLANES // 2 + 3 * UNROLL
    coef = GAIN * weight / 2

    slots = tile_facet * NP + (tile_patch & 3) * SIDE + (tile_patch >> 2)
    live = jnp.arange(TILE_CAP, dtype=jnp.int32) < tile_count[0]
    which = jnp.maximum(tile_facet - (FIRST - 1), 0)
    near = jnp.where(tile_facet < FIRST, slots, slots & (NP - 1))
    codes = jnp.where(live, (which << 10) + (tile_wplane << 6) + near, LISTS << 10)
    neighbour = [(i, i ^ 1) for i in range(devices)]
    codes = jnp.concatenate([codes, lax.ppermute(codes, "vis", neighbour)])
    all_codes = jnp.concatenate([codes] + [shift(codes, 2 * k, devices) for k in range(1, devices // 2)])
    items = tile_lists(all_codes, stride)

    lanes, row_flip = flip_tables()
    tables = [column_tables(devices), lanes, row_flip, inverse_row_tables(), inverse_column_table(weight)]
    tables = [jnp.asarray(t) for t in tables]
    here = position.reshape(1)
    smem = pl.BlockSpec(memory_space=pltpu.SMEM)
    vmem = pl.BlockSpec(memory_space=pltpu.VMEM)
    hbm = pl.BlockSpec(memory_space=pl.ANY)
    share, far = S // devices, devices // 2
    split = share % 16 == 0

    def image_shapes(facets):
        if split:
            return [jax.ShapeDtypeStruct((far, facets, SIDE, share, P_SIZE), BF16)] * 2
        return [jax.ShapeDtypeStruct((facets, SIDE, S, P_SIZE), BF16)]

    def halves_of(images):
        return images if split else split_image(images[0], position, devices)

    params = pltpu.CompilerParams(vmem_limit_bytes=VMEM_BYTES)
    outs = 2 if split else 1
    half_shape = (2 * F * rows, 2 * P_SIZE)
    gram_shape = (WPLANES, PAIR, PAIR)
    table_scratch = [pltpu.VMEM((P_SIZE, 2 * rows), BF16)] + [pltpu.VMEM(t.shape, BF16) for t in tables[1:]]

    gram, back, half_rows, *images = pl.pallas_call(
        functools.partial(first_kernel, FIRST, LISTS * stride, rows, coef, devices, outs),
        out_shape=[
            jax.ShapeDtypeStruct(gram_shape, BF16),
            jax.ShapeDtypeStruct(((F - FIRST) * NP, S, PAIR), BF16),
            jax.ShapeDtypeStruct(half_shape, BF16),
            *image_shapes(FIRST),
        ],
        in_specs=[smem] * 5 + [hbm] * 9,
        out_specs=[hbm] * 3 + [vmem] * outs,
        scratch_shapes=[
            pltpu.VMEM(w_kernels.shape, BF16),
            pltpu.VMEM(visibilities.shape, BF16),
            pltpu.VMEM((2 * F * rows, P_SIZE), BF16),
            pltpu.VMEM((2 * SIDE, P_SIZE, S), BF16),
            *table_scratch,
            pltpu.VMEM(gram_shape, BF16),
            pltpu.VMEM(half_shape, BF16),
            pltpu.VMEM((F * NP, S, PAIR), BF16),
            pltpu.VMEM(gram_shape, BF16),
            pltpu.VMEM(gram_shape, BF16),
            pltpu.VMEM((F * NP + 1, S, PAIR), F32),
            pltpu.VMEM((FIRST * NP, S, PAIR), BF16),
            pltpu.VMEM((FIRST * NP, S, PAIR), BF16),
            pltpu.VMEM((UNROLL, PAIR, PAIR), BF16),
            pltpu.SemaphoreType.DMA((12,)),
        ],
        compiler_params=params,
        cost_estimate=pl.CostEstimate(flops=30 * 10**9, bytes_accessed=12 * 2**20, transcendentals=0),
        name="first",
    )(
        here,
        items,
        slots,
        tile_wplane,
        tile_count,
        w_kernels,
        visibilities,
        model_input.reshape(2 * F * rows, P_SIZE),
        jnp.asarray(row_table()),
        *tables,
    )

    keep, send = halves_of(images)
    pairs = [(keep, lax.ppermute(send, "vis", neighbour))]
    merged, others = [], []

    def to_each_z(group):
        merged.append(merge_pair(*pairs[group]))
        others.append([shift(part, 2 * k, devices) for k, part in enumerate(merged[-1], 1)])

    for facet in range(FIRST, F):
        part = facet - FIRST + 1
        if part == 2:
            to_each_z(0)
            here, _ = lax.optimization_barrier((here, merged[0]))
        images = pl.pallas_call(
            functools.partial(
                later_kernel, facet, (facet - FIRST) * NP, part * stride, LISTS * stride, part, rows, coef, devices, outs
            ),
            out_shape=image_shapes(1),
            in_specs=[smem] * 2 + [hbm] * 8,
            out_specs=[vmem] * outs,
            scratch_shapes=[
                pltpu.VMEM(gram_shape, BF16),
                pltpu.VMEM((NP, S, PAIR), BF16),
                pltpu.VMEM((2, rows, 2 * P_SIZE), BF16),
                *table_scratch,
                pltpu.VMEM((SPARE + 1, S, PAIR), F32),
                pltpu.VMEM((NP, S, PAIR), BF16),
                pltpu.VMEM((NP, S, PAIR), BF16),
                pltpu.VMEM((UNROLL, PAIR, PAIR), BF16),
                pltpu.SemaphoreType.DMA((9,)),
            ],
            compiler_params=params,
            cost_estimate=pl.CostEstimate(flops=14 * 10**9, bytes_accessed=6 * 2**20, transcendentals=0),
            name="facet",
        )(here, items, gram, back, half_rows, *tables)
        keep, send = halves_of(images)
        if part == 2:
            send, others[0] = lax.optimization_barrier((send, others[0]))
        pairs.append((keep, lax.ppermute(send, "vis", neighbour)))
    for group in range(1, LISTS):
        to_each_z(group)

    def finish(groups, first, facets, before):
        in_specs, operands = [], []
        for group in groups:
            block = (1,) + pairs[group][0].shape[1:]
            in_specs += [pl.BlockSpec(block, lambda i: (0, 0, 0, 0, 0))] * 2 + [vmem] * len(others[group])
            operands += [*pairs[group], *others[group]]
        parts = len(operands) // len(groups)
        aliases = {len(operands): 0} if before else {}
        return pl.pallas_call(
            functools.partial(final_kernel, parts, len(groups)),
            out_shape=jax.ShapeDtypeStruct((F, rows, P_SIZE), F32),
            grid=(1,),
            in_specs=in_specs + [hbm] * len(before),
            out_specs=pl.BlockSpec((facets, rows, P_SIZE), lambda i: (first // facets, 0, 0)),
            scratch_shapes=[pltpu.VMEM((facets, SIDE, rows, S), F32)],
            input_output_aliases=aliases,
            cost_estimate=pl.CostEstimate(flops=10**6, bytes_accessed=2**20, transcendentals=0),
            name="final",
        )(*operands, *before)

    done = finish(range(LISTS - 1), 0, F - 1, [])
    return finish([LISTS - 1], F - 1, 1, [done])


def solution(mesh):
    return jax.shard_map(
        local,
        mesh=mesh,
        in_specs=(
            P(None, "freq", "vis", None),
            P("freq", None, None, None),
            P(("freq", "vis"), None, None, None),
            P(("freq", "vis")),
            P(("freq", "vis")),
            P(("freq", "vis")),
            P(("freq", "vis")),
        ),
        out_specs=P("freq", "vis", None),
        check_vma=False,
    )
```

```python
import functools
import math

import jax
import jax.numpy as jnp
import ml_dtypes
import numpy as np
from jax import lax
from jax.experimental import pallas as pl
from jax.experimental.pallas import tpu as pltpu
from jax.sharding import PartitionSpec as P

P_SIZE = 512
S = 128
F = 4
WPLANES = 16
TILE_CAP = 32
NP = 16
SIDE = P_SIZE // S
PAIR = 2 * S
UNROLL = 6
PREP_UNROLL = 8
FIRST = 2
LISTS = F - FIRST + 1
SPARE = FIRST * NP
GAIN = 0.5
VMEM_BYTES = 60 * 1024 * 1024
FINAL_VMEM = 6 * 1024 * 1024

BF16 = jnp.bfloat16
F32 = jnp.float32


def angle_tables():
    index = np.arange(P_SIZE)
    angles = (index[:, None] * index[None, :] % P_SIZE) * (2.0 * np.pi / P_SIZE)
    return np.cos(angles) / np.sqrt(P_SIZE), np.sin(angles) / np.sqrt(P_SIZE)


def half(array):
    return np.asarray(array, np.float32).astype(ml_dtypes.bfloat16)


def complex_block(real, imag):
    return np.block([[real, -imag], [imag, real]])


def by_columns(table):
    rows, columns = table.shape
    return table.reshape(rows, columns // S, S).transpose(1, 0, 2)


def wide(ref, chunk):
    return jnp.concatenate([ref[chunk], ref[chunk + 1]], axis=1)


def row_table():
    cosine, sine = angle_tables()
    parts = [cosine.reshape(P_SIZE, SIDE, 1, S), -sine.reshape(P_SIZE, SIDE, 1, S)]
    return half(by_columns(np.concatenate(parts, axis=2).reshape(P_SIZE, 2 * P_SIZE)))


def column_tables(devices):
    cosine, sine = angle_tables()
    rows = P_SIZE // devices
    parts = [t.reshape(P_SIZE, devices, rows).transpose(1, 0, 2) for t in (cosine, sine)]
    return half(np.concatenate(parts, axis=2))


def flip_tables():
    small = np.zeros((S, S))
    for k in range(1, S):
        small[S - k, k] = 1.0
    zero = np.zeros((S, S))
    lanes = np.block([[small, zero], [zero, -small]])
    rows = np.zeros((PAIR, PAIR))
    for i in range(1, PAIR):
        rows[i, PAIR - i] = 1.0
    return half(by_columns(lanes)), half(by_columns(rows))


def inverse_row_tables():
    a, i = np.arange(S)[:, None], np.arange(S)[None, :]
    blocks = []
    for q in range(SIDE):
        angles = ((SIDE * a + q) * i % P_SIZE) * (2.0 * np.pi / P_SIZE)
        blocks.append(by_columns(complex_block(np.cos(angles), np.sin(angles)) / np.sqrt(P_SIZE)))
    return half(np.concatenate(blocks))


def inverse_column_table(weight):
    cosine, sine = angle_tables()
    parts = [cosine.reshape(SIDE, 1, S, P_SIZE), -sine.reshape(SIDE, 1, S, P_SIZE)]
    return half(by_columns(np.concatenate(parts, axis=1).reshape(2 * P_SIZE, P_SIZE) * weight))


def dot(a, b):
    return jnp.dot(a, b, preferred_element_type=F32)


def restack(pair):
    top = jnp.concatenate([pair[:S, :S], pair[S:, :S]], axis=1)
    bottom = jnp.concatenate([pair[:S, S:], pair[S:, S:]], axis=1)
    return jnp.concatenate([top, bottom], axis=0)


def turn_pair(pair):
    return jnp.concatenate([pair[:, :S], pair[:, S:]], axis=0)


def prepare(slot_ref, plane_ref, count_ref, wk_ref, vis_ref, sky_ref, row_ref, gram_ref, half_ref, kern, kern_t, acc, held, loads, leave):
    acc[...] = jnp.zeros_like(acc)
    loads[0].wait()
    for load in loads[4:]:
        load.start()
    for w in range(WPLANES):
        real, imag = wk_ref[w, 0], wk_ref[w, 1]
        block = jnp.concatenate(
            [jnp.concatenate([real, -imag], axis=1), jnp.concatenate([imag, real], axis=1)], axis=0
        )
        real_t, imag_t = real.T, imag.T
        block_t = jnp.concatenate(
            [jnp.concatenate([real_t, imag_t], axis=1), jnp.concatenate([-imag_t, real_t], axis=1)], axis=0
        )
        kern[w] = block
        kern_t[w] = block_t
        gram_ref[w] = dot(block_t, block).astype(BF16)
    leave[0].start()

    loads[1].wait()
    loads[2].wait()
    for pc in range(SIDE):
        half_ref[:, pc * PAIR : (pc + 1) * PAIR] = dot(sky_ref[...], wide(row_ref, 2 * pc)).astype(BF16)
    leave[1].start()

    loads[3].wait()
    count = count_ref[0]

    def right_products(n):
        for lane in range(PREP_UNROLL):
            t = jnp.minimum(n * PREP_UNROLL + lane, TILE_CAP - 1)
            alive = jnp.where(n * PREP_UNROLL + lane < count, 1.0, 0.0).astype(F32)
            observed = jnp.concatenate([vis_ref[t, 0], vis_ref[t, 1]], axis=1)
            right = (dot(observed, kern[plane_ref[t]]) * alive).astype(BF16)
            held[lane, :, :S] = turn_pair(right)

    def left_products(n):
        for lane in range(PREP_UNROLL):
            t = jnp.minimum(n * PREP_UNROLL + lane, TILE_CAP - 1)
            slot = slot_ref[t]
            both = dot(kern_t[plane_ref[t]], held[lane, :, :S])
            acc[slot] = acc[slot] + jnp.concatenate([both[:S], both[S:]], axis=1)

    def step(n, carry):
        left_products(n - 1)
        right_products(n)
        return carry

    batches = jnp.maximum((count + PREP_UNROLL - 1) // PREP_UNROLL, 1)
    right_products(0)
    lax.fori_loop(1, batches, step, 0)
    left_products(batches - 1)


def degrid_grid(items_ref, base, times, count, gram_ref, grid_ref, acc, held):
    def right_products(n):
        for lane in range(UNROLL):
            code = items_ref[base + n * UNROLL + lane]
            first, second = (code >> 4) & (SPARE - 1), (code >> 10) & (SPARE - 1)
            pair = jnp.concatenate([grid_ref[first], grid_ref[second]], axis=0)
            right = dot(pair, gram_ref[code & (WPLANES - 1)])
            equal = items_ref[times + base + n * UNROLL + lane]
            right = [right[:S] * (equal & 0xFFFF).astype(F32), right[S:] * (equal >> 16).astype(F32)]
            held[lane] = restack(jnp.concatenate(right, axis=0).astype(BF16))

    def left_products(n):
        for lane in range(UNROLL):
            code = items_ref[base + n * UNROLL + lane]
            both = dot(gram_ref[code & (WPLANES - 1)], held[lane])
            for k, slot in enumerate(((code >> 4) & 63, (code >> 10) & 63)):
                cols = slice(k * S, (k + 1) * S)
                acc[slot] = acc[slot] - jnp.concatenate([both[:S, cols], both[S:, cols]], axis=1)

    def step(n, carry):
        left_products(n - 1)
        right_products(n)
        return carry

    batches = jnp.maximum((count + UNROLL - 1) // UNROLL, 1)
    right_products(0)
    lax.fori_loop(1, batches, step, 0)
    left_products(batches - 1)


def both_cycles(
    facets, coef, base, times, count, pos, devices, items_ref, gram_ref, back_ref, half_of, tables, grid, acc, flip, held, keep_ref, send_ref
):
    column_ref, lanes_ref, rows_ref, inv_row_ref, inv_col_ref = tables[:5]
    loads = tables[5]

    def block(ref, facet, pc):
        first = facet * NP + pc * SIDE
        return ref[first : first + SIDE].reshape(P_SIZE, PAIR)

    def column_pass(cycle, facet, pc):
        part = half_of(cycle, facet, pc)
        turned = jnp.concatenate([part[:, S:], -part[:, :S]], axis=1)
        return dot(column_ref[...], jnp.concatenate([part, turned], axis=0))

    def place(ref, facet, pc, value):
        first = facet * NP + pc * SIDE
        ref[first : first + SIDE] = value.reshape(SIDE, S, PAIR)

    loads[1].wait()
    for facet in range(facets):
        for pc in range(SIDE):
            place(grid, facet, pc, column_pass(0, facet, pc).astype(BF16))
    if loads[0] is not None:
        loads[7].wait()
        acc[:NP] = back_ref[...].astype(F32)
        loads[0].wait()
    degrid_grid(items_ref, base, times, count, gram_ref, grid, acc, held)

    for load in loads[2:5]:
        if load is not None:
            load.wait()
    lane = lax.broadcasted_iota(jnp.int32, (1, PAIR), 1)
    row = lax.broadcasted_iota(jnp.int32, (PAIR, 1), 0)
    sign = jnp.where(lane < S, 1.0, -1.0).astype(F32)
    for facet in range(facets):
        for pc in range(SIDE):
            place(flip, facet, pc, block(acc, facet, pc).astype(BF16))
        for pc in range(SIDE):
            turned = dot(block(flip, facet, SIDE - 1 - pc), wide(lanes_ref, 0))
            edge = block(flip, facet, (SIDE - pc) % SIDE).astype(F32) * sign
            mirrored = jnp.where(lane % S == 0, edge, turned)
            mirrored_half = mirrored.astype(BF16)
            fresh = column_pass(1, facet, pc)
            own = block(acc, facet, pc)
            parts = []
            for b in range(2):
                mine = slice(b * PAIR, (b + 1) * PAIR)
                other = slice((1 - b) * PAIR, (2 - b) * PAIR)
                swapped = dot(wide(rows_ref, 0), mirrored_half[other])
                swapped = jnp.where(row == 0, mirrored[mine], swapped)
                parts.append((fresh[mine] + coef * (own[mine] + swapped)).astype(BF16))
            place(grid, facet, pc, jnp.concatenate(parts, axis=0))
    for facet in range(facets):
        for pc in range(SIDE):
            place(acc, facet, pc, block(back_ref, facet, pc).astype(F32))
    degrid_grid(items_ref, base, times, count, gram_ref, grid, acc, held)

    loads[5].wait()
    loads[6].wait()
    share, far = S // devices, devices // 2
    for facet in range(facets):
        mixed = [[] for _ in range(SIDE)]
        for pc in range(SIDE):
            r0, r1, r2, r3 = (acc[facet * NP + pc * SIDE + p] for p in range(SIDE))
            even, odd = r0 + r2, r0 - r2
            even_b, odd_b = r1 + r3, r1 - r3
            turned = jnp.concatenate([-odd_b[:, S:], odd_b[:, :S]], axis=1)
            for q, value in enumerate((even + even_b, odd + turned, even - even_b, odd - turned)):
                mixed[q].append(turn_pair(value.astype(BF16)))
        for q in range(SIDE):
            spec = dot(wide(inv_row_ref, 2 * q), jnp.concatenate(mixed[q], axis=1)).astype(BF16)
            parts = []
            for pc in range(SIDE):
                cols = slice(pc * S, (pc + 1) * S)
                parts += [spec[:S, cols], spec[S:, cols]]
            spec = jnp.concatenate(parts, axis=1)
            image = jnp.concatenate([dot(spec, wide(inv_col_ref, j)) for j in range(0, SIDE, 2)], axis=1)
            if send_ref is None:
                keep_ref[facet, q] = image.astype(BF16)
                continue
            odd, mine = pos & 1, pos >> 1
            for there in range(far):
                zero = image[2 * there * share : (2 * there + 1) * share].astype(BF16)
                one = image[(2 * there + 1) * share : (2 * there + 2) * share].astype(BF16)
                offset = there ^ mine
                keep_ref[offset, facet, q] = jnp.where(odd == 0, zero, one)
                send_ref[offset, facet, q] = jnp.where(odd == 0, one, zero)


def copies(moves, sems, first=0):
    return [pltpu.make_async_copy(src, dst, sems.at[first + k]) for k, (src, dst) in enumerate(moves)]


def first_kernel(facets, times, rows, coef, devices, outs, *refs):
    pos_ref, items_ref, slot_ref, plane_ref, live_ref = refs[:5]
    wk_hbm, vis_hbm, sky_hbm, row_hbm, column_hbm, *table_hbm = refs[5:14]
    gram_hbm, back_hbm, half_hbm, *images = refs[14 : 17 + outs]
    wk_ref, vis_ref, sky_ref, row_ref, column_ref, *table_refs = refs[17 + outs : 26 + outs]
    gram_ref, half_ref, back_ref, kern, kern_t, acc, grid, flip, held, sems = refs[26 + outs :]
    moves = [(wk_hbm, wk_ref), (sky_hbm, sky_ref), (row_hbm, row_ref), (vis_hbm, vis_ref), (column_hbm.at[pos_ref[0]], column_ref)]
    loads = copies(moves + list(zip(table_hbm, table_refs)), sems)
    for load in loads[:4]:
        load.start()
    later = facets * NP
    leave = copies(
        [(gram_ref, gram_hbm), (half_ref, half_hbm), (back_ref.at[pl.ds(later, F * NP - later)], back_hbm)], sems, len(loads)
    )
    prepare(
        slot_ref, plane_ref, live_ref, wk_ref, vis_ref, sky_ref, row_ref, gram_ref, half_ref, kern, kern_t, acc, held, loads, leave
    )
    for slot in range(0, F * NP, NP):
        back_ref[slot : slot + NP] = acc[slot : slot + NP].astype(BF16)
    leave[2].start()

    def half_of(cycle, facet, pc):
        first = (cycle * F + facet) * rows
        return half_ref[first : first + rows, pc * PAIR : (pc + 1) * PAIR]

    tables = (column_ref, *table_refs, [None, loads[4], None, *loads[5:]])
    keep_ref, send_ref = images if outs == 2 else (images[0], None)
    both_cycles(
        facets, coef, 0, times, items_ref[2 * times], pos_ref[0], devices, items_ref, gram_ref, back_ref, half_of, tables, grid, acc, flip, held, keep_ref, send_ref
    )
    for out in leave:
        out.wait()


def later_kernel(facet, offset, base, times, part, rows, coef, devices, outs, *refs):
    pos_ref, items_ref = refs[:2]
    gram_hbm, back_hbm, half_hbm, column_hbm, *table_hbm = refs[2:10]
    images = refs[10 : 10 + outs]
    gram_ref, back_ref, half_ref, column_ref, *table_refs = refs[10 + outs : 18 + outs]
    acc, grid, flip, held, sems = refs[18 + outs :]
    moves = [
        (half_hbm.at[pl.ds(facet * rows, rows)], half_ref.at[0]),
        (column_hbm.at[pos_ref[0]], column_ref),
        (back_hbm.at[pl.ds(offset, NP)], back_ref),
        (gram_hbm, gram_ref),
        (half_hbm.at[pl.ds((F + facet) * rows, rows)], half_ref.at[1]),
    ]
    loads = copies(moves + list(zip(table_hbm, table_refs)), sems)
    for load in loads[:4]:
        load.start()
    for load in loads[4:]:
        load.start()
    loads[0].wait()

    def half_of(cycle, _, pc):
        return half_ref[cycle, :, pc * PAIR : (pc + 1) * PAIR]

    tables = (column_ref, *table_refs, [loads[3], loads[1], *loads[4:], loads[2]])
    keep_ref, send_ref = images if outs == 2 else (images[0], None)
    both_cycles(
        1, coef, base, times, items_ref[2 * times + part], pos_ref[0], devices, items_ref, gram_ref, back_ref, half_of, tables, grid, acc, flip, held, keep_ref, send_ref
    )


def tile_lists(codes, stride):
    total = codes.shape[0]
    ids = jnp.arange(total, dtype=jnp.int32)
    before = ids[None, :] < ids[:, None]
    equal = codes[:, None] == codes[None, :]
    again = jnp.sum((equal & before).astype(jnp.int32), axis=1) > 0
    times = jnp.sum(equal.astype(jnp.int32), axis=1)
    group = jnp.where(again, LISTS * WPLANES, codes >> 6)
    rank = jnp.sum(((group[:, None] == group[None, :]) & before).astype(jnp.int32), axis=1)
    planes = jnp.arange(LISTS * WPLANES, dtype=jnp.int32)
    pairs = (jnp.sum((group[None, :] == planes[:, None]).astype(jnp.int32), axis=1) + 1) >> 1
    which = group >> 4
    earlier = (planes[None, :] < group[:, None]) & ((planes[None, :] >> 4) == which[:, None])
    base = jnp.sum(jnp.where(earlier, pairs[None, :], 0), axis=1)
    where = which * stride + base + (rank >> 1)
    slot, plane = codes & 63, (codes >> 6) & (WPLANES - 1)
    even = (rank & 1) == 0
    delta = jnp.where(even, plane + ((slot - SPARE) << 4), (slot - SPARE) << 10)
    places = jnp.arange(LISTS * stride, dtype=jnp.int32)
    hit = (places[:, None] == where[None, :]) & (which < LISTS)[None, :]
    items = (SPARE << 4) + (SPARE << 10) + jnp.sum(jnp.where(hit, delta[None, :], 0), axis=1)
    times = jnp.sum(jnp.where(hit, jnp.where(even, times, times << 16)[None, :], 0), axis=1)
    counts = jnp.sum(pairs.reshape(LISTS, WPLANES), axis=1)
    return jnp.concatenate([items, times, counts])


def exchange(value, bits, devices):
    return lax.ppermute(value, "vis", [(i, i ^ bits) for i in range(devices)])


def split_image(image, position, devices):
    share, far = S // devices, devices // 2
    parts = image.reshape(-1, SIDE, far, 2, share, P_SIZE).transpose(3, 2, 0, 1, 4, 5)
    parts = jnp.take(parts, jnp.arange(far) ^ (position >> 1), axis=1)
    odd = position & 1
    return lax.dynamic_index_in_dim(parts, odd, 0, False), lax.dynamic_index_in_dim(parts, 1 - odd, 0, False)


def merge_pair(keep, taken):
    return [(keep[k].astype(F32) + taken[k].astype(F32)).astype(BF16) for k in range(1, keep.shape[0])]


def final_kernel(parts, groups, *refs):
    out_ref, mixed = refs[-2:]
    f = 0
    for group in range(groups):
        keep_ref, taken_ref, *others = refs[group * parts : (group + 1) * parts]
        for k in range(keep_ref.shape[1]):
            for q in range(SIDE):
                total = keep_ref[0, k, q].astype(F32) + taken_ref[0, k, q].astype(F32)
                for other in others:
                    total = total + other[k, q].astype(F32)
                for c in range(SIDE):
                    mixed[f, c, pl.ds(q, total.shape[0], stride=SIDE), :] = total[:, c * S : (c + 1) * S]
            for c in range(SIDE):
                out_ref[f, :, c * S : (c + 1) * S] = mixed[f, c]
            f += 1


def local(model_input, w_kernels, visibilities, tile_facet, tile_patch, tile_wplane, tile_count):
    devices = lax.axis_size("vis")
    position = lax.axis_index("vis").astype(jnp.int32)
    rows = P_SIZE // devices
    weight = math.sqrt(F * NP / (TILE_CAP * devices))
    total = TILE_CAP * devices
    stride = total // 2 + WPLANES // 2 + UNROLL
    coef = GAIN * weight / 2

    slots = tile_facet * NP + (tile_patch & 3) * SIDE + (tile_patch >> 2)
    live = jnp.arange(TILE_CAP, dtype=jnp.int32) < tile_count[0]
    which = jnp.maximum(tile_facet - (FIRST - 1), 0)
    near = jnp.where(tile_facet < FIRST, slots, slots & (NP - 1))
    codes = jnp.where(live, (which << 10) + (tile_wplane << 6) + near, LISTS << 10)
    bits = 1
    while bits < devices:
        codes = jnp.concatenate([codes, exchange(codes, bits, devices)])
        bits *= 2
    items = tile_lists(codes, stride)

    lanes, row_flip = flip_tables()
    tables = [column_tables(devices), lanes, row_flip, inverse_row_tables(), inverse_column_table(weight)]
    tables = [jnp.asarray(t) for t in tables]
    here = position.reshape(1)
    smem = pl.BlockSpec(memory_space=pltpu.SMEM)
    vmem = pl.BlockSpec(memory_space=pltpu.VMEM)
    hbm = pl.BlockSpec(memory_space=pl.ANY)
    share, far = S // devices, devices // 2
    split = share % 16 == 0

    def image_shapes(facets):
        if split:
            return [jax.ShapeDtypeStruct((far, facets, SIDE, share, P_SIZE), BF16)] * 2
        return [jax.ShapeDtypeStruct((facets, SIDE, S, P_SIZE), BF16)]

    def halves_of(images):
        return images if split else split_image(images[0], position, devices)

    params = pltpu.CompilerParams(vmem_limit_bytes=VMEM_BYTES)
    outs = 2 if split else 1
    half_shape = (2 * F * rows, 2 * P_SIZE)
    gram_shape = (WPLANES, PAIR, PAIR)
    table_scratch = [pltpu.VMEM((P_SIZE, 2 * rows), BF16)] + [pltpu.VMEM(t.shape, BF16) for t in tables[1:]]

    gram, back, half_rows, *images = pl.pallas_call(
        functools.partial(first_kernel, FIRST, LISTS * stride, rows, coef, devices, outs),
        out_shape=[
            jax.ShapeDtypeStruct(gram_shape, BF16),
            jax.ShapeDtypeStruct(((F - FIRST) * NP, S, PAIR), BF16),
            jax.ShapeDtypeStruct(half_shape, BF16),
            *image_shapes(FIRST),
        ],
        in_specs=[smem] * 5 + [hbm] * 9,
        out_specs=[hbm] * 3 + [vmem] * outs,
        scratch_shapes=[
            pltpu.VMEM(w_kernels.shape, BF16),
            pltpu.VMEM(visibilities.shape, BF16),
            pltpu.VMEM((2 * F * rows, P_SIZE), BF16),
            pltpu.VMEM((2 * SIDE, P_SIZE, S), BF16),
            *table_scratch,
            pltpu.VMEM(gram_shape, BF16),
            pltpu.VMEM(half_shape, BF16),
            pltpu.VMEM((F * NP, S, PAIR), BF16),
            pltpu.VMEM(gram_shape, BF16),
            pltpu.VMEM(gram_shape, BF16),
            pltpu.VMEM((F * NP + 1, S, PAIR), F32),
            pltpu.VMEM((FIRST * NP, S, PAIR), BF16),
            pltpu.VMEM((FIRST * NP, S, PAIR), BF16),
            pltpu.VMEM((max(UNROLL, PREP_UNROLL), PAIR, PAIR), BF16),
            pltpu.SemaphoreType.DMA((12,)),
        ],
        compiler_params=params,
        cost_estimate=pl.CostEstimate(flops=30 * 10**9, bytes_accessed=12 * 2**20, transcendentals=0),
        name="first",
    )(
        here,
        items,
        slots,
        tile_wplane,
        tile_count,
        w_kernels,
        visibilities,
        model_input.reshape(2 * F * rows, P_SIZE),
        jnp.asarray(row_table()),
        *tables,
    )

    keep, send = halves_of(images)
    pairs = [(keep, exchange(send, 1, devices))]
    merged, others = [], []

    def to_each_z(group):
        merged.append(merge_pair(*pairs[group]))
        others.append([exchange(part, 2 * k, devices) for k, part in enumerate(merged[-1], 1)])

    for facet in range(FIRST, F):
        part = facet - FIRST + 1
        if part == 2:
            to_each_z(0)
            here, _ = lax.optimization_barrier((here, merged[0]))
        images = pl.pallas_call(
            functools.partial(
                later_kernel, facet, (facet - FIRST) * NP, part * stride, LISTS * stride, part, rows, coef, devices, outs
            ),
            out_shape=image_shapes(1),
            in_specs=[smem] * 2 + [hbm] * 8,
            out_specs=[vmem] * outs,
            scratch_shapes=[
                pltpu.VMEM(gram_shape, BF16),
                pltpu.VMEM((NP, S, PAIR), BF16),
                pltpu.VMEM((2, rows, 2 * P_SIZE), BF16),
                *table_scratch,
                pltpu.VMEM((SPARE + 1, S, PAIR), F32),
                pltpu.VMEM((NP, S, PAIR), BF16),
                pltpu.VMEM((NP, S, PAIR), BF16),
                pltpu.VMEM((max(UNROLL, PREP_UNROLL), PAIR, PAIR), BF16),
                pltpu.SemaphoreType.DMA((9,)),
            ],
            compiler_params=params,
            cost_estimate=pl.CostEstimate(flops=14 * 10**9, bytes_accessed=6 * 2**20, transcendentals=0),
            name="facet",
        )(here, items, gram, back, half_rows, *tables)
        keep, send = halves_of(images)
        if part == 2:
            send, others[0] = lax.optimization_barrier((send, others[0]))
        pairs.append((keep, exchange(send, 1, devices)))
    for group in range(1, LISTS):
        to_each_z(group)

    def finish(groups, first, facets, before):
        in_specs, operands = [], []
        for group in groups:
            block = (1,) + pairs[group][0].shape[1:]
            in_specs += [pl.BlockSpec(block, lambda i: (0, 0, 0, 0, 0))] * 2 + [vmem] * len(others[group])
            operands += [*pairs[group], *others[group]]
        parts = len(operands) // len(groups)
        aliases = {len(operands): 0} if before else {}
        return pl.pallas_call(
            functools.partial(final_kernel, parts, len(groups)),
            out_shape=jax.ShapeDtypeStruct((F, rows, P_SIZE), F32),
            grid=(1,),
            in_specs=in_specs + [hbm] * len(before),
            out_specs=pl.BlockSpec((facets, rows, P_SIZE), lambda i: (first // facets, 0, 0)),
            scratch_shapes=[pltpu.VMEM((facets, SIDE, rows, S), F32)],
            input_output_aliases=aliases,
            compiler_params=pltpu.CompilerParams(vmem_limit_bytes=FINAL_VMEM),
            cost_estimate=pl.CostEstimate(flops=10**6, bytes_accessed=2**20, transcendentals=0),
            name="final",
        )(*operands, *before)

    done = finish(range(LISTS - 1), 0, F - 1, [])
    return finish([LISTS - 1], F - 1, 1, [done])


def solution(mesh):
    return jax.shard_map(
        local,
        mesh=mesh,
        in_specs=(
            P(None, "freq", "vis", None),
            P("freq", None, None, None),
            P(("freq", "vis"), None, None, None),
            P(("freq", "vis")),
            P(("freq", "vis")),
            P(("freq", "vis")),
            P(("freq", "vis")),
        ),
        out_specs=P("freq", "vis", None),
        check_vma=False,
    )
```

```python
import functools
import math

import jax
import jax.numpy as jnp
import ml_dtypes
import numpy as np
from jax import lax
from jax.experimental import pallas as pl
from jax.experimental.pallas import tpu as pltpu
from jax.sharding import PartitionSpec as P

P_SIZE = 512
S = 128
F = 4
WPLANES = 16
TILE_CAP = 32
NP = 16
SIDE = P_SIZE // S
PAIR = 2 * S
UNROLL = 6
PREP_UNROLL = 8
FIRST = 2
LISTS = F - FIRST + 1
SPARE = FIRST * NP
GAIN = 0.5
VMEM_BYTES = 60 * 1024 * 1024
FINAL_VMEM = 6 * 1024 * 1024

BF16 = jnp.bfloat16
F32 = jnp.float32


def angle_tables():
    index = np.arange(P_SIZE)
    angles = (index[:, None] * index[None, :] % P_SIZE) * (2.0 * np.pi / P_SIZE)
    return np.cos(angles) / np.sqrt(P_SIZE), np.sin(angles) / np.sqrt(P_SIZE)


def half(array):
    return np.asarray(array, np.float32).astype(ml_dtypes.bfloat16)


def complex_block(real, imag):
    return np.block([[real, -imag], [imag, real]])


def by_columns(table):
    rows, columns = table.shape
    return table.reshape(rows, columns // S, S).transpose(1, 0, 2)


def wide(ref, chunk):
    return jnp.concatenate([ref[chunk], ref[chunk + 1]], axis=1)


def row_table():
    cosine, sine = angle_tables()
    parts = [cosine.reshape(P_SIZE, SIDE, 1, S), -sine.reshape(P_SIZE, SIDE, 1, S)]
    return half(by_columns(np.concatenate(parts, axis=2).reshape(P_SIZE, 2 * P_SIZE)))


def column_tables(devices):
    cosine, sine = angle_tables()
    rows = P_SIZE // devices
    parts = [t.reshape(P_SIZE, devices, rows).transpose(1, 0, 2) for t in (cosine, sine)]
    return half(np.concatenate(parts, axis=2))


def flip_tables():
    small = np.zeros((S, S))
    for k in range(1, S):
        small[S - k, k] = 1.0
    zero = np.zeros((S, S))
    lanes = np.block([[small, zero], [zero, -small]])
    rows = np.zeros((PAIR, PAIR))
    for i in range(1, PAIR):
        rows[i, PAIR - i] = 1.0
    return half(by_columns(lanes)), half(by_columns(rows))


def inverse_row_tables():
    a, i = np.arange(S)[:, None], np.arange(S)[None, :]
    blocks = []
    for q in range(SIDE):
        angles = ((SIDE * a + q) * i % P_SIZE) * (2.0 * np.pi / P_SIZE)
        blocks.append(by_columns(complex_block(np.cos(angles), np.sin(angles)) / np.sqrt(P_SIZE)))
    return half(np.concatenate(blocks))


def inverse_column_table(weight):
    cosine, sine = angle_tables()
    parts = [cosine.reshape(SIDE, 1, S, P_SIZE), -sine.reshape(SIDE, 1, S, P_SIZE)]
    return half(by_columns(np.concatenate(parts, axis=1).reshape(2 * P_SIZE, P_SIZE) * weight))


def dot(a, b):
    return jnp.dot(a, b, preferred_element_type=F32)


def restack(pair):
    top = jnp.concatenate([pair[:S, :S], pair[S:, :S]], axis=1)
    bottom = jnp.concatenate([pair[:S, S:], pair[S:, S:]], axis=1)
    return jnp.concatenate([top, bottom], axis=0)


def turn_pair(pair):
    return jnp.concatenate([pair[:, :S], pair[:, S:]], axis=0)


def prepare(slot_ref, plane_ref, count_ref, wk_ref, vis_ref, sky_ref, row_ref, gram_ref, half_ref, kern, kern_t, acc, held, loads, leave):
    acc[...] = jnp.zeros_like(acc)
    loads[0].wait()
    for load in loads[4:]:
        load.start()
    for w in range(WPLANES):
        real, imag = wk_ref[w, 0], wk_ref[w, 1]
        block = jnp.concatenate(
            [jnp.concatenate([real, -imag], axis=1), jnp.concatenate([imag, real], axis=1)], axis=0
        )
        real_t, imag_t = real.T, imag.T
        block_t = jnp.concatenate(
            [jnp.concatenate([real_t, imag_t], axis=1), jnp.concatenate([-imag_t, real_t], axis=1)], axis=0
        )
        kern[w] = block
        kern_t[w] = block_t
        gram_ref[w] = dot(block_t, block).astype(BF16)
    leave[0].start()

    loads[1].wait()
    loads[2].wait()
    for pc in range(SIDE):
        half_ref[:, pc * PAIR : (pc + 1) * PAIR] = dot(sky_ref[...], wide(row_ref, 2 * pc)).astype(BF16)
    leave[1].start()

    loads[3].wait()
    count = count_ref[0]

    def right_product(n, lane):
        t = jnp.minimum(n * PREP_UNROLL + lane, TILE_CAP - 1)
        alive = jnp.where(n * PREP_UNROLL + lane < count, 1.0, 0.0).astype(F32)
        observed = jnp.concatenate([vis_ref[t, 0], vis_ref[t, 1]], axis=1)
        right = (dot(observed, kern[plane_ref[t]]) * alive).astype(BF16)
        held[lane, :, :S] = turn_pair(right)

    def left_product(n, lane):
        t = jnp.minimum(n * PREP_UNROLL + lane, TILE_CAP - 1)
        slot = slot_ref[t]
        both = dot(kern_t[plane_ref[t]], held[lane, :, :S])
        acc[slot] = acc[slot] + jnp.concatenate([both[:S], both[S:]], axis=1)

    def step(n, carry):
        for lane in range(PREP_UNROLL):
            left_product(n - 1, lane)
            right_product(n, lane)
        return carry

    batches = jnp.maximum((count + PREP_UNROLL - 1) // PREP_UNROLL, 1)
    for lane in range(PREP_UNROLL):
        right_product(0, lane)
    lax.fori_loop(1, batches, step, 0)
    for lane in range(PREP_UNROLL):
        left_product(batches - 1, lane)


def degrid_grid(items_ref, base, times, count, gram_ref, grid_ref, acc, held):
    def right_product(n, lane):
        code = items_ref[base + n * UNROLL + lane]
        first, second = (code >> 4) & (SPARE - 1), (code >> 10) & (SPARE - 1)
        pair = jnp.concatenate([grid_ref[first], grid_ref[second]], axis=0)
        right = dot(pair, gram_ref[code & (WPLANES - 1)])
        equal = items_ref[times + base + n * UNROLL + lane]
        right = [right[:S] * (equal & 0xFFFF).astype(F32), right[S:] * (equal >> 16).astype(F32)]
        held[lane] = restack(jnp.concatenate(right, axis=0).astype(BF16))

    def left_product(n, lane):
        code = items_ref[base + n * UNROLL + lane]
        both = dot(gram_ref[code & (WPLANES - 1)], held[lane])
        for k, slot in enumerate(((code >> 4) & 63, (code >> 10) & 63)):
            cols = slice(k * S, (k + 1) * S)
            acc[slot] = acc[slot] - jnp.concatenate([both[:S, cols], both[S:, cols]], axis=1)

    def step(n, carry):
        for lane in range(UNROLL):
            left_product(n - 1, lane)
            right_product(n, lane)
        return carry

    batches = jnp.maximum((count + UNROLL - 1) // UNROLL, 1)
    for lane in range(UNROLL):
        right_product(0, lane)
    lax.fori_loop(1, batches, step, 0)
    for lane in range(UNROLL):
        left_product(batches - 1, lane)


def both_cycles(
    facets, coef, base, times, count, pos, devices, items_ref, gram_ref, back_ref, half_of, tables, grid, acc, flip, held, keep_ref, send_ref
):
    column_ref, lanes_ref, rows_ref, inv_row_ref, inv_col_ref = tables[:5]
    loads = tables[5]

    def block(ref, facet, pc):
        first = facet * NP + pc * SIDE
        return ref[first : first + SIDE].reshape(P_SIZE, PAIR)

    def column_pass(cycle, facet, pc):
        part = half_of(cycle, facet, pc)
        turned = jnp.concatenate([part[:, S:], -part[:, :S]], axis=1)
        return dot(column_ref[...], jnp.concatenate([part, turned], axis=0))

    def place(ref, facet, pc, value):
        first = facet * NP + pc * SIDE
        ref[first : first + SIDE] = value.reshape(SIDE, S, PAIR)

    loads[1].wait()
    for facet in range(facets):
        for pc in range(SIDE):
            place(grid, facet, pc, column_pass(0, facet, pc).astype(BF16))
    if loads[0] is not None:
        loads[7].wait()
        acc[:NP] = back_ref[...].astype(F32)
        loads[0].wait()
    degrid_grid(items_ref, base, times, count, gram_ref, grid, acc, held)

    for load in loads[2:5]:
        if load is not None:
            load.wait()
    lane = lax.broadcasted_iota(jnp.int32, (1, PAIR), 1)
    row = lax.broadcasted_iota(jnp.int32, (PAIR, 1), 0)
    sign = jnp.where(lane < S, 1.0, -1.0).astype(F32)
    for facet in range(facets):
        for pc in range(SIDE):
            place(flip, facet, pc, block(acc, facet, pc).astype(BF16))
        for pc in range(SIDE):
            turned = dot(block(flip, facet, SIDE - 1 - pc), wide(lanes_ref, 0))
            edge = block(flip, facet, (SIDE - pc) % SIDE).astype(F32) * sign
            mirrored = jnp.where(lane % S == 0, edge, turned)
            mirrored_half = mirrored.astype(BF16)
            fresh = column_pass(1, facet, pc)
            own = block(acc, facet, pc)
            parts = []
            for b in range(2):
                mine = slice(b * PAIR, (b + 1) * PAIR)
                other = slice((1 - b) * PAIR, (2 - b) * PAIR)
                swapped = dot(wide(rows_ref, 0), mirrored_half[other])
                swapped = jnp.where(row == 0, mirrored[mine], swapped)
                parts.append((fresh[mine] + coef * (own[mine] + swapped)).astype(BF16))
            place(grid, facet, pc, jnp.concatenate(parts, axis=0))
    for facet in range(facets):
        for pc in range(SIDE):
            place(acc, facet, pc, block(back_ref, facet, pc).astype(F32))
    degrid_grid(items_ref, base, times, count, gram_ref, grid, acc, held)

    loads[5].wait()
    loads[6].wait()
    share, far = S // devices, devices // 2
    for facet in range(facets):
        mixed = [[] for _ in range(SIDE)]
        for pc in range(SIDE):
            r0, r1, r2, r3 = (acc[facet * NP + pc * SIDE + p] for p in range(SIDE))
            even, odd = r0 + r2, r0 - r2
            even_b, odd_b = r1 + r3, r1 - r3
            turned = jnp.concatenate([-odd_b[:, S:], odd_b[:, :S]], axis=1)
            for q, value in enumerate((even + even_b, odd + turned, even - even_b, odd - turned)):
                mixed[q].append(turn_pair(value.astype(BF16)))
        for q in range(SIDE):
            spec = dot(wide(inv_row_ref, 2 * q), jnp.concatenate(mixed[q], axis=1)).astype(BF16)
            parts = []
            for pc in range(SIDE):
                cols = slice(pc * S, (pc + 1) * S)
                parts += [spec[:S, cols], spec[S:, cols]]
            spec = jnp.concatenate(parts, axis=1)
            image = jnp.concatenate([dot(spec, wide(inv_col_ref, j)) for j in range(0, SIDE, 2)], axis=1)
            if send_ref is None:
                keep_ref[facet, q] = image.astype(BF16)
                continue
            odd, mine = pos & 1, pos >> 1
            for there in range(far):
                zero = image[2 * there * share : (2 * there + 1) * share].astype(BF16)
                one = image[(2 * there + 1) * share : (2 * there + 2) * share].astype(BF16)
                offset = there ^ mine
                keep_ref[offset, facet, q] = jnp.where(odd == 0, zero, one)
                send_ref[offset, facet, q] = jnp.where(odd == 0, one, zero)


def copies(moves, sems, first=0):
    return [pltpu.make_async_copy(src, dst, sems.at[first + k]) for k, (src, dst) in enumerate(moves)]


def first_kernel(facets, times, rows, coef, devices, outs, *refs):
    pos_ref, items_ref, slot_ref, plane_ref, live_ref = refs[:5]
    wk_hbm, vis_hbm, sky_hbm, row_hbm, column_hbm, *table_hbm = refs[5:14]
    gram_hbm, back_hbm, half_hbm, *images = refs[14 : 17 + outs]
    wk_ref, vis_ref, sky_ref, row_ref, column_ref, *table_refs = refs[17 + outs : 26 + outs]
    gram_ref, half_ref, back_ref, kern, kern_t, acc, grid, flip, held, sems = refs[26 + outs :]
    moves = [(wk_hbm, wk_ref), (sky_hbm, sky_ref), (row_hbm, row_ref), (vis_hbm, vis_ref), (column_hbm.at[pos_ref[0]], column_ref)]
    loads = copies(moves + list(zip(table_hbm, table_refs)), sems)
    for load in loads[:4]:
        load.start()
    later = facets * NP
    leave = copies(
        [(gram_ref, gram_hbm), (half_ref, half_hbm), (back_ref.at[pl.ds(later, F * NP - later)], back_hbm)], sems, len(loads)
    )
    prepare(
        slot_ref, plane_ref, live_ref, wk_ref, vis_ref, sky_ref, row_ref, gram_ref, half_ref, kern, kern_t, acc, held, loads, leave
    )
    for slot in range(0, F * NP, NP):
        back_ref[slot : slot + NP] = acc[slot : slot + NP].astype(BF16)
    leave[2].start()

    def half_of(cycle, facet, pc):
        first = (cycle * F + facet) * rows
        return half_ref[first : first + rows, pc * PAIR : (pc + 1) * PAIR]

    tables = (column_ref, *table_refs, [None, loads[4], None, *loads[5:]])
    keep_ref, send_ref = images if outs == 2 else (images[0], None)
    both_cycles(
        facets, coef, 0, times, items_ref[2 * times], pos_ref[0], devices, items_ref, gram_ref, back_ref, half_of, tables, grid, acc, flip, held, keep_ref, send_ref
    )
    for out in leave:
        out.wait()


def later_kernel(facet, offset, base, times, part, rows, coef, devices, outs, *refs):
    pos_ref, items_ref = refs[:2]
    gram_hbm, back_hbm, half_hbm, column_hbm, *table_hbm = refs[2:10]
    images = refs[10 : 10 + outs]
    gram_ref, back_ref, half_ref, column_ref, *table_refs = refs[10 + outs : 18 + outs]
    acc, grid, flip, held, sems = refs[18 + outs :]
    moves = [
        (half_hbm.at[pl.ds(facet * rows, rows)], half_ref.at[0]),
        (column_hbm.at[pos_ref[0]], column_ref),
        (back_hbm.at[pl.ds(offset, NP)], back_ref),
        (gram_hbm, gram_ref),
        (half_hbm.at[pl.ds((F + facet) * rows, rows)], half_ref.at[1]),
    ]
    loads = copies(moves + list(zip(table_hbm, table_refs)), sems)
    for load in loads[:4]:
        load.start()
    for load in loads[4:]:
        load.start()
    loads[0].wait()

    def half_of(cycle, _, pc):
        return half_ref[cycle, :, pc * PAIR : (pc + 1) * PAIR]

    tables = (column_ref, *table_refs, [loads[3], loads[1], *loads[4:], loads[2]])
    keep_ref, send_ref = images if outs == 2 else (images[0], None)
    both_cycles(
        1, coef, base, times, items_ref[2 * times + part], pos_ref[0], devices, items_ref, gram_ref, back_ref, half_of, tables, grid, acc, flip, held, keep_ref, send_ref
    )


def tile_lists(codes, stride):
    total = codes.shape[0]
    ids = jnp.arange(total, dtype=jnp.int32)
    before = ids[None, :] < ids[:, None]
    equal = codes[:, None] == codes[None, :]
    again = jnp.sum((equal & before).astype(jnp.int32), axis=1) > 0
    times = jnp.sum(equal.astype(jnp.int32), axis=1)
    group = jnp.where(again, LISTS * WPLANES, codes >> 6)
    rank = jnp.sum(((group[:, None] == group[None, :]) & before).astype(jnp.int32), axis=1)
    planes = jnp.arange(LISTS * WPLANES, dtype=jnp.int32)
    pairs = (jnp.sum((group[None, :] == planes[:, None]).astype(jnp.int32), axis=1) + 1) >> 1
    which = group >> 4
    earlier = (planes[None, :] < group[:, None]) & ((planes[None, :] >> 4) == which[:, None])
    base = jnp.sum(jnp.where(earlier, pairs[None, :], 0), axis=1)
    where = which * stride + base + (rank >> 1)
    slot, plane = codes & 63, (codes >> 6) & (WPLANES - 1)
    even = (rank & 1) == 0
    delta = jnp.where(even, plane + ((slot - SPARE) << 4), (slot - SPARE) << 10)
    places = jnp.arange(LISTS * stride, dtype=jnp.int32)
    hit = (places[:, None] == where[None, :]) & (which < LISTS)[None, :]
    items = (SPARE << 4) + (SPARE << 10) + jnp.sum(jnp.where(hit, delta[None, :], 0), axis=1)
    times = jnp.sum(jnp.where(hit, jnp.where(even, times, times << 16)[None, :], 0), axis=1)
    counts = jnp.sum(pairs.reshape(LISTS, WPLANES), axis=1)
    return jnp.concatenate([items, times, counts])


def exchange(value, bits, devices):
    return lax.ppermute(value, "vis", [(i, i ^ bits) for i in range(devices)])


def split_image(image, position, devices):
    share, far = S // devices, devices // 2
    parts = image.reshape(-1, SIDE, far, 2, share, P_SIZE).transpose(3, 2, 0, 1, 4, 5)
    parts = jnp.take(parts, jnp.arange(far) ^ (position >> 1), axis=1)
    odd = position & 1
    return lax.dynamic_index_in_dim(parts, odd, 0, False), lax.dynamic_index_in_dim(parts, 1 - odd, 0, False)


def merge_pair(keep, taken):
    return [(keep[k].astype(F32) + taken[k].astype(F32)).astype(BF16) for k in range(1, keep.shape[0])]


def final_kernel(parts, groups, *refs):
    out_ref, mixed = refs[-2:]
    f = 0
    for group in range(groups):
        keep_ref, taken_ref, *others = refs[group * parts : (group + 1) * parts]
        for k in range(keep_ref.shape[1]):
            for q in range(SIDE):
                total = keep_ref[0, k, q].astype(F32) + taken_ref[0, k, q].astype(F32)
                for other in others:
                    total = total + other[k, q].astype(F32)
                for c in range(SIDE):
                    mixed[f, c, pl.ds(q, total.shape[0], stride=SIDE), :] = total[:, c * S : (c + 1) * S]
            for c in range(SIDE):
                out_ref[f, :, c * S : (c + 1) * S] = mixed[f, c]
            f += 1


def local(model_input, w_kernels, visibilities, tile_facet, tile_patch, tile_wplane, tile_count):
    devices = lax.axis_size("vis")
    position = lax.axis_index("vis").astype(jnp.int32)
    rows = P_SIZE // devices
    weight = math.sqrt(F * NP / (TILE_CAP * devices))
    total = TILE_CAP * devices
    stride = total // 2 + WPLANES // 2 + UNROLL
    coef = GAIN * weight / 2

    slots = tile_facet * NP + (tile_patch & 3) * SIDE + (tile_patch >> 2)
    live = jnp.arange(TILE_CAP, dtype=jnp.int32) < tile_count[0]
    which = jnp.maximum(tile_facet - (FIRST - 1), 0)
    near = jnp.where(tile_facet < FIRST, slots, slots & (NP - 1))
    codes = jnp.where(live, (which << 10) + (tile_wplane << 6) + near, LISTS << 10)
    bits = 1
    while bits < devices:
        codes = jnp.concatenate([codes, exchange(codes, bits, devices)])
        bits *= 2
    items = tile_lists(codes, stride)

    lanes, row_flip = flip_tables()
    tables = [column_tables(devices), lanes, row_flip, inverse_row_tables(), inverse_column_table(weight)]
    tables = [jnp.asarray(t) for t in tables]
    here = position.reshape(1)
    smem = pl.BlockSpec(memory_space=pltpu.SMEM)
    vmem = pl.BlockSpec(memory_space=pltpu.VMEM)
    hbm = pl.BlockSpec(memory_space=pl.ANY)
    share, far = S // devices, devices // 2
    split = share % 16 == 0

    def image_shapes(facets):
        if split:
            return [jax.ShapeDtypeStruct((far, facets, SIDE, share, P_SIZE), BF16)] * 2
        return [jax.ShapeDtypeStruct((facets, SIDE, S, P_SIZE), BF16)]

    def halves_of(images):
        return images if split else split_image(images[0], position, devices)

    params = pltpu.CompilerParams(vmem_limit_bytes=VMEM_BYTES)
    outs = 2 if split else 1
    half_shape = (2 * F * rows, 2 * P_SIZE)
    gram_shape = (WPLANES, PAIR, PAIR)
    table_scratch = [pltpu.VMEM((P_SIZE, 2 * rows), BF16)] + [pltpu.VMEM(t.shape, BF16) for t in tables[1:]]

    gram, back, half_rows, *images = pl.pallas_call(
        functools.partial(first_kernel, FIRST, LISTS * stride, rows, coef, devices, outs),
        out_shape=[
            jax.ShapeDtypeStruct(gram_shape, BF16),
            jax.ShapeDtypeStruct(((F - FIRST) * NP, S, PAIR), BF16),
            jax.ShapeDtypeStruct(half_shape, BF16),
            *image_shapes(FIRST),
        ],
        in_specs=[smem] * 5 + [hbm] * 9,
        out_specs=[hbm] * 3 + [vmem] * outs,
        scratch_shapes=[
            pltpu.VMEM(w_kernels.shape, BF16),
            pltpu.VMEM(visibilities.shape, BF16),
            pltpu.VMEM((2 * F * rows, P_SIZE), BF16),
            pltpu.VMEM((2 * SIDE, P_SIZE, S), BF16),
            *table_scratch,
            pltpu.VMEM(gram_shape, BF16),
            pltpu.VMEM(half_shape, BF16),
            pltpu.VMEM((F * NP, S, PAIR), BF16),
            pltpu.VMEM(gram_shape, BF16),
            pltpu.VMEM(gram_shape, BF16),
            pltpu.VMEM((F * NP + 1, S, PAIR), F32),
            pltpu.VMEM((FIRST * NP, S, PAIR), BF16),
            pltpu.VMEM((FIRST * NP, S, PAIR), BF16),
            pltpu.VMEM((max(UNROLL, PREP_UNROLL), PAIR, PAIR), BF16),
            pltpu.SemaphoreType.DMA((12,)),
        ],
        compiler_params=params,
        cost_estimate=pl.CostEstimate(flops=30 * 10**9, bytes_accessed=12 * 2**20, transcendentals=0),
        name="first",
    )(
        here,
        items,
        slots,
        tile_wplane,
        tile_count,
        w_kernels,
        visibilities,
        model_input.reshape(2 * F * rows, P_SIZE),
        jnp.asarray(row_table()),
        *tables,
    )

    keep, send = halves_of(images)
    pairs = [(keep, exchange(send, 1, devices))]
    merged, others = [], []

    def to_each_z(group):
        merged.append(merge_pair(*pairs[group]))
        others.append([exchange(part, 2 * k, devices) for k, part in enumerate(merged[-1], 1)])

    for facet in range(FIRST, F):
        part = facet - FIRST + 1
        if part == 2:
            to_each_z(0)
            here, _ = lax.optimization_barrier((here, merged[0]))
        images = pl.pallas_call(
            functools.partial(
                later_kernel, facet, (facet - FIRST) * NP, part * stride, LISTS * stride, part, rows, coef, devices, outs
            ),
            out_shape=image_shapes(1),
            in_specs=[smem] * 2 + [hbm] * 8,
            out_specs=[vmem] * outs,
            scratch_shapes=[
                pltpu.VMEM(gram_shape, BF16),
                pltpu.VMEM((NP, S, PAIR), BF16),
                pltpu.VMEM((2, rows, 2 * P_SIZE), BF16),
                *table_scratch,
                pltpu.VMEM((SPARE + 1, S, PAIR), F32),
                pltpu.VMEM((NP, S, PAIR), BF16),
                pltpu.VMEM((NP, S, PAIR), BF16),
                pltpu.VMEM((max(UNROLL, PREP_UNROLL), PAIR, PAIR), BF16),
                pltpu.SemaphoreType.DMA((9,)),
            ],
            compiler_params=params,
            cost_estimate=pl.CostEstimate(flops=14 * 10**9, bytes_accessed=6 * 2**20, transcendentals=0),
            name="facet",
        )(here, items, gram, back, half_rows, *tables)
        keep, send = halves_of(images)
        if part == 2:
            send, others[0] = lax.optimization_barrier((send, others[0]))
        pairs.append((keep, exchange(send, 1, devices)))
    for group in range(1, LISTS):
        to_each_z(group)

    def finish(groups, first, facets, before):
        in_specs, operands = [], []
        for group in groups:
            block = (1,) + pairs[group][0].shape[1:]
            in_specs += [pl.BlockSpec(block, lambda i: (0, 0, 0, 0, 0))] * 2 + [vmem] * len(others[group])
            operands += [*pairs[group], *others[group]]
        parts = len(operands) // len(groups)
        aliases = {len(operands): 0} if before else {}
        return pl.pallas_call(
            functools.partial(final_kernel, parts, len(groups)),
            out_shape=jax.ShapeDtypeStruct((F, rows, P_SIZE), F32),
            grid=(1,),
            in_specs=in_specs + [hbm] * len(before),
            out_specs=pl.BlockSpec((facets, rows, P_SIZE), lambda i: (first // facets, 0, 0)),
            scratch_shapes=[pltpu.VMEM((facets, SIDE, rows, S), F32)],
            input_output_aliases=aliases,
            compiler_params=pltpu.CompilerParams(vmem_limit_bytes=FINAL_VMEM),
            cost_estimate=pl.CostEstimate(flops=10**6, bytes_accessed=2**20, transcendentals=0),
            name="final",
        )(*operands, *before)

    done = finish(range(LISTS - 1), 0, F - 1, [])
    return finish([LISTS - 1], F - 1, 1, [done])


def solution(mesh):
    return jax.shard_map(
        local,
        mesh=mesh,
        in_specs=(
            P(None, "freq", "vis", None),
            P("freq", None, None, None),
            P(("freq", "vis"), None, None, None),
            P(("freq", "vis")),
            P(("freq", "vis")),
            P(("freq", "vis")),
            P(("freq", "vis")),
        ),
        out_specs=P("freq", "vis", None),
        check_vma=False,
    )
```

```python
import functools
import math

import jax
import jax.numpy as jnp
import ml_dtypes
import numpy as np
from jax import lax
from jax.experimental import pallas as pl
from jax.experimental.pallas import tpu as pltpu
from jax.sharding import PartitionSpec as P

P_SIZE = 512
S = 128
F = 4
WPLANES = 16
TILE_CAP = 32
NP = 16
SIDE = P_SIZE // S
PAIR = 2 * S
UNROLL = 6
PREP_UNROLL = 8
FIRST = 2
LISTS = F - FIRST + 1
SPARE = FIRST * NP
GAIN = 0.5
VMEM_BYTES = 60 * 1024 * 1024
LATER_VMEM = 52 * 1024 * 1024
FINAL_VMEM = 6 * 1024 * 1024

BF16 = jnp.bfloat16
F32 = jnp.float32


def angle_tables():
    index = np.arange(P_SIZE)
    angles = (index[:, None] * index[None, :] % P_SIZE) * (2.0 * np.pi / P_SIZE)
    return np.cos(angles) / np.sqrt(P_SIZE), np.sin(angles) / np.sqrt(P_SIZE)


def half(array):
    return np.asarray(array, np.float32).astype(ml_dtypes.bfloat16)


def complex_block(real, imag):
    return np.block([[real, -imag], [imag, real]])


def by_columns(table):
    rows, columns = table.shape
    return table.reshape(rows, columns // S, S).transpose(1, 0, 2)


def wide(ref, chunk):
    return jnp.concatenate([ref[chunk], ref[chunk + 1]], axis=1)


def row_table():
    cosine, sine = angle_tables()
    parts = [cosine.reshape(P_SIZE, SIDE, 1, S), -sine.reshape(P_SIZE, SIDE, 1, S)]
    return half(by_columns(np.concatenate(parts, axis=2).reshape(P_SIZE, 2 * P_SIZE)))


def column_tables(devices):
    cosine, sine = angle_tables()
    rows = P_SIZE // devices
    parts = [t.reshape(P_SIZE, devices, rows).transpose(1, 0, 2) for t in (cosine, sine)]
    return half(np.concatenate(parts, axis=2))


def flip_tables():
    small = np.zeros((S, S))
    for k in range(1, S):
        small[S - k, k] = 1.0
    zero = np.zeros((S, S))
    lanes = np.block([[small, zero], [zero, -small]])
    rows = np.zeros((PAIR, PAIR))
    for i in range(1, PAIR):
        rows[i, PAIR - i] = 1.0
    return half(by_columns(lanes)), half(by_columns(rows))


def inverse_row_tables():
    a, i = np.arange(S)[:, None], np.arange(S)[None, :]
    blocks = []
    for q in range(SIDE):
        angles = ((SIDE * a + q) * i % P_SIZE) * (2.0 * np.pi / P_SIZE)
        blocks.append(by_columns(complex_block(np.cos(angles), np.sin(angles)) / np.sqrt(P_SIZE)))
    return half(np.concatenate(blocks))


def inverse_column_table(weight):
    cosine, sine = angle_tables()
    parts = [cosine.reshape(SIDE, 1, S, P_SIZE), -sine.reshape(SIDE, 1, S, P_SIZE)]
    return half(by_columns(np.concatenate(parts, axis=1).reshape(2 * P_SIZE, P_SIZE) * weight))


def dot(a, b):
    return jnp.dot(a, b, preferred_element_type=F32)


def restack(pair):
    top = jnp.concatenate([pair[:S, :S], pair[S:, :S]], axis=1)
    bottom = jnp.concatenate([pair[:S, S:], pair[S:, S:]], axis=1)
    return jnp.concatenate([top, bottom], axis=0)


def turn_pair(pair):
    return jnp.concatenate([pair[:, :S], pair[:, S:]], axis=0)


def prepare(slot_ref, plane_ref, count_ref, wk_ref, vis_ref, sky_ref, row_ref, gram_ref, half_ref, kern, kern_t, acc, held, loads, leave):
    acc[...] = jnp.zeros_like(acc)
    loads[0].wait()
    for load in loads[4:]:
        load.start()
    for w in range(WPLANES):
        real, imag = wk_ref[w, 0], wk_ref[w, 1]
        block = jnp.concatenate(
            [jnp.concatenate([real, -imag], axis=1), jnp.concatenate([imag, real], axis=1)], axis=0
        )
        real_t, imag_t = real.T, imag.T
        block_t = jnp.concatenate(
            [jnp.concatenate([real_t, imag_t], axis=1), jnp.concatenate([-imag_t, real_t], axis=1)], axis=0
        )
        kern[w] = block
        kern_t[w] = block_t
        gram_ref[w] = dot(block_t, block).astype(BF16)
    leave[0].start()

    loads[1].wait()
    loads[2].wait()
    for pc in range(SIDE):
        half_ref[:, pc * PAIR : (pc + 1) * PAIR] = dot(sky_ref[...], wide(row_ref, 2 * pc)).astype(BF16)
    leave[1].start()

    loads[3].wait()
    count = count_ref[0]

    def right_product(n, lane):
        t = jnp.minimum(n * PREP_UNROLL + lane, TILE_CAP - 1)
        alive = jnp.where(n * PREP_UNROLL + lane < count, 1.0, 0.0).astype(F32)
        observed = jnp.concatenate([vis_ref[t, 0], vis_ref[t, 1]], axis=1)
        right = (dot(observed, kern[plane_ref[t]]) * alive).astype(BF16)
        held[lane, :, :S] = turn_pair(right)

    def left_product(n, lane):
        t = jnp.minimum(n * PREP_UNROLL + lane, TILE_CAP - 1)
        slot = slot_ref[t]
        both = dot(kern_t[plane_ref[t]], held[lane, :, :S])
        acc[slot] = acc[slot] + jnp.concatenate([both[:S], both[S:]], axis=1)

    def step(n, carry):
        for lane in range(PREP_UNROLL):
            left_product(n - 1, lane)
            right_product(n, lane)
        return carry

    batches = jnp.maximum((count + PREP_UNROLL - 1) // PREP_UNROLL, 1)
    for lane in range(PREP_UNROLL):
        right_product(0, lane)
    lax.fori_loop(1, batches, step, 0)
    for lane in range(PREP_UNROLL):
        left_product(batches - 1, lane)


def degrid_grid(items_ref, base, times, count, gram_ref, grid_ref, acc, held):
    def right_product(n, lane):
        code = items_ref[base + n * UNROLL + lane]
        first, second = (code >> 4) & (SPARE - 1), (code >> 10) & (SPARE - 1)
        pair = jnp.concatenate([grid_ref[first], grid_ref[second]], axis=0)
        right = dot(pair, gram_ref[code & (WPLANES - 1)])
        equal = items_ref[times + base + n * UNROLL + lane]
        right = [right[:S] * (equal & 0xFFFF).astype(F32), right[S:] * (equal >> 16).astype(F32)]
        held[lane] = restack(jnp.concatenate(right, axis=0).astype(BF16))

    def left_product(n, lane):
        code = items_ref[base + n * UNROLL + lane]
        both = dot(gram_ref[code & (WPLANES - 1)], held[lane])
        for k, slot in enumerate(((code >> 4) & 63, (code >> 10) & 63)):
            cols = slice(k * S, (k + 1) * S)
            acc[slot] = acc[slot] - jnp.concatenate([both[:S, cols], both[S:, cols]], axis=1)

    def step(n, carry):
        for lane in range(UNROLL):
            left_product(n - 1, lane)
            right_product(n, lane)
        return carry

    batches = jnp.maximum((count + UNROLL - 1) // UNROLL, 1)
    for lane in range(UNROLL):
        right_product(0, lane)
    lax.fori_loop(1, batches, step, 0)
    for lane in range(UNROLL):
        left_product(batches - 1, lane)


def both_cycles(
    facets, coef, base, times, count, pos, devices, items_ref, gram_ref, back_ref, half_of, tables, grid, acc, flip, held, keep_ref, send_ref
):
    column_ref, lanes_ref, rows_ref, inv_row_ref, inv_col_ref = tables[:5]
    loads = tables[5]

    def block(ref, facet, pc):
        first = facet * NP + pc * SIDE
        return ref[first : first + SIDE].reshape(P_SIZE, PAIR)

    def column_pass(cycle, facet, pc):
        part = half_of(cycle, facet, pc)
        turned = jnp.concatenate([part[:, S:], -part[:, :S]], axis=1)
        return dot(column_ref[...], jnp.concatenate([part, turned], axis=0))

    def place(ref, facet, pc, value):
        first = facet * NP + pc * SIDE
        ref[first : first + SIDE] = value.reshape(SIDE, S, PAIR)

    loads[1].wait()
    for facet in range(facets):
        for pc in range(SIDE):
            place(grid, facet, pc, column_pass(0, facet, pc).astype(BF16))
    if loads[0] is not None:
        loads[7].wait()
        acc[:NP] = back_ref[...].astype(F32)
        loads[0].wait()
    degrid_grid(items_ref, base, times, count, gram_ref, grid, acc, held)

    for load in loads[2:5]:
        if load is not None:
            load.wait()
    lane = lax.broadcasted_iota(jnp.int32, (1, PAIR), 1)
    row = lax.broadcasted_iota(jnp.int32, (PAIR, 1), 0)
    sign = jnp.where(lane < S, 1.0, -1.0).astype(F32)
    for facet in range(facets):
        for pc in range(SIDE):
            place(flip, facet, pc, block(acc, facet, pc).astype(BF16))
        for pc in range(SIDE):
            turned = dot(block(flip, facet, SIDE - 1 - pc), wide(lanes_ref, 0))
            edge = block(flip, facet, (SIDE - pc) % SIDE).astype(F32) * sign
            mirrored = jnp.where(lane % S == 0, edge, turned)
            mirrored_half = mirrored.astype(BF16)
            fresh = column_pass(1, facet, pc)
            own = block(acc, facet, pc)
            parts = []
            for b in range(2):
                mine = slice(b * PAIR, (b + 1) * PAIR)
                other = slice((1 - b) * PAIR, (2 - b) * PAIR)
                swapped = dot(wide(rows_ref, 0), mirrored_half[other])
                swapped = jnp.where(row == 0, mirrored[mine], swapped)
                parts.append((fresh[mine] + coef * (own[mine] + swapped)).astype(BF16))
            place(grid, facet, pc, jnp.concatenate(parts, axis=0))
    for facet in range(facets):
        for pc in range(SIDE):
            place(acc, facet, pc, block(back_ref, facet, pc).astype(F32))
    degrid_grid(items_ref, base, times, count, gram_ref, grid, acc, held)

    loads[5].wait()
    loads[6].wait()
    share, far = S // devices, devices // 2
    for facet in range(facets):
        mixed = [[] for _ in range(SIDE)]
        for pc in range(SIDE):
            r0, r1, r2, r3 = (acc[facet * NP + pc * SIDE + p] for p in range(SIDE))
            even, odd = r0 + r2, r0 - r2
            even_b, odd_b = r1 + r3, r1 - r3
            turned = jnp.concatenate([-odd_b[:, S:], odd_b[:, :S]], axis=1)
            for q, value in enumerate((even + even_b, odd + turned, even - even_b, odd - turned)):
                mixed[q].append(turn_pair(value.astype(BF16)))
        for q in range(SIDE):
            spec = dot(wide(inv_row_ref, 2 * q), jnp.concatenate(mixed[q], axis=1)).astype(BF16)
            parts = []
            for pc in range(SIDE):
                cols = slice(pc * S, (pc + 1) * S)
                parts += [spec[:S, cols], spec[S:, cols]]
            spec = jnp.concatenate(parts, axis=1)
            image = jnp.concatenate([dot(spec, wide(inv_col_ref, j)) for j in range(0, SIDE, 2)], axis=1)
            if send_ref is None:
                keep_ref[facet, q] = image.astype(BF16)
                continue
            odd, mine = pos & 1, pos >> 1
            for there in range(far):
                zero = image[2 * there * share : (2 * there + 1) * share].astype(BF16)
                one = image[(2 * there + 1) * share : (2 * there + 2) * share].astype(BF16)
                offset = there ^ mine
                keep_ref[offset, facet, q] = jnp.where(odd == 0, zero, one)
                send_ref[offset, facet, q] = jnp.where(odd == 0, one, zero)


def copies(moves, sems, first=0):
    return [pltpu.make_async_copy(src, dst, sems.at[first + k]) for k, (src, dst) in enumerate(moves)]


def first_kernel(facets, times, rows, coef, devices, outs, *refs):
    pos_ref, items_ref, slot_ref, plane_ref, live_ref = refs[:5]
    wk_hbm, vis_hbm, sky_hbm, row_hbm, column_hbm, *table_hbm = refs[5:14]
    gram_hbm, back_hbm, half_hbm, *images = refs[14 : 17 + outs]
    wk_ref, vis_ref, sky_ref, row_ref, column_ref, *table_refs = refs[17 + outs : 26 + outs]
    gram_ref, half_ref, back_ref, kern, kern_t, acc, grid, flip, held, sems = refs[26 + outs :]
    moves = [(wk_hbm, wk_ref), (sky_hbm, sky_ref), (row_hbm, row_ref), (vis_hbm, vis_ref), (column_hbm.at[pos_ref[0]], column_ref)]
    loads = copies(moves + list(zip(table_hbm, table_refs)), sems)
    for load in loads[:4]:
        load.start()
    later = facets * NP
    leave = copies(
        [(gram_ref, gram_hbm), (half_ref, half_hbm), (back_ref.at[pl.ds(later, F * NP - later)], back_hbm)], sems, len(loads)
    )
    prepare(
        slot_ref, plane_ref, live_ref, wk_ref, vis_ref, sky_ref, row_ref, gram_ref, half_ref, kern, kern_t, acc, held, loads, leave
    )
    for slot in range(0, F * NP, NP):
        back_ref[slot : slot + NP] = acc[slot : slot + NP].astype(BF16)
    leave[2].start()

    def half_of(cycle, facet, pc):
        first = (cycle * F + facet) * rows
        return half_ref[first : first + rows, pc * PAIR : (pc + 1) * PAIR]

    tables = (column_ref, *table_refs, [None, loads[4], None, *loads[5:]])
    keep_ref, send_ref = images if outs == 2 else (images[0], None)
    both_cycles(
        facets, coef, 0, times, items_ref[2 * times], pos_ref[0], devices, items_ref, gram_ref, back_ref, half_of, tables, grid, acc, flip, held, keep_ref, send_ref
    )
    for out in leave:
        out.wait()


def later_kernel(facet, offset, base, times, part, rows, coef, devices, outs, *refs):
    pos_ref, items_ref = refs[:2]
    gram_hbm, back_hbm, half_hbm, column_hbm, *table_hbm = refs[2:10]
    images = refs[10 : 10 + outs]
    gram_ref, back_ref, half_ref, column_ref, *table_refs = refs[10 + outs : 18 + outs]
    acc, grid, flip, held, sems = refs[18 + outs :]
    moves = [
        (half_hbm.at[pl.ds(facet * rows, rows)], half_ref.at[0]),
        (column_hbm.at[pos_ref[0]], column_ref),
        (back_hbm.at[pl.ds(offset, NP)], back_ref),
        (gram_hbm, gram_ref),
        (half_hbm.at[pl.ds((F + facet) * rows, rows)], half_ref.at[1]),
    ]
    loads = copies(moves + list(zip(table_hbm, table_refs)), sems)
    for load in loads[:4]:
        load.start()
    for load in loads[4:]:
        load.start()
    loads[0].wait()

    def half_of(cycle, _, pc):
        return half_ref[cycle, :, pc * PAIR : (pc + 1) * PAIR]

    tables = (column_ref, *table_refs, [loads[3], loads[1], *loads[4:], loads[2]])
    keep_ref, send_ref = images if outs == 2 else (images[0], None)
    both_cycles(
        1, coef, base, times, items_ref[2 * times + part], pos_ref[0], devices, items_ref, gram_ref, back_ref, half_of, tables, grid, acc, flip, held, keep_ref, send_ref
    )


def tile_lists(codes, stride):
    total = codes.shape[0]
    ids = jnp.arange(total, dtype=jnp.int32)
    before = ids[None, :] < ids[:, None]
    equal = codes[:, None] == codes[None, :]
    again = jnp.sum((equal & before).astype(jnp.int32), axis=1) > 0
    times = jnp.sum(equal.astype(jnp.int32), axis=1)
    group = jnp.where(again, LISTS * WPLANES, codes >> 6)
    rank = jnp.sum(((group[:, None] == group[None, :]) & before).astype(jnp.int32), axis=1)
    planes = jnp.arange(LISTS * WPLANES, dtype=jnp.int32)
    pairs = (jnp.sum((group[None, :] == planes[:, None]).astype(jnp.int32), axis=1) + 1) >> 1
    which = group >> 4
    earlier = (planes[None, :] < group[:, None]) & ((planes[None, :] >> 4) == which[:, None])
    base = jnp.sum(jnp.where(earlier, pairs[None, :], 0), axis=1)
    where = which * stride + base + (rank >> 1)
    slot, plane = codes & 63, (codes >> 6) & (WPLANES - 1)
    even = (rank & 1) == 0
    delta = jnp.where(even, plane + ((slot - SPARE) << 4), (slot - SPARE) << 10)
    places = jnp.arange(LISTS * stride, dtype=jnp.int32)
    hit = (places[:, None] == where[None, :]) & (which < LISTS)[None, :]
    items = (SPARE << 4) + (SPARE << 10) + jnp.sum(jnp.where(hit, delta[None, :], 0), axis=1)
    times = jnp.sum(jnp.where(hit, jnp.where(even, times, times << 16)[None, :], 0), axis=1)
    counts = jnp.sum(pairs.reshape(LISTS, WPLANES), axis=1)
    return jnp.concatenate([items, times, counts])


def exchange(value, bits, devices):
    return lax.ppermute(value, "vis", [(i, i ^ bits) for i in range(devices)])


def split_image(image, position, devices):
    share, far = S // devices, devices // 2
    parts = image.reshape(-1, SIDE, far, 2, share, P_SIZE).transpose(3, 2, 0, 1, 4, 5)
    parts = jnp.take(parts, jnp.arange(far) ^ (position >> 1), axis=1)
    odd = position & 1
    return lax.dynamic_index_in_dim(parts, odd, 0, False), lax.dynamic_index_in_dim(parts, 1 - odd, 0, False)


def merge(arrays, first, last):
    parts = [a[first:last].astype(F32) for a in arrays if a.shape[0] >= last]
    return functools.reduce(jnp.add, parts).astype(BF16)


def final_kernel(groups, *refs):
    out_ref, mixed = refs[-2:]
    f = first = 0
    for parts in groups:
        for k in range(refs[first].shape[1]):
            for q in range(SIDE):
                total = functools.reduce(jnp.add, [ref[0, k, q].astype(F32) for ref in refs[first : first + parts]])
                for c in range(SIDE):
                    mixed[f, c, pl.ds(q, total.shape[0], stride=SIDE), :] = total[:, c * S : (c + 1) * S]
            for c in range(SIDE):
                out_ref[f, :, c * S : (c + 1) * S] = mixed[f, c]
            f += 1
        first += parts


def local(model_input, w_kernels, visibilities, tile_facet, tile_patch, tile_wplane, tile_count):
    devices = lax.axis_size("vis")
    position = lax.axis_index("vis").astype(jnp.int32)
    rows = P_SIZE // devices
    weight = math.sqrt(F * NP / (TILE_CAP * devices))
    total = TILE_CAP * devices
    stride = total // 2 + WPLANES // 2 + UNROLL
    coef = GAIN * weight / 2

    slots = tile_facet * NP + (tile_patch & 3) * SIDE + (tile_patch >> 2)
    live = jnp.arange(TILE_CAP, dtype=jnp.int32) < tile_count[0]
    which = jnp.maximum(tile_facet - (FIRST - 1), 0)
    near = jnp.where(tile_facet < FIRST, slots, slots & (NP - 1))
    codes = jnp.where(live, (which << 10) + (tile_wplane << 6) + near, LISTS << 10)
    bits = 1
    while bits < devices:
        codes = jnp.concatenate([codes, exchange(codes, bits, devices)])
        bits *= 2
    items = tile_lists(codes, stride)

    lanes, row_flip = flip_tables()
    tables = [column_tables(devices), lanes, row_flip, inverse_row_tables(), inverse_column_table(weight)]
    tables = [jnp.asarray(t) for t in tables]
    here = position.reshape(1)
    smem = pl.BlockSpec(memory_space=pltpu.SMEM)
    vmem = pl.BlockSpec(memory_space=pltpu.VMEM)
    hbm = pl.BlockSpec(memory_space=pl.ANY)
    share, far = S // devices, devices // 2
    split = share % 16 == 0

    def image_shapes(facets):
        if split:
            return [jax.ShapeDtypeStruct((far, facets, SIDE, share, P_SIZE), BF16)] * 2
        return [jax.ShapeDtypeStruct((facets, SIDE, S, P_SIZE), BF16)]

    def halves_of(images):
        return images if split else split_image(images[0], position, devices)

    params = pltpu.CompilerParams(vmem_limit_bytes=VMEM_BYTES)
    outs = 2 if split else 1
    half_shape = (2 * F * rows, 2 * P_SIZE)
    gram_shape = (WPLANES, PAIR, PAIR)
    table_scratch = [pltpu.VMEM((P_SIZE, 2 * rows), BF16)] + [pltpu.VMEM(t.shape, BF16) for t in tables[1:]]

    gram, back, half_rows, *images = pl.pallas_call(
        functools.partial(first_kernel, FIRST, LISTS * stride, rows, coef, devices, outs),
        out_shape=[
            jax.ShapeDtypeStruct(gram_shape, BF16),
            jax.ShapeDtypeStruct(((F - FIRST) * NP, S, PAIR), BF16),
            jax.ShapeDtypeStruct(half_shape, BF16),
            *image_shapes(FIRST),
        ],
        in_specs=[smem] * 5 + [hbm] * 9,
        out_specs=[hbm] * 3 + [vmem] * outs,
        scratch_shapes=[
            pltpu.VMEM(w_kernels.shape, BF16),
            pltpu.VMEM(visibilities.shape, BF16),
            pltpu.VMEM((2 * F * rows, P_SIZE), BF16),
            pltpu.VMEM((2 * SIDE, P_SIZE, S), BF16),
            *table_scratch,
            pltpu.VMEM(gram_shape, BF16),
            pltpu.VMEM(half_shape, BF16),
            pltpu.VMEM((F * NP, S, PAIR), BF16),
            pltpu.VMEM(gram_shape, BF16),
            pltpu.VMEM(gram_shape, BF16),
            pltpu.VMEM((F * NP + 1, S, PAIR), F32),
            pltpu.VMEM((FIRST * NP, S, PAIR), BF16),
            pltpu.VMEM((FIRST * NP, S, PAIR), BF16),
            pltpu.VMEM((max(UNROLL, PREP_UNROLL), PAIR, PAIR), BF16),
            pltpu.SemaphoreType.DMA((12,)),
        ],
        compiler_params=params,
        cost_estimate=pl.CostEstimate(flops=30 * 10**9, bytes_accessed=12 * 2**20, transcendentals=0),
        name="first",
    )(
        here,
        items,
        slots,
        tile_wplane,
        tile_count,
        w_kernels,
        visibilities,
        model_input.reshape(2 * F * rows, P_SIZE),
        jnp.asarray(row_table()),
        *tables,
    )

    keep, send = halves_of(images)
    arrays = [[keep, exchange(send, 1, devices)]]

    def halve(group, width):
        sent = merge(arrays[group], width, 2 * width)
        return sent, exchange(sent, 2 * width, devices)

    for facet in range(FIRST, F):
        part = facet - FIRST + 1
        if part == 2:
            width = far // 2
            sent, got = halve(0, width)
            here, _ = lax.optimization_barrier((here, sent))
        images = pl.pallas_call(
            functools.partial(
                later_kernel, facet, (facet - FIRST) * NP, part * stride, LISTS * stride, part, rows, coef, devices, outs
            ),
            out_shape=image_shapes(1),
            in_specs=[smem] * 2 + [hbm] * 8,
            out_specs=[vmem] * outs,
            scratch_shapes=[
                pltpu.VMEM(gram_shape, BF16),
                pltpu.VMEM((NP, S, PAIR), BF16),
                pltpu.VMEM((2, rows, 2 * P_SIZE), BF16),
                *table_scratch,
                pltpu.VMEM((SPARE + 1, S, PAIR), F32),
                pltpu.VMEM((NP, S, PAIR), BF16),
                pltpu.VMEM((NP, S, PAIR), BF16),
                pltpu.VMEM((max(UNROLL, PREP_UNROLL), PAIR, PAIR), BF16),
                pltpu.SemaphoreType.DMA((9,)),
            ],
            compiler_params=pltpu.CompilerParams(vmem_limit_bytes=LATER_VMEM),
            cost_estimate=pl.CostEstimate(flops=14 * 10**9, bytes_accessed=6 * 2**20, transcendentals=0),
            name="facet",
        )(here, items, gram, back, half_rows, *tables)
        keep, send = halves_of(images)
        if part == 2:
            send, got = lax.optimization_barrier((send, got))
            arrays[0].append(got)
        arrays.append([keep, exchange(send, 1, devices)])
    while width > 1:
        width //= 2
        arrays[0].append(halve(0, width)[1])
    for group in range(1, LISTS):
        arrays[group] += [exchange(merge(arrays[group], k, k + 1), 2 * k, devices) for k in range(1, far)]

    def finish(groups, first, facets, before):
        operands = [a for group in groups for a in arrays[group]]
        in_specs = [pl.BlockSpec((1,) + a.shape[1:], lambda i: (0, 0, 0, 0, 0)) for a in operands]
        aliases = {len(operands): 0} if before else {}
        return pl.pallas_call(
            functools.partial(final_kernel, [len(arrays[group]) for group in groups]),
            out_shape=jax.ShapeDtypeStruct((F, rows, P_SIZE), F32),
            grid=(1,),
            in_specs=in_specs + [hbm] * len(before),
            out_specs=pl.BlockSpec((facets, rows, P_SIZE), lambda i: (first // facets, 0, 0)),
            scratch_shapes=[pltpu.VMEM((facets, SIDE, rows, S), F32)],
            input_output_aliases=aliases,
            compiler_params=pltpu.CompilerParams(vmem_limit_bytes=FINAL_VMEM),
            cost_estimate=pl.CostEstimate(flops=10**6, bytes_accessed=2**20, transcendentals=0),
            name="final",
        )(*operands, *before)

    done = finish(range(LISTS - 1), 0, F - 1, [])
    return finish([LISTS - 1], F - 1, 1, [done])


def solution(mesh):
    return jax.shard_map(
        local,
        mesh=mesh,
        in_specs=(
            P(None, "freq", "vis", None),
            P("freq", None, None, None),
            P(("freq", "vis"), None, None, None),
            P(("freq", "vis")),
            P(("freq", "vis")),
            P(("freq", "vis")),
            P(("freq", "vis")),
        ),
        out_specs=P("freq", "vis", None),
        check_vma=False,
    )
```

```python
import functools
import math

import jax
import jax.numpy as jnp
import ml_dtypes
import numpy as np
from jax import lax
from jax.experimental import pallas as pl
from jax.experimental.pallas import tpu as pltpu
from jax.sharding import PartitionSpec as P

P_SIZE = 512
S = 128
F = 4
WPLANES = 16
TILE_CAP = 32
NP = 16
SIDE = P_SIZE // S
PAIR = 2 * S
UNROLL = 6
PREP_UNROLL = 8
FIRST = 2
LISTS = F - FIRST + 1
SPARE = FIRST * NP
GAIN = 0.5
VMEM_BYTES = 60 * 1024 * 1024
LATER_VMEM = 52 * 1024 * 1024
FINAL_VMEM = 6 * 1024 * 1024

BF16 = jnp.bfloat16
F32 = jnp.float32


def angle_tables():
    index = np.arange(P_SIZE)
    angles = (index[:, None] * index[None, :] % P_SIZE) * (2.0 * np.pi / P_SIZE)
    return np.cos(angles) / np.sqrt(P_SIZE), np.sin(angles) / np.sqrt(P_SIZE)


def half(array):
    return np.asarray(array, np.float32).astype(ml_dtypes.bfloat16)


def complex_block(real, imag):
    return np.block([[real, -imag], [imag, real]])


def by_columns(table):
    rows, columns = table.shape
    return table.reshape(rows, columns // S, S).transpose(1, 0, 2)


def wide(ref, chunk):
    return jnp.concatenate([ref[chunk], ref[chunk + 1]], axis=1)


def row_table():
    cosine, sine = angle_tables()
    parts = [cosine.reshape(P_SIZE, SIDE, 1, S), -sine.reshape(P_SIZE, SIDE, 1, S)]
    return half(by_columns(np.concatenate(parts, axis=2).reshape(P_SIZE, 2 * P_SIZE)))


def column_tables(devices):
    cosine, sine = angle_tables()
    rows = P_SIZE // devices
    parts = [t.reshape(P_SIZE, devices, rows).transpose(1, 0, 2) for t in (cosine, sine)]
    return half(np.concatenate(parts, axis=2))


def flip_tables():
    small = np.zeros((S, S))
    for k in range(1, S):
        small[S - k, k] = 1.0
    zero = np.zeros((S, S))
    lanes = np.block([[small, zero], [zero, -small]])
    rows = np.zeros((PAIR, PAIR))
    for i in range(1, PAIR):
        rows[i, PAIR - i] = 1.0
    return half(by_columns(lanes)), half(by_columns(rows))


def inverse_row_tables():
    a, i = np.arange(S)[:, None], np.arange(S)[None, :]
    blocks = []
    for q in range(SIDE):
        angles = ((SIDE * a + q) * i % P_SIZE) * (2.0 * np.pi / P_SIZE)
        blocks.append(by_columns(complex_block(np.cos(angles), np.sin(angles)) / np.sqrt(P_SIZE)))
    return half(np.concatenate(blocks))


def inverse_column_table(weight):
    cosine, sine = angle_tables()
    parts = [cosine.reshape(SIDE, 1, S, P_SIZE), -sine.reshape(SIDE, 1, S, P_SIZE)]
    return half(by_columns(np.concatenate(parts, axis=1).reshape(2 * P_SIZE, P_SIZE) * weight))


def dot(a, b):
    return jnp.dot(a, b, preferred_element_type=F32)


def restack(pair):
    top = jnp.concatenate([pair[:S, :S], pair[S:, :S]], axis=1)
    bottom = jnp.concatenate([pair[:S, S:], pair[S:, S:]], axis=1)
    return jnp.concatenate([top, bottom], axis=0)


def turn_pair(pair):
    return jnp.concatenate([pair[:, :S], pair[:, S:]], axis=0)


def prepare(slot_ref, plane_ref, count_ref, wk_ref, vis_ref, sky_ref, row_ref, gram_ref, half_ref, kern, kern_t, acc, held, loads, leave):
    acc[...] = jnp.zeros_like(acc)
    loads[0].wait()
    for load in loads[4:]:
        load.start()
    for w in range(WPLANES):
        real, imag = wk_ref[w, 0], wk_ref[w, 1]
        block = jnp.concatenate(
            [jnp.concatenate([real, -imag], axis=1), jnp.concatenate([imag, real], axis=1)], axis=0
        )
        real_t, imag_t = real.T, imag.T
        block_t = jnp.concatenate(
            [jnp.concatenate([real_t, imag_t], axis=1), jnp.concatenate([-imag_t, real_t], axis=1)], axis=0
        )
        kern[w] = block
        kern_t[w] = block_t
        gram_ref[w] = dot(block_t, block).astype(BF16)
    leave[0].start()

    loads[1].wait()
    loads[2].wait()
    for pc in range(SIDE):
        half_ref[:, pc * PAIR : (pc + 1) * PAIR] = dot(sky_ref[...], wide(row_ref, 2 * pc)).astype(BF16)
    leave[1].start()

    loads[3].wait()
    count = count_ref[0]

    def right_product(n, lane):
        t = jnp.minimum(n * PREP_UNROLL + lane, TILE_CAP - 1)
        alive = jnp.where(n * PREP_UNROLL + lane < count, 1.0, 0.0).astype(F32)
        observed = jnp.concatenate([vis_ref[t, 0], vis_ref[t, 1]], axis=1)
        right = (dot(observed, kern[plane_ref[t]]) * alive).astype(BF16)
        held[lane, :, :S] = turn_pair(right)

    def left_product(n, lane):
        t = jnp.minimum(n * PREP_UNROLL + lane, TILE_CAP - 1)
        slot = slot_ref[t]
        both = dot(kern_t[plane_ref[t]], held[lane, :, :S])
        acc[slot] = acc[slot] + jnp.concatenate([both[:S], both[S:]], axis=1)

    def step(n, carry):
        for lane in range(PREP_UNROLL):
            left_product(n - 1, lane)
            right_product(n, lane)
        return carry

    batches = jnp.maximum((count + PREP_UNROLL - 1) // PREP_UNROLL, 1)
    for lane in range(PREP_UNROLL):
        right_product(0, lane)
    lax.fori_loop(1, batches, step, 0)
    for lane in range(PREP_UNROLL):
        left_product(batches - 1, lane)


def degrid_grid(items_ref, base, times, count, gram_ref, grid_ref, acc, held):
    def right_product(n, lane):
        code = items_ref[base + n * UNROLL + lane]
        first, second = (code >> 4) & (SPARE - 1), (code >> 10) & (SPARE - 1)
        pair = jnp.concatenate([grid_ref[first], grid_ref[second]], axis=0)
        right = dot(pair, gram_ref[code & (WPLANES - 1)])
        equal = items_ref[times + base + n * UNROLL + lane]
        right = [right[:S] * (equal & 0xFFFF).astype(F32), right[S:] * (equal >> 16).astype(F32)]
        held[lane] = restack(jnp.concatenate(right, axis=0).astype(BF16))

    def left_product(n, lane):
        code = items_ref[base + n * UNROLL + lane]
        both = dot(gram_ref[code & (WPLANES - 1)], held[lane])
        for k, slot in enumerate(((code >> 4) & 63, (code >> 10) & 63)):
            cols = slice(k * S, (k + 1) * S)
            acc[slot] = acc[slot] - jnp.concatenate([both[:S, cols], both[S:, cols]], axis=1)

    def step(n, carry):
        for lane in range(UNROLL):
            left_product(n - 1, lane)
            right_product(n, lane)
        return carry

    batches = jnp.maximum((count + UNROLL - 1) // UNROLL, 1)
    for lane in range(UNROLL):
        right_product(0, lane)
    lax.fori_loop(1, batches, step, 0)
    for lane in range(UNROLL):
        left_product(batches - 1, lane)


def both_cycles(
    facets, coef, base, times, count, pos, devices, items_ref, gram_ref, back_ref, half_of, tables, grid, acc, flip, held, keep_ref, send_ref
):
    column_ref, lanes_ref, rows_ref, inv_row_ref, inv_col_ref = tables[:5]
    loads = tables[5]

    def block(ref, facet, pc):
        first = facet * NP + pc * SIDE
        return ref[first : first + SIDE].reshape(P_SIZE, PAIR)

    def column_pass(cycle, facet, pc):
        part = half_of(cycle, facet, pc)
        turned = jnp.concatenate([part[:, S:], -part[:, :S]], axis=1)
        return dot(column_ref[...], jnp.concatenate([part, turned], axis=0))

    def place(ref, facet, pc, value):
        first = facet * NP + pc * SIDE
        ref[first : first + SIDE] = value.reshape(SIDE, S, PAIR)

    loads[1].wait()
    for facet in range(facets):
        for pc in range(SIDE):
            place(grid, facet, pc, column_pass(0, facet, pc).astype(BF16))
    if loads[0] is not None:
        loads[7].wait()
        acc[:NP] = back_ref[...].astype(F32)
        loads[0].wait()
    degrid_grid(items_ref, base, times, count, gram_ref, grid, acc, held)

    for load in loads[2:5]:
        if load is not None:
            load.wait()
    lane = lax.broadcasted_iota(jnp.int32, (1, PAIR), 1)
    row = lax.broadcasted_iota(jnp.int32, (PAIR, 1), 0)
    sign = jnp.where(lane < S, 1.0, -1.0).astype(F32)
    for facet in range(facets):
        for pc in range(SIDE):
            place(flip, facet, pc, block(acc, facet, pc).astype(BF16))
        for pc in range(SIDE):
            turned = dot(block(flip, facet, SIDE - 1 - pc), wide(lanes_ref, 0))
            edge = block(flip, facet, (SIDE - pc) % SIDE).astype(F32) * sign
            mirrored = jnp.where(lane % S == 0, edge, turned)
            mirrored_half = mirrored.astype(BF16)
            fresh = column_pass(1, facet, pc)
            own = block(acc, facet, pc)
            parts = []
            for b in range(2):
                mine = slice(b * PAIR, (b + 1) * PAIR)
                other = slice((1 - b) * PAIR, (2 - b) * PAIR)
                swapped = dot(wide(rows_ref, 0), mirrored_half[other])
                swapped = jnp.where(row == 0, mirrored[mine], swapped)
                parts.append((fresh[mine] + coef * (own[mine] + swapped)).astype(BF16))
            place(grid, facet, pc, jnp.concatenate(parts, axis=0))
    for facet in range(facets):
        for pc in range(SIDE):
            place(acc, facet, pc, block(back_ref, facet, pc).astype(F32))
    degrid_grid(items_ref, base, times, count, gram_ref, grid, acc, held)

    loads[5].wait()
    loads[6].wait()
    share, far = S // devices, devices // 2
    for facet in range(facets):
        mixed = [[] for _ in range(SIDE)]
        for pc in range(SIDE):
            r0, r1, r2, r3 = (acc[facet * NP + pc * SIDE + p] for p in range(SIDE))
            even, odd = r0 + r2, r0 - r2
            even_b, odd_b = r1 + r3, r1 - r3
            turned = jnp.concatenate([-odd_b[:, S:], odd_b[:, :S]], axis=1)
            for q, value in enumerate((even + even_b, odd + turned, even - even_b, odd - turned)):
                mixed[q].append(turn_pair(value.astype(BF16)))
        for q in range(SIDE):
            spec = dot(wide(inv_row_ref, 2 * q), jnp.concatenate(mixed[q], axis=1)).astype(BF16)
            for pc in range(SIDE):
                cols = slice(pc * S, (pc + 1) * S)
                flip[facet * NP + pc * SIDE + q] = jnp.concatenate([spec[:S, cols], spec[S:, cols]], axis=1)
        spec = jnp.concatenate([block(flip, facet, pc) for pc in range(SIDE)], axis=1)
        image = jnp.concatenate([dot(spec, wide(inv_col_ref, j)) for j in range(0, SIDE, 2)], axis=1).astype(BF16)
        for q in range(SIDE):
            part = image[q * S : (q + 1) * S]
            if send_ref is None:
                keep_ref[facet, q] = part
                continue
            odd, mine = pos & 1, pos >> 1
            for there in range(far):
                zero = part[2 * there * share : (2 * there + 1) * share]
                one = part[(2 * there + 1) * share : (2 * there + 2) * share]
                offset = there ^ mine
                keep_ref[offset, facet, q] = jnp.where(odd == 0, zero, one)
                send_ref[offset, facet, q] = jnp.where(odd == 0, one, zero)


def copies(moves, sems, first=0):
    return [pltpu.make_async_copy(src, dst, sems.at[first + k]) for k, (src, dst) in enumerate(moves)]


def first_kernel(facets, times, rows, coef, devices, outs, *refs):
    pos_ref, items_ref, slot_ref, plane_ref, live_ref = refs[:5]
    wk_hbm, vis_hbm, sky_hbm, row_hbm, column_hbm, *table_hbm = refs[5:14]
    gram_hbm, back_hbm, half_hbm, *images = refs[14 : 17 + outs]
    wk_ref, vis_ref, sky_ref, row_ref, column_ref, *table_refs = refs[17 + outs : 26 + outs]
    gram_ref, half_ref, back_ref, kern, kern_t, acc, grid, flip, held, sems = refs[26 + outs :]
    moves = [(wk_hbm, wk_ref), (sky_hbm, sky_ref), (row_hbm, row_ref), (vis_hbm, vis_ref), (column_hbm.at[pos_ref[0]], column_ref)]
    loads = copies(moves + list(zip(table_hbm, table_refs)), sems)
    for load in loads[:4]:
        load.start()
    later = facets * NP
    leave = copies(
        [(gram_ref, gram_hbm), (half_ref, half_hbm), (back_ref.at[pl.ds(later, F * NP - later)], back_hbm)], sems, len(loads)
    )
    prepare(
        slot_ref, plane_ref, live_ref, wk_ref, vis_ref, sky_ref, row_ref, gram_ref, half_ref, kern, kern_t, acc, held, loads, leave
    )
    for slot in range(0, F * NP, NP):
        back_ref[slot : slot + NP] = acc[slot : slot + NP].astype(BF16)
    leave[2].start()

    def half_of(cycle, facet, pc):
        first = (cycle * F + facet) * rows
        return half_ref[first : first + rows, pc * PAIR : (pc + 1) * PAIR]

    tables = (column_ref, *table_refs, [None, loads[4], None, *loads[5:]])
    keep_ref, send_ref = images if outs == 2 else (images[0], None)
    both_cycles(
        facets, coef, 0, times, items_ref[2 * times], pos_ref[0], devices, items_ref, gram_ref, back_ref, half_of, tables, grid, acc, flip, held, keep_ref, send_ref
    )
    for out in leave:
        out.wait()


def later_kernel(facet, offset, base, times, part, rows, coef, devices, outs, *refs):
    pos_ref, items_ref = refs[:2]
    gram_hbm, back_hbm, half_hbm, column_hbm, *table_hbm = refs[2:10]
    images = refs[10 : 10 + outs]
    gram_ref, back_ref, half_ref, column_ref, *table_refs = refs[10 + outs : 18 + outs]
    acc, grid, flip, held, sems = refs[18 + outs :]
    moves = [
        (half_hbm.at[pl.ds(facet * rows, rows)], half_ref.at[0]),
        (column_hbm.at[pos_ref[0]], column_ref),
        (back_hbm.at[pl.ds(offset, NP)], back_ref),
        (gram_hbm, gram_ref),
        (half_hbm.at[pl.ds((F + facet) * rows, rows)], half_ref.at[1]),
    ]
    loads = copies(moves + list(zip(table_hbm, table_refs)), sems)
    for load in loads[:4]:
        load.start()
    for load in loads[4:]:
        load.start()
    loads[0].wait()

    def half_of(cycle, _, pc):
        return half_ref[cycle, :, pc * PAIR : (pc + 1) * PAIR]

    tables = (column_ref, *table_refs, [loads[3], loads[1], *loads[4:], loads[2]])
    keep_ref, send_ref = images if outs == 2 else (images[0], None)
    both_cycles(
        1, coef, base, times, items_ref[2 * times + part], pos_ref[0], devices, items_ref, gram_ref, back_ref, half_of, tables, grid, acc, flip, held, keep_ref, send_ref
    )


def tile_lists(codes, stride):
    total = codes.shape[0]
    ids = jnp.arange(total, dtype=jnp.int32)
    before = ids[None, :] < ids[:, None]
    equal = codes[:, None] == codes[None, :]
    again = jnp.sum((equal & before).astype(jnp.int32), axis=1) > 0
    times = jnp.sum(equal.astype(jnp.int32), axis=1)
    group = jnp.where(again, LISTS * WPLANES, codes >> 6)
    rank = jnp.sum(((group[:, None] == group[None, :]) & before).astype(jnp.int32), axis=1)
    planes = jnp.arange(LISTS * WPLANES, dtype=jnp.int32)
    pairs = (jnp.sum((group[None, :] == planes[:, None]).astype(jnp.int32), axis=1) + 1) >> 1
    which = group >> 4
    earlier = (planes[None, :] < group[:, None]) & ((planes[None, :] >> 4) == which[:, None])
    base = jnp.sum(jnp.where(earlier, pairs[None, :], 0), axis=1)
    where = which * stride + base + (rank >> 1)
    slot, plane = codes & 63, (codes >> 6) & (WPLANES - 1)
    even = (rank & 1) == 0
    delta = jnp.where(even, plane + ((slot - SPARE) << 4), (slot - SPARE) << 10)
    size = LISTS * stride
    places = jnp.arange(2 * size + LISTS, dtype=jnp.int32)[:, None]
    is_item, is_times = places < size, places < 2 * size
    goal = jnp.where(is_item, places, jnp.where(is_times, places - size, places - 2 * size))
    hit = (goal == jnp.where(is_times, where[None, :], which[None, :])) & (which < LISTS)[None, :]
    times = jnp.where(even, times, times << 16)
    value = jnp.where(is_item, delta[None, :], jnp.where(is_times, times[None, :], even.astype(jnp.int32)[None, :]))
    dummy = jnp.where(places[:, 0] < size, (SPARE << 4) + (SPARE << 10), 0)
    return dummy + jnp.sum(jnp.where(hit, value, 0), axis=1)


def exchange(value, bits, devices):
    return lax.ppermute(value, "vis", [(i, i ^ bits) for i in range(devices)])


def split_image(image, position, devices):
    share, far = S // devices, devices // 2
    parts = image.reshape(-1, SIDE, far, 2, share, P_SIZE).transpose(3, 2, 0, 1, 4, 5)
    parts = jnp.take(parts, jnp.arange(far) ^ (position >> 1), axis=1)
    odd = position & 1
    return lax.dynamic_index_in_dim(parts, odd, 0, False), lax.dynamic_index_in_dim(parts, 1 - odd, 0, False)


def merge(arrays, first, last):
    parts = [a[first:last].astype(F32) for a in arrays if a.shape[0] >= last]
    return functools.reduce(jnp.add, parts).astype(BF16)


def final_kernel(groups, *refs):
    out_ref, mixed = refs[-2:]
    f = first = 0
    for parts in groups:
        for k in range(refs[first].shape[1]):
            for q in range(SIDE):
                total = functools.reduce(jnp.add, [ref[0, k, q].astype(F32) for ref in refs[first : first + parts]])
                for c in range(SIDE):
                    mixed[f, c, pl.ds(q, total.shape[0], stride=SIDE), :] = total[:, c * S : (c + 1) * S]
            for c in range(SIDE):
                out_ref[f, :, c * S : (c + 1) * S] = mixed[f, c]
            f += 1
        first += parts


def local(model_input, w_kernels, visibilities, tile_facet, tile_patch, tile_wplane, tile_count):
    devices = lax.axis_size("vis")
    position = lax.axis_index("vis").astype(jnp.int32)
    rows = P_SIZE // devices
    weight = math.sqrt(F * NP / (TILE_CAP * devices))
    total = TILE_CAP * devices
    stride = total // 2 + WPLANES // 2 + UNROLL
    coef = GAIN * weight / 2

    slots = tile_facet * NP + (tile_patch & 3) * SIDE + (tile_patch >> 2)
    live = jnp.arange(TILE_CAP, dtype=jnp.int32) < tile_count[0]
    which = jnp.maximum(tile_facet - (FIRST - 1), 0)
    near = jnp.where(tile_facet < FIRST, slots, slots & (NP - 1))
    codes = jnp.where(live, (which << 10) + (tile_wplane << 6) + near, LISTS << 10)
    bits = 1
    while bits < devices:
        codes = jnp.concatenate([codes, exchange(codes, bits, devices)])
        bits *= 2
    items = tile_lists(codes, stride)

    lanes, row_flip = flip_tables()
    tables = [column_tables(devices), lanes, row_flip, inverse_row_tables(), inverse_column_table(weight)]
    tables = [jnp.asarray(t) for t in tables]
    here = position.reshape(1)
    smem = pl.BlockSpec(memory_space=pltpu.SMEM)
    vmem = pl.BlockSpec(memory_space=pltpu.VMEM)
    hbm = pl.BlockSpec(memory_space=pl.ANY)
    share, far = S // devices, devices // 2
    split = share % 16 == 0

    def image_shapes(facets):
        if split:
            return [jax.ShapeDtypeStruct((far, facets, SIDE, share, P_SIZE), BF16)] * 2
        return [jax.ShapeDtypeStruct((facets, SIDE, S, P_SIZE), BF16)]

    def halves_of(images):
        return images if split else split_image(images[0], position, devices)

    params = pltpu.CompilerParams(vmem_limit_bytes=VMEM_BYTES)
    outs = 2 if split else 1
    half_shape = (2 * F * rows, 2 * P_SIZE)
    gram_shape = (WPLANES, PAIR, PAIR)
    table_scratch = [pltpu.VMEM((P_SIZE, 2 * rows), BF16)] + [pltpu.VMEM(t.shape, BF16) for t in tables[1:]]

    gram, back, half_rows, *images = pl.pallas_call(
        functools.partial(first_kernel, FIRST, LISTS * stride, rows, coef, devices, outs),
        out_shape=[
            jax.ShapeDtypeStruct(gram_shape, BF16),
            jax.ShapeDtypeStruct(((F - FIRST) * NP, S, PAIR), BF16),
            jax.ShapeDtypeStruct(half_shape, BF16),
            *image_shapes(FIRST),
        ],
        in_specs=[smem] * 5 + [hbm] * 9,
        out_specs=[hbm] * 3 + [vmem] * outs,
        scratch_shapes=[
            pltpu.VMEM(w_kernels.shape, BF16),
            pltpu.VMEM(visibilities.shape, BF16),
            pltpu.VMEM((2 * F * rows, P_SIZE), BF16),
            pltpu.VMEM((2 * SIDE, P_SIZE, S), BF16),
            *table_scratch,
            pltpu.VMEM(gram_shape, BF16),
            pltpu.VMEM(half_shape, BF16),
            pltpu.VMEM((F * NP, S, PAIR), BF16),
            pltpu.VMEM(gram_shape, BF16),
            pltpu.VMEM(gram_shape, BF16),
            pltpu.VMEM((F * NP + 1, S, PAIR), F32),
            pltpu.VMEM((FIRST * NP, S, PAIR), BF16),
            pltpu.VMEM((FIRST * NP, S, PAIR), BF16),
            pltpu.VMEM((max(UNROLL, PREP_UNROLL), PAIR, PAIR), BF16),
            pltpu.SemaphoreType.DMA((12,)),
        ],
        compiler_params=params,
        cost_estimate=pl.CostEstimate(flops=30 * 10**9, bytes_accessed=12 * 2**20, transcendentals=0),
        name="first",
    )(
        here,
        items,
        slots,
        tile_wplane,
        tile_count,
        w_kernels,
        visibilities,
        model_input.reshape(2 * F * rows, P_SIZE),
        jnp.asarray(row_table()),
        *tables,
    )

    keep, send = halves_of(images)
    arrays = [[keep, exchange(send, 1, devices)]]

    def halve(group, width):
        sent = merge(arrays[group], width, 2 * width)
        return sent, exchange(sent, 2 * width, devices)

    for facet in range(FIRST, F):
        part = facet - FIRST + 1
        if part == 2:
            width = far // 2
            sent, got = halve(0, width)
            here, _ = lax.optimization_barrier((here, sent))
        images = pl.pallas_call(
            functools.partial(
                later_kernel, facet, (facet - FIRST) * NP, part * stride, LISTS * stride, part, rows, coef, devices, outs
            ),
            out_shape=image_shapes(1),
            in_specs=[smem] * 2 + [hbm] * 8,
            out_specs=[vmem] * outs,
            scratch_shapes=[
                pltpu.VMEM(gram_shape, BF16),
                pltpu.VMEM((NP, S, PAIR), BF16),
                pltpu.VMEM((2, rows, 2 * P_SIZE), BF16),
                *table_scratch,
                pltpu.VMEM((SPARE + 1, S, PAIR), F32),
                pltpu.VMEM((NP, S, PAIR), BF16),
                pltpu.VMEM((NP, S, PAIR), BF16),
                pltpu.VMEM((max(UNROLL, PREP_UNROLL), PAIR, PAIR), BF16),
                pltpu.SemaphoreType.DMA((9,)),
            ],
            compiler_params=pltpu.CompilerParams(vmem_limit_bytes=LATER_VMEM),
            cost_estimate=pl.CostEstimate(flops=14 * 10**9, bytes_accessed=6 * 2**20, transcendentals=0),
            name="facet",
        )(here, items, gram, back, half_rows, *tables)
        keep, send = halves_of(images)
        if part == 2:
            send, got = lax.optimization_barrier((send, got))
            arrays[0].append(got)
        arrays.append([keep, exchange(send, 1, devices)])
    while width > 1:
        width //= 2
        arrays[0].append(halve(0, width)[1])
    for group in range(1, LISTS):
        arrays[group] += [exchange(merge(arrays[group], k, k + 1), 2 * k, devices) for k in range(1, far)]

    def finish(groups, first, facets, before):
        operands = [a for group in groups for a in arrays[group]]
        in_specs = [pl.BlockSpec((1,) + a.shape[1:], lambda i: (0, 0, 0, 0, 0)) for a in operands]
        aliases = {len(operands): 0} if before else {}
        return pl.pallas_call(
            functools.partial(final_kernel, [len(arrays[group]) for group in groups]),
            out_shape=jax.ShapeDtypeStruct((F, rows, P_SIZE), F32),
            grid=(1,),
            in_specs=in_specs + [hbm] * len(before),
            out_specs=pl.BlockSpec((facets, rows, P_SIZE), lambda i: (first // facets, 0, 0)),
            scratch_shapes=[pltpu.VMEM((facets, SIDE, rows, S), F32)],
            input_output_aliases=aliases,
            compiler_params=pltpu.CompilerParams(vmem_limit_bytes=FINAL_VMEM),
            cost_estimate=pl.CostEstimate(flops=10**6, bytes_accessed=2**20, transcendentals=0),
            name="final",
        )(*operands, *before)

    done = finish(range(LISTS - 1), 0, F - 1, [])
    return finish([LISTS - 1], F - 1, 1, [done])


def solution(mesh):
    return jax.shard_map(
        local,
        mesh=mesh,
        in_specs=(
            P(None, "freq", "vis", None),
            P("freq", None, None, None),
            P(("freq", "vis"), None, None, None),
            P(("freq", "vis")),
            P(("freq", "vis")),
            P(("freq", "vis")),
            P(("freq", "vis")),
        ),
        out_specs=P("freq", "vis", None),
        check_vma=False,
    )
```

```python
import functools
import math

import jax
import jax.numpy as jnp
import ml_dtypes
import numpy as np
from jax import lax
from jax.experimental import pallas as pl
from jax.experimental.pallas import tpu as pltpu
from jax.sharding import PartitionSpec as P

P_SIZE = 512
S = 128
F = 4
WPLANES = 16
TILE_CAP = 32
NP = 16
SIDE = P_SIZE // S
PAIR = 2 * S
UNROLL = 6
PREP_UNROLL = 8
FIRST = 2
LISTS = F - FIRST + 1
SPARE = FIRST * NP
GAIN = 0.5
FIRST_VMEM = 53 * 1024 * 1024
LATER_VMEM = 53 * 1024 * 1024
FINAL_VMEM = 6 * 1024 * 1024

BF16 = jnp.bfloat16
F32 = jnp.float32


def angle_tables():
    index = np.arange(P_SIZE)
    angles = (index[:, None] * index[None, :] % P_SIZE) * (2.0 * np.pi / P_SIZE)
    return np.cos(angles) / np.sqrt(P_SIZE), np.sin(angles) / np.sqrt(P_SIZE)


def half(array):
    return np.asarray(array, np.float32).astype(ml_dtypes.bfloat16)


def complex_block(real, imag):
    return np.block([[real, -imag], [imag, real]])


def by_columns(table):
    rows, columns = table.shape
    return table.reshape(rows, columns // S, S).transpose(1, 0, 2)


def wide(ref, chunk):
    return jnp.concatenate([ref[chunk], ref[chunk + 1]], axis=1)


def row_table():
    cosine, sine = angle_tables()
    parts = [cosine.reshape(P_SIZE, SIDE, 1, S), -sine.reshape(P_SIZE, SIDE, 1, S)]
    return half(by_columns(np.concatenate(parts, axis=2).reshape(P_SIZE, 2 * P_SIZE)))


def column_tables(devices):
    cosine, sine = angle_tables()
    rows = P_SIZE // devices
    parts = [t.reshape(P_SIZE, devices, rows).transpose(1, 0, 2) for t in (cosine, sine)]
    return half(np.concatenate(parts, axis=2))


def flip_tables():
    small = np.zeros((S, S))
    for k in range(1, S):
        small[S - k, k] = 1.0
    zero = np.zeros((S, S))
    lanes = np.block([[small, zero], [zero, -small]])
    rows = np.zeros((PAIR, PAIR))
    for i in range(1, PAIR):
        rows[i, PAIR - i] = 1.0
    return half(by_columns(lanes)), half(by_columns(rows))


def inverse_row_tables():
    a, i = np.arange(S)[:, None], np.arange(S)[None, :]
    blocks = []
    for q in range(SIDE):
        angles = ((SIDE * a + q) * i % P_SIZE) * (2.0 * np.pi / P_SIZE)
        blocks.append(by_columns(complex_block(np.cos(angles), np.sin(angles)) / np.sqrt(P_SIZE)))
    return half(np.concatenate(blocks))


def inverse_column_table(weight):
    cosine, sine = angle_tables()
    parts = [cosine.reshape(SIDE, 1, S, P_SIZE), -sine.reshape(SIDE, 1, S, P_SIZE)]
    return half(by_columns(np.concatenate(parts, axis=1).reshape(2 * P_SIZE, P_SIZE) * weight))


def small_tables(weight):
    lanes, rows = flip_tables()
    columns = inverse_column_table(weight).reshape(SIDE * SIDE, PAIR, S)
    return np.concatenate([lanes, rows, inverse_row_tables(), columns])


def inverse_columns(ref, chunk):
    first = 4 + 2 * SIDE
    parts = [ref[first + SIDE * k : first + SIDE * (k + 1)].reshape(2 * P_SIZE, S) for k in (chunk, chunk + 1)]
    return jnp.concatenate(parts, axis=1)


def dot(a, b):
    return jnp.dot(a, b, preferred_element_type=F32)


def restack(pair):
    top = jnp.concatenate([pair[:S, :S], pair[S:, :S]], axis=1)
    bottom = jnp.concatenate([pair[:S, S:], pair[S:, S:]], axis=1)
    return jnp.concatenate([top, bottom], axis=0)


def turn_pair(pair):
    return jnp.concatenate([pair[:, :S], pair[:, S:]], axis=0)


def prepare(spot_ref, count_ref, wk_ref, vis_ref, sky_ref, row_ref, gram_ref, half_ref, kern, kern_t, acc, held, loads, leave):
    acc[...] = jnp.zeros_like(acc)
    loads[0].wait()
    for load in loads[4:]:
        load.start()
    for w in range(WPLANES):
        real, imag = wk_ref[w, 0], wk_ref[w, 1]
        block = jnp.concatenate(
            [jnp.concatenate([real, -imag], axis=1), jnp.concatenate([imag, real], axis=1)], axis=0
        )
        real_t, imag_t = real.T, imag.T
        block_t = jnp.concatenate(
            [jnp.concatenate([real_t, imag_t], axis=1), jnp.concatenate([-imag_t, real_t], axis=1)], axis=0
        )
        kern[w] = block
        kern_t[w] = block_t
        part = dot(block_t, block[:, :S]).astype(BF16)
        turned = jnp.concatenate([-part[S:], part[:S]], axis=0)
        gram_ref[w] = jnp.concatenate([part, turned], axis=1)
    leave[0].start()

    loads[1].wait()
    loads[2].wait()
    for pc in range(SIDE):
        half_ref[:, pc * PAIR : (pc + 1) * PAIR] = dot(sky_ref[...], wide(row_ref, 2 * pc)).astype(BF16)
    leave[1].start()

    loads[3].wait()
    count = count_ref[0]

    def right_product(n, lane):
        t = jnp.minimum(n * PREP_UNROLL + lane, TILE_CAP - 1)
        alive = jnp.where(n * PREP_UNROLL + lane < count, 1.0, 0.0).astype(F32)
        observed = jnp.concatenate([vis_ref[t, 0], vis_ref[t, 1]], axis=1)
        right = (dot(observed, kern[spot_ref[t] >> 8]) * alive).astype(BF16)
        held[lane, :, :S] = turn_pair(right)

    def left_product(n, lane):
        t = jnp.minimum(n * PREP_UNROLL + lane, TILE_CAP - 1)
        slot = spot_ref[t] & 255
        both = dot(kern_t[spot_ref[t] >> 8], held[lane, :, :S])
        acc[slot] = acc[slot] + jnp.concatenate([both[:S], both[S:]], axis=1)

    def step(n, carry):
        for lane in range(PREP_UNROLL):
            left_product(n - 1, lane)
            right_product(n, lane)
        return carry

    batches = jnp.maximum((count + PREP_UNROLL - 1) // PREP_UNROLL, 1)
    for lane in range(PREP_UNROLL):
        right_product(0, lane)
    lax.fori_loop(1, batches, step, 0)
    for lane in range(PREP_UNROLL):
        left_product(batches - 1, lane)


def degrid_grid(items_ref, base, times, count, gram_ref, grid_ref, acc, held):
    def right_product(n, lane):
        code = items_ref[base + n * UNROLL + lane]
        first, second = (code >> 4) & (SPARE - 1), (code >> 10) & (SPARE - 1)
        pair = jnp.concatenate([grid_ref[first], grid_ref[second]], axis=0)
        right = dot(pair, gram_ref[code & (WPLANES - 1)])
        equal = items_ref[times + base + n * UNROLL + lane]
        right = [right[:S] * (equal & 0xFFFF).astype(F32), right[S:] * (equal >> 16).astype(F32)]
        held[lane] = restack(jnp.concatenate(right, axis=0).astype(BF16))

    def left_product(n, lane):
        code = items_ref[base + n * UNROLL + lane]
        both = dot(gram_ref[code & (WPLANES - 1)], held[lane])
        for k, slot in enumerate(((code >> 4) & 63, (code >> 10) & 63)):
            cols = slice(k * S, (k + 1) * S)
            acc[slot] = acc[slot] - jnp.concatenate([both[:S, cols], both[S:, cols]], axis=1)

    def step(n, carry):
        for lane in range(UNROLL):
            left_product(n - 1, lane)
            right_product(n, lane)
        return carry

    batches = jnp.maximum((count + UNROLL - 1) // UNROLL, 1)
    for lane in range(UNROLL):
        right_product(0, lane)
    lax.fori_loop(1, batches, step, 0)
    for lane in range(UNROLL):
        left_product(batches - 1, lane)


def both_cycles(
    facets, coef, base, times, count, pos, devices, items_ref, gram_ref, back_ref, half_of, tables, grid, acc, flip, held, keep_ref, send_ref
):
    column_ref, table_ref, loads = tables

    def block(ref, facet, pc):
        first = facet * NP + pc * SIDE
        return ref[first : first + SIDE].reshape(P_SIZE, PAIR)

    def column_pass(cycle, facet, pc):
        part = half_of(cycle, facet, pc)
        turned = jnp.concatenate([part[:, S:], -part[:, :S]], axis=1)
        return dot(column_ref[...], jnp.concatenate([part, turned], axis=0))

    def place(ref, facet, pc, value):
        first = facet * NP + pc * SIDE
        ref[first : first + SIDE] = value.reshape(SIDE, S, PAIR)

    loads[1].wait()
    for facet in range(facets):
        for pc in range(SIDE):
            place(grid, facet, pc, column_pass(0, facet, pc).astype(BF16))
    if loads[0] is not None:
        loads[4].wait()
        acc[:NP] = back_ref[...].astype(F32)
        loads[0].wait()
    degrid_grid(items_ref, base, times, count, gram_ref, grid, acc, held)

    for load in loads[2:4]:
        if load is not None:
            load.wait()
    lane = lax.broadcasted_iota(jnp.int32, (1, PAIR), 1)
    row = lax.broadcasted_iota(jnp.int32, (PAIR, 1), 0)
    sign = jnp.where(lane < S, 1.0, -1.0).astype(F32)
    for facet in range(facets):
        for pc in range(SIDE):
            place(flip, facet, pc, block(acc, facet, pc).astype(BF16))
        for pc in range(SIDE):
            turned = dot(block(flip, facet, SIDE - 1 - pc), wide(table_ref, 0))
            edge = block(flip, facet, (SIDE - pc) % SIDE).astype(F32) * sign
            mirrored = jnp.where(lane % S == 0, edge, turned)
            mirrored_half = mirrored.astype(BF16)
            fresh = column_pass(1, facet, pc)
            own = block(acc, facet, pc)
            parts = []
            for b in range(2):
                mine = slice(b * PAIR, (b + 1) * PAIR)
                other = slice((1 - b) * PAIR, (2 - b) * PAIR)
                swapped = dot(wide(table_ref, 2), mirrored_half[other])
                swapped = jnp.where(row == 0, mirrored[mine], swapped)
                parts.append((fresh[mine] + coef * (own[mine] + swapped)).astype(BF16))
            place(grid, facet, pc, jnp.concatenate(parts, axis=0))
    for facet in range(facets):
        for pc in range(SIDE):
            place(acc, facet, pc, block(back_ref, facet, pc).astype(F32))
    degrid_grid(items_ref, base, times, count, gram_ref, grid, acc, held)

    share, far = S // devices, devices // 2
    for facet in range(facets):
        mixed = [[] for _ in range(SIDE)]
        for pc in range(SIDE):
            r0, r1, r2, r3 = (acc[facet * NP + pc * SIDE + p] for p in range(SIDE))
            even, odd = r0 + r2, r0 - r2
            even_b, odd_b = r1 + r3, r1 - r3
            turned = jnp.concatenate([-odd_b[:, S:], odd_b[:, :S]], axis=1)
            for q, value in enumerate((even + even_b, odd + turned, even - even_b, odd - turned)):
                mixed[q].append(turn_pair(value.astype(BF16)))
        for q in range(SIDE):
            spec = dot(wide(table_ref, 4 + 2 * q), jnp.concatenate(mixed[q], axis=1)).astype(BF16)
            for pc in range(SIDE):
                cols = slice(pc * S, (pc + 1) * S)
                flip[facet * NP + pc * SIDE + q] = jnp.concatenate([spec[:S, cols], spec[S:, cols]], axis=1)
        spec = jnp.concatenate([block(flip, facet, pc) for pc in range(SIDE)], axis=1)
        image = jnp.concatenate([dot(spec, inverse_columns(table_ref, j)) for j in range(0, SIDE, 2)], axis=1).astype(BF16)
        for q in range(SIDE):
            part = image[q * S : (q + 1) * S]
            if send_ref is None:
                keep_ref[facet, q] = part
                continue
            odd, mine = pos & 1, pos >> 1
            for there in range(far):
                zero = part[2 * there * share : (2 * there + 1) * share]
                one = part[(2 * there + 1) * share : (2 * there + 2) * share]
                offset = there ^ mine
                keep_ref[offset, facet, q] = jnp.where(odd == 0, zero, one)
                send_ref[offset, facet, q] = jnp.where(odd == 0, one, zero)


def copies(moves, sems, first=0):
    return [pltpu.make_async_copy(src, dst, sems.at[first + k]) for k, (src, dst) in enumerate(moves)]


def first_kernel(facets, times, rows, coef, devices, outs, *refs):
    pos_ref, items_ref, spot_ref, live_ref = refs[:4]
    wk_hbm, vis_hbm, sky_hbm, row_hbm, column_hbm, table_hbm = refs[4:10]
    gram_hbm, back_hbm, half_hbm, *images = refs[10 : 13 + outs]
    wk_ref, vis_ref, sky_ref, row_ref, column_ref, table_ref = refs[13 + outs : 19 + outs]
    gram_ref, half_ref, back_ref, kern, kern_t, acc, grid, flip, held, sems = refs[19 + outs :]
    moves = [(wk_hbm, wk_ref), (sky_hbm, sky_ref), (row_hbm, row_ref), (vis_hbm, vis_ref), (column_hbm.at[pos_ref[0]], column_ref)]
    loads = copies(moves + [(table_hbm, table_ref)], sems)
    for load in loads[:4]:
        load.start()
    later = facets * NP
    leave = copies(
        [(gram_ref, gram_hbm), (half_ref, half_hbm), (back_ref.at[pl.ds(later, F * NP - later)], back_hbm)], sems, len(loads)
    )
    prepare(
        spot_ref, live_ref, wk_ref, vis_ref, sky_ref, row_ref, gram_ref, half_ref, kern, kern_t, acc, held, loads, leave
    )
    for slot in range(0, F * NP, NP):
        back_ref[slot : slot + NP] = acc[slot : slot + NP].astype(BF16)
    leave[2].start()

    def half_of(cycle, facet, pc):
        first = (cycle * F + facet) * rows
        return half_ref[first : first + rows, pc * PAIR : (pc + 1) * PAIR]

    tables = (column_ref, table_ref, [None, loads[4], None, loads[5]])
    keep_ref, send_ref = images if outs == 2 else (images[0], None)
    both_cycles(
        facets, coef, 0, times, items_ref[2 * times], pos_ref[0], devices, items_ref, gram_ref, back_ref, half_of, tables, grid, acc, flip, held, keep_ref, send_ref
    )
    for out in leave:
        out.wait()


def later_kernel(facet, offset, base, times, part, rows, coef, devices, outs, *refs):
    pos_ref, items_ref = refs[:2]
    gram_hbm, back_hbm, half_hbm, column_hbm, table_hbm = refs[2:7]
    images = refs[7 : 7 + outs]
    gram_ref, back_ref, half_ref, column_ref, table_ref = refs[7 + outs : 12 + outs]
    acc, grid, flip, held, sems = refs[12 + outs :]
    moves = [
        (half_hbm.at[pl.ds(facet * rows, rows)], half_ref.at[0]),
        (column_hbm.at[pos_ref[0]], column_ref),
        (back_hbm.at[pl.ds(offset, NP)], back_ref),
        (gram_hbm, gram_ref),
        (half_hbm.at[pl.ds((F + facet) * rows, rows)], half_ref.at[1]),
    ]
    loads = copies(moves + [(table_hbm, table_ref)], sems)
    for load in loads[:4]:
        load.start()
    for load in loads[4:]:
        load.start()
    loads[0].wait()

    def half_of(cycle, _, pc):
        return half_ref[cycle, :, pc * PAIR : (pc + 1) * PAIR]

    tables = (column_ref, table_ref, [loads[3], loads[1], loads[4], loads[5], loads[2]])
    keep_ref, send_ref = images if outs == 2 else (images[0], None)
    both_cycles(
        1, coef, base, times, items_ref[2 * times + part], pos_ref[0], devices, items_ref, gram_ref, back_ref, half_of, tables, grid, acc, flip, held, keep_ref, send_ref
    )


def tile_lists(codes, stride):
    total = codes.shape[0]
    ids = jnp.arange(total, dtype=jnp.int32)
    before = ids[None, :] < ids[:, None]
    equal = codes[:, None] == codes[None, :]
    again = jnp.sum((equal & before).astype(jnp.int32), axis=1) > 0
    times = jnp.sum(equal.astype(jnp.int32), axis=1)
    group = jnp.where(again, LISTS * WPLANES, codes >> 6)
    rank = jnp.sum(((group[:, None] == group[None, :]) & before).astype(jnp.int32), axis=1)
    planes = jnp.arange(LISTS * WPLANES, dtype=jnp.int32)
    pairs = (jnp.sum((group[None, :] == planes[:, None]).astype(jnp.int32), axis=1) + 1) >> 1
    which = group >> 4
    earlier = (planes[None, :] < group[:, None]) & ((planes[None, :] >> 4) == which[:, None])
    base = jnp.sum(jnp.where(earlier, pairs[None, :], 0), axis=1)
    where = which * stride + base + (rank >> 1)
    slot, plane = codes & 63, (codes >> 6) & (WPLANES - 1)
    even = (rank & 1) == 0
    delta = jnp.where(even, plane + ((slot - SPARE) << 4), (slot - SPARE) << 10)
    size = LISTS * stride
    places = jnp.arange(2 * size + LISTS, dtype=jnp.int32)[:, None]
    is_item, is_times = places < size, places < 2 * size
    goal = jnp.where(is_item, places, jnp.where(is_times, places - size, places - 2 * size))
    hit = (goal == jnp.where(is_times, where[None, :], which[None, :])) & (which < LISTS)[None, :]
    times = jnp.where(even, times, times << 16)
    value = jnp.where(is_item, delta[None, :], jnp.where(is_times, times[None, :], even.astype(jnp.int32)[None, :]))
    dummy = jnp.where(places[:, 0] < size, (SPARE << 4) + (SPARE << 10), 0)
    return dummy + jnp.sum(jnp.where(hit, value, 0), axis=1)


def exchange(value, bits, devices):
    return lax.ppermute(value, "vis", [(i, i ^ bits) for i in range(devices)])


def split_image(image, position, devices):
    share, far = S // devices, devices // 2
    parts = image.reshape(-1, SIDE, far, 2, share, P_SIZE).transpose(3, 2, 0, 1, 4, 5)
    parts = jnp.take(parts, jnp.arange(far) ^ (position >> 1), axis=1)
    odd = position & 1
    return lax.dynamic_index_in_dim(parts, odd, 0, False), lax.dynamic_index_in_dim(parts, 1 - odd, 0, False)


def merge(arrays, first, last):
    parts = [a[first:last].astype(F32) for a in arrays if a.shape[0] >= last]
    return functools.reduce(jnp.add, parts).astype(BF16)


def final_kernel(groups, *refs):
    out_ref, mixed = refs[-2:]
    f = first = 0
    for parts in groups:
        for k in range(refs[first].shape[1]):
            for q in range(SIDE):
                total = functools.reduce(jnp.add, [ref[0, k, q].astype(F32) for ref in refs[first : first + parts]])
                for c in range(SIDE):
                    mixed[f, c, pl.ds(q, total.shape[0], stride=SIDE), :] = total[:, c * S : (c + 1) * S]
            for c in range(SIDE):
                out_ref[f, :, c * S : (c + 1) * S] = mixed[f, c]
            f += 1
        first += parts


def local(model_input, w_kernels, visibilities, tile_facet, tile_patch, tile_wplane, tile_count):
    devices = lax.axis_size("vis")
    position = lax.axis_index("vis").astype(jnp.int32)
    rows = P_SIZE // devices
    weight = math.sqrt(F * NP / (TILE_CAP * devices))
    total = TILE_CAP * devices
    stride = total // 2 + WPLANES // 2 + UNROLL
    coef = GAIN * weight / 2

    slots = tile_facet * NP + (tile_patch & 3) * SIDE + (tile_patch >> 2)
    live = jnp.arange(TILE_CAP, dtype=jnp.int32) < tile_count[0]
    which = jnp.maximum(tile_facet - (FIRST - 1), 0)
    near = jnp.where(tile_facet < FIRST, slots, slots & (NP - 1))
    codes = jnp.where(live, (which << 10) + (tile_wplane << 6) + near, LISTS << 10)
    bits = 1
    while bits < devices:
        codes = jnp.concatenate([codes, exchange(codes, bits, devices)])
        bits *= 2
    items = tile_lists(codes, stride)

    tables = [jnp.asarray(column_tables(devices)), jnp.asarray(small_tables(weight))]
    here = position.reshape(1)
    smem = pl.BlockSpec(memory_space=pltpu.SMEM)
    vmem = pl.BlockSpec(memory_space=pltpu.VMEM)
    hbm = pl.BlockSpec(memory_space=pl.ANY)
    share, far = S // devices, devices // 2
    split = share % 16 == 0

    def image_shapes(facets):
        if split:
            return [jax.ShapeDtypeStruct((far, facets, SIDE, share, P_SIZE), BF16)] * 2
        return [jax.ShapeDtypeStruct((facets, SIDE, S, P_SIZE), BF16)]

    def halves_of(images):
        return images if split else split_image(images[0], position, devices)

    params = pltpu.CompilerParams(vmem_limit_bytes=FIRST_VMEM)
    outs = 2 if split else 1
    half_shape = (2 * F * rows, 2 * P_SIZE)
    gram_shape = (WPLANES, PAIR, PAIR)
    table_scratch = [pltpu.VMEM((P_SIZE, 2 * rows), BF16), pltpu.VMEM(tables[1].shape, BF16)]

    gram, back, half_rows, *images = pl.pallas_call(
        functools.partial(first_kernel, FIRST, LISTS * stride, rows, coef, devices, outs),
        out_shape=[
            jax.ShapeDtypeStruct(gram_shape, BF16),
            jax.ShapeDtypeStruct(((F - FIRST) * NP, S, PAIR), BF16),
            jax.ShapeDtypeStruct(half_shape, BF16),
            *image_shapes(FIRST),
        ],
        in_specs=[smem] * 4 + [hbm] * 6,
        out_specs=[hbm] * 3 + [vmem] * outs,
        scratch_shapes=[
            pltpu.VMEM(w_kernels.shape, BF16),
            pltpu.VMEM(visibilities.shape, BF16),
            pltpu.VMEM((2 * F * rows, P_SIZE), BF16),
            pltpu.VMEM((2 * SIDE, P_SIZE, S), BF16),
            *table_scratch,
            pltpu.VMEM(gram_shape, BF16),
            pltpu.VMEM(half_shape, BF16),
            pltpu.VMEM((F * NP, S, PAIR), BF16),
            pltpu.VMEM(gram_shape, BF16),
            pltpu.VMEM(gram_shape, BF16),
            pltpu.VMEM((F * NP + 1, S, PAIR), F32),
            pltpu.VMEM((FIRST * NP, S, PAIR), BF16),
            pltpu.VMEM((FIRST * NP, S, PAIR), BF16),
            pltpu.VMEM((max(UNROLL, PREP_UNROLL), PAIR, PAIR), BF16),
            pltpu.SemaphoreType.DMA((12,)),
        ],
        compiler_params=params,
        cost_estimate=pl.CostEstimate(flops=30 * 10**9, bytes_accessed=12 * 2**20, transcendentals=0),
        name="first",
    )(
        here,
        items,
        slots + (tile_wplane << 8),
        tile_count,
        w_kernels,
        visibilities,
        model_input.reshape(2 * F * rows, P_SIZE),
        jnp.asarray(row_table()),
        *tables,
    )

    keep, send = halves_of(images)
    arrays = [[keep, exchange(send, 1, devices)]]

    def halve(group, width):
        sent = merge(arrays[group], width, 2 * width)
        return sent, exchange(sent, 2 * width, devices)

    for facet in range(FIRST, F):
        part = facet - FIRST + 1
        if part == 2:
            width = far // 2
            sent, got = halve(0, width)
            here, _ = lax.optimization_barrier((here, sent))
        images = pl.pallas_call(
            functools.partial(
                later_kernel, facet, (facet - FIRST) * NP, part * stride, LISTS * stride, part, rows, coef, devices, outs
            ),
            out_shape=image_shapes(1),
            in_specs=[smem] * 2 + [hbm] * 5,
            out_specs=[vmem] * outs,
            scratch_shapes=[
                pltpu.VMEM(gram_shape, BF16),
                pltpu.VMEM((NP, S, PAIR), BF16),
                pltpu.VMEM((2, rows, 2 * P_SIZE), BF16),
                *table_scratch,
                pltpu.VMEM((SPARE + 1, S, PAIR), F32),
                pltpu.VMEM((NP, S, PAIR), BF16),
                pltpu.VMEM((NP, S, PAIR), BF16),
                pltpu.VMEM((max(UNROLL, PREP_UNROLL), PAIR, PAIR), BF16),
                pltpu.SemaphoreType.DMA((9,)),
            ],
            compiler_params=pltpu.CompilerParams(vmem_limit_bytes=LATER_VMEM),
            cost_estimate=pl.CostEstimate(flops=14 * 10**9, bytes_accessed=6 * 2**20, transcendentals=0),
            name="facet",
        )(here, items, gram, back, half_rows, *tables)
        keep, send = halves_of(images)
        if part == 2:
            send, got = lax.optimization_barrier((send, got))
            arrays[0].append(got)
        arrays.append([keep, exchange(send, 1, devices)])
    while width > 1:
        width //= 2
        arrays[0].append(halve(0, width)[1])
    for group in range(1, LISTS):
        arrays[group] += [exchange(merge(arrays[group], k, k + 1), 2 * k, devices) for k in range(1, far)]

    def finish(groups, first, facets, before):
        operands = [a for group in groups for a in arrays[group]]
        in_specs = [pl.BlockSpec((1,) + a.shape[1:], lambda i: (0, 0, 0, 0, 0)) for a in operands]
        aliases = {len(operands): 0} if before else {}
        return pl.pallas_call(
            functools.partial(final_kernel, [len(arrays[group]) for group in groups]),
            out_shape=jax.ShapeDtypeStruct((F, rows, P_SIZE), F32),
            grid=(1,),
            in_specs=in_specs + [hbm] * len(before),
            out_specs=pl.BlockSpec((facets, rows, P_SIZE), lambda i: (first // facets, 0, 0)),
            scratch_shapes=[pltpu.VMEM((facets, SIDE, rows, S), F32)],
            input_output_aliases=aliases,
            compiler_params=pltpu.CompilerParams(vmem_limit_bytes=FINAL_VMEM),
            cost_estimate=pl.CostEstimate(flops=10**6, bytes_accessed=2**20, transcendentals=0),
            name="final",
        )(*operands, *before)

    done = finish(range(LISTS - 1), 0, F - 1, [])
    return finish([LISTS - 1], F - 1, 1, [done])


def solution(mesh):
    return jax.shard_map(
        local,
        mesh=mesh,
        in_specs=(
            P(None, "freq", "vis", None),
            P("freq", None, None, None),
            P(("freq", "vis"), None, None, None),
            P(("freq", "vis")),
            P(("freq", "vis")),
            P(("freq", "vis")),
            P(("freq", "vis")),
        ),
        out_specs=P("freq", "vis", None),
        check_vma=False,
    )
```

```python
import functools
import math

import jax
import jax.numpy as jnp
import ml_dtypes
import numpy as np
from jax import lax
from jax.experimental import pallas as pl
from jax.experimental.pallas import tpu as pltpu
from jax.sharding import PartitionSpec as P

P_SIZE = 512
S = 128
F = 4
WPLANES = 16
TILE_CAP = 32
NP = 16
SIDE = P_SIZE // S
PAIR = 2 * S
UNROLL = 7
PREP_UNROLL = 8
FIRST = 2
LISTS = F - FIRST + 1
SPARE = FIRST * NP
GAIN = 0.5
FIRST_VMEM = 53 * 1024 * 1024
LATER_VMEM = 53 * 1024 * 1024
FINAL_VMEM = 6 * 1024 * 1024

BF16 = jnp.bfloat16
F32 = jnp.float32


def angle_tables():
    index = np.arange(P_SIZE)
    angles = (index[:, None] * index[None, :] % P_SIZE) * (2.0 * np.pi / P_SIZE)
    return np.cos(angles) / np.sqrt(P_SIZE), np.sin(angles) / np.sqrt(P_SIZE)


def half(array):
    return np.asarray(array, np.float32).astype(ml_dtypes.bfloat16)


def complex_block(real, imag):
    return np.block([[real, -imag], [imag, real]])


def by_columns(table):
    rows, columns = table.shape
    return table.reshape(rows, columns // S, S).transpose(1, 0, 2)


def wide(ref, chunk):
    return jnp.concatenate([ref[chunk], ref[chunk + 1]], axis=1)


def row_table():
    cosine, sine = angle_tables()
    parts = [cosine.reshape(P_SIZE, SIDE, 1, S), -sine.reshape(P_SIZE, SIDE, 1, S)]
    return half(by_columns(np.concatenate(parts, axis=2).reshape(P_SIZE, 2 * P_SIZE)))


def column_tables(devices):
    cosine, sine = angle_tables()
    rows = P_SIZE // devices
    parts = [t.reshape(P_SIZE, devices, rows).transpose(1, 0, 2) for t in (cosine, sine)]
    return half(np.concatenate(parts, axis=2))


def flip_tables():
    small = np.zeros((S, S))
    for k in range(1, S):
        small[S - k, k] = 1.0
    zero = np.zeros((S, S))
    lanes = np.block([[small, zero], [zero, -small]])
    rows = np.zeros((PAIR, PAIR))
    for i in range(1, PAIR):
        rows[i, PAIR - i] = 1.0
    return half(by_columns(lanes)), half(by_columns(rows))


def inverse_row_tables():
    a, i = np.arange(S)[:, None], np.arange(S)[None, :]
    blocks = []
    for q in range(SIDE):
        angles = ((SIDE * a + q) * i % P_SIZE) * (2.0 * np.pi / P_SIZE)
        blocks.append(by_columns(complex_block(np.cos(angles), np.sin(angles)) / np.sqrt(P_SIZE)))
    return half(np.concatenate(blocks))


def inverse_column_table(weight):
    cosine, sine = angle_tables()
    parts = [cosine.reshape(SIDE, 1, S, P_SIZE), -sine.reshape(SIDE, 1, S, P_SIZE)]
    return half(by_columns(np.concatenate(parts, axis=1).reshape(2 * P_SIZE, P_SIZE) * weight))


def small_tables(weight):
    lanes, rows = flip_tables()
    columns = inverse_column_table(weight).reshape(SIDE * SIDE, PAIR, S)
    return np.concatenate([lanes, rows, inverse_row_tables(), columns])


def inverse_columns(ref, chunk):
    first = 4 + 2 * SIDE
    parts = [ref[first + SIDE * k : first + SIDE * (k + 1)].reshape(2 * P_SIZE, S) for k in (chunk, chunk + 1)]
    return jnp.concatenate(parts, axis=1)


def dot(a, b):
    return jnp.dot(a, b, preferred_element_type=F32)


def restack(pair):
    top = jnp.concatenate([pair[:S, :S], pair[S:, :S]], axis=1)
    bottom = jnp.concatenate([pair[:S, S:], pair[S:, S:]], axis=1)
    return jnp.concatenate([top, bottom], axis=0)


def turn_pair(pair):
    return jnp.concatenate([pair[:, :S], pair[:, S:]], axis=0)


def prepare(spot_ref, count_ref, wk_ref, vis_ref, sky_ref, row_ref, gram_ref, half_ref, kern, kern_t, acc, held, loads, leave):
    acc[...] = jnp.zeros_like(acc)
    loads[0].wait()
    for load in loads[4:]:
        load.start()
    for w in range(WPLANES):
        real, imag = wk_ref[w, 0], wk_ref[w, 1]
        block = jnp.concatenate(
            [jnp.concatenate([real, -imag], axis=1), jnp.concatenate([imag, real], axis=1)], axis=0
        )
        real_t, imag_t = real.T, imag.T
        block_t = jnp.concatenate(
            [jnp.concatenate([real_t, imag_t], axis=1), jnp.concatenate([-imag_t, real_t], axis=1)], axis=0
        )
        kern[w] = block
        kern_t[w] = block_t
        part = dot(block_t, block[:, :S]).astype(BF16)
        turned = jnp.concatenate([-part[S:], part[:S]], axis=0)
        gram_ref[w] = jnp.concatenate([part, turned], axis=1)
    leave[0].start()

    loads[1].wait()
    loads[2].wait()
    for pc in range(SIDE):
        half_ref[:, pc * PAIR : (pc + 1) * PAIR] = dot(sky_ref[...], wide(row_ref, 2 * pc)).astype(BF16)
    leave[1].start()

    loads[3].wait()
    count = count_ref[0]

    def right_product(n, lane):
        t = jnp.minimum(n * PREP_UNROLL + lane, TILE_CAP - 1)
        alive = jnp.where(n * PREP_UNROLL + lane < count, 1.0, 0.0).astype(F32)
        observed = jnp.concatenate([vis_ref[t, 0], vis_ref[t, 1]], axis=1)
        right = (dot(observed, kern[spot_ref[t] >> 8]) * alive).astype(BF16)
        held[lane, :, :S] = turn_pair(right)

    def left_product(n, lane):
        t = jnp.minimum(n * PREP_UNROLL + lane, TILE_CAP - 1)
        slot = spot_ref[t] & 255
        both = dot(kern_t[spot_ref[t] >> 8], held[lane, :, :S])
        acc[slot] = acc[slot] + jnp.concatenate([both[:S], both[S:]], axis=1)

    def step(n, carry):
        for lane in range(PREP_UNROLL):
            left_product(n - 1, lane)
            right_product(n, lane)
        return carry

    batches = jnp.maximum((count + PREP_UNROLL - 1) // PREP_UNROLL, 1)
    for lane in range(PREP_UNROLL):
        right_product(0, lane)
    lax.fori_loop(1, batches, step, 0)
    for lane in range(PREP_UNROLL):
        left_product(batches - 1, lane)


def degrid_grid(items_ref, base, times, count, gram_ref, grid_ref, acc, held):
    def right_product(n, lane):
        code = items_ref[base + n * UNROLL + lane]
        first, second = (code >> 4) & (SPARE - 1), (code >> 10) & (SPARE - 1)
        pair = jnp.concatenate([grid_ref[first], grid_ref[second]], axis=0)
        right = dot(pair, gram_ref[code & (WPLANES - 1)])
        equal = items_ref[times + base + n * UNROLL + lane]
        right = [right[:S] * (equal & 0xFFFF).astype(F32), right[S:] * (equal >> 16).astype(F32)]
        held[lane] = restack(jnp.concatenate(right, axis=0).astype(BF16))

    def left_product(n, lane):
        code = items_ref[base + n * UNROLL + lane]
        both = dot(gram_ref[code & (WPLANES - 1)], held[lane])
        for k, slot in enumerate(((code >> 4) & 63, (code >> 10) & 63)):
            cols = slice(k * S, (k + 1) * S)
            acc[slot] = acc[slot] - jnp.concatenate([both[:S, cols], both[S:, cols]], axis=1)

    def step(n, carry):
        for lane in range(UNROLL):
            left_product(n - 1, lane)
            right_product(n, lane)
        return carry

    batches = jnp.maximum((count + UNROLL - 1) // UNROLL, 1)
    for lane in range(UNROLL):
        right_product(0, lane)
    lax.fori_loop(1, batches, step, 0)
    for lane in range(UNROLL):
        left_product(batches - 1, lane)


def both_cycles(
    facets, coef, base, times, count, pos, devices, items_ref, gram_ref, back_ref, half_of, tables, grid, acc, flip, held, keep_ref, send_ref
):
    column_ref, table_ref, loads = tables

    def block(ref, facet, pc):
        first = facet * NP + pc * SIDE
        return ref[first : first + SIDE].reshape(P_SIZE, PAIR)

    def column_pass(cycle, facet, pc):
        part = half_of(cycle, facet, pc)
        turned = jnp.concatenate([part[:, S:], -part[:, :S]], axis=1)
        return dot(column_ref[...], jnp.concatenate([part, turned], axis=0))

    def place(ref, facet, pc, value):
        first = facet * NP + pc * SIDE
        ref[first : first + SIDE] = value.reshape(SIDE, S, PAIR)

    loads[1].wait()
    for facet in range(facets):
        for pc in range(SIDE):
            place(grid, facet, pc, column_pass(0, facet, pc).astype(BF16))
    if loads[0] is not None:
        loads[4].wait()
        acc[:NP] = back_ref[...].astype(F32)
        loads[0].wait()
    degrid_grid(items_ref, base, times, count, gram_ref, grid, acc, held)

    for load in loads[2:4]:
        if load is not None:
            load.wait()
    lane = lax.broadcasted_iota(jnp.int32, (1, PAIR), 1)
    row = lax.broadcasted_iota(jnp.int32, (PAIR, 1), 0)
    sign = jnp.where(lane < S, 1.0, -1.0).astype(F32)
    for facet in range(facets):
        for pc in range(SIDE):
            place(flip, facet, pc, block(acc, facet, pc).astype(BF16))
        for pc in range(SIDE):
            turned = dot(block(flip, facet, SIDE - 1 - pc), wide(table_ref, 0))
            edge = block(flip, facet, (SIDE - pc) % SIDE).astype(F32) * sign
            mirrored = jnp.where(lane % S == 0, edge, turned)
            mirrored_half = mirrored.astype(BF16)
            fresh = column_pass(1, facet, pc)
            own = block(acc, facet, pc)
            parts = []
            for b in range(2):
                mine = slice(b * PAIR, (b + 1) * PAIR)
                other = slice((1 - b) * PAIR, (2 - b) * PAIR)
                swapped = dot(wide(table_ref, 2), mirrored_half[other])
                swapped = jnp.where(row == 0, mirrored[mine], swapped)
                parts.append((fresh[mine] + coef * (own[mine] + swapped)).astype(BF16))
            place(grid, facet, pc, jnp.concatenate(parts, axis=0))
    for facet in range(facets):
        for pc in range(SIDE):
            place(acc, facet, pc, block(back_ref, facet, pc).astype(F32))
    degrid_grid(items_ref, base, times, count, gram_ref, grid, acc, held)

    share, far = S // devices, devices // 2
    for facet in range(facets):
        mixed = [[] for _ in range(SIDE)]
        for pc in range(SIDE):
            r0, r1, r2, r3 = (acc[facet * NP + pc * SIDE + p] for p in range(SIDE))
            even, odd = r0 + r2, r0 - r2
            even_b, odd_b = r1 + r3, r1 - r3
            turned = jnp.concatenate([-odd_b[:, S:], odd_b[:, :S]], axis=1)
            for q, value in enumerate((even + even_b, odd + turned, even - even_b, odd - turned)):
                mixed[q].append(turn_pair(value.astype(BF16)))
        for q in range(SIDE):
            spec = dot(wide(table_ref, 4 + 2 * q), jnp.concatenate(mixed[q], axis=1)).astype(BF16)
            for pc in range(SIDE):
                cols = slice(pc * S, (pc + 1) * S)
                flip[facet * NP + pc * SIDE + q] = jnp.concatenate([spec[:S, cols], spec[S:, cols]], axis=1)
        spec = jnp.concatenate([block(flip, facet, pc) for pc in range(SIDE)], axis=1)
        image = jnp.concatenate([dot(spec, inverse_columns(table_ref, j)) for j in range(0, SIDE, 2)], axis=1).astype(BF16)
        for q in range(SIDE):
            part = image[q * S : (q + 1) * S]
            if send_ref is None:
                keep_ref[facet, q] = part
                continue
            odd, mine = pos & 1, pos >> 1
            for there in range(far):
                zero = part[2 * there * share : (2 * there + 1) * share]
                one = part[(2 * there + 1) * share : (2 * there + 2) * share]
                offset = there ^ mine
                keep_ref[offset, facet, q] = jnp.where(odd == 0, zero, one)
                send_ref[offset, facet, q] = jnp.where(odd == 0, one, zero)


def copies(moves, sems, first=0):
    return [pltpu.make_async_copy(src, dst, sems.at[first + k]) for k, (src, dst) in enumerate(moves)]


def first_kernel(facets, times, rows, coef, devices, outs, *refs):
    pos_ref, items_ref, spot_ref, live_ref = refs[:4]
    wk_hbm, vis_hbm, sky_hbm, row_hbm, column_hbm, table_hbm = refs[4:10]
    gram_hbm, back_hbm, half_hbm, *images = refs[10 : 13 + outs]
    wk_ref, vis_ref, sky_ref, row_ref, column_ref, table_ref = refs[13 + outs : 19 + outs]
    gram_ref, half_ref, back_ref, kern, kern_t, acc, grid, flip, held, sems = refs[19 + outs :]
    moves = [(wk_hbm, wk_ref), (sky_hbm, sky_ref), (row_hbm, row_ref), (vis_hbm, vis_ref), (column_hbm.at[pos_ref[0]], column_ref)]
    loads = copies(moves + [(table_hbm, table_ref)], sems)
    for load in loads[:4]:
        load.start()
    later = facets * NP
    leave = copies(
        [(gram_ref, gram_hbm), (half_ref, half_hbm), (back_ref.at[pl.ds(later, F * NP - later)], back_hbm)], sems, len(loads)
    )
    prepare(
        spot_ref, live_ref, wk_ref, vis_ref, sky_ref, row_ref, gram_ref, half_ref, kern, kern_t, acc, held, loads, leave
    )
    for slot in range(0, F * NP, NP):
        back_ref[slot : slot + NP] = acc[slot : slot + NP].astype(BF16)
    leave[2].start()

    def half_of(cycle, facet, pc):
        first = (cycle * F + facet) * rows
        return half_ref[first : first + rows, pc * PAIR : (pc + 1) * PAIR]

    tables = (column_ref, table_ref, [None, loads[4], None, loads[5]])
    keep_ref, send_ref = images if outs == 2 else (images[0], None)
    both_cycles(
        facets, coef, 0, times, items_ref[2 * times], pos_ref[0], devices, items_ref, gram_ref, back_ref, half_of, tables, grid, acc, flip, held, keep_ref, send_ref
    )
    for out in leave:
        out.wait()


def later_kernel(facet, offset, base, times, part, rows, coef, devices, outs, *refs):
    pos_ref, items_ref = refs[:2]
    gram_hbm, back_hbm, half_hbm, column_hbm, table_hbm = refs[2:7]
    images = refs[7 : 7 + outs]
    gram_ref, back_ref, half_ref, column_ref, table_ref = refs[7 + outs : 12 + outs]
    acc, grid, flip, held, sems = refs[12 + outs :]
    moves = [
        (half_hbm.at[pl.ds(facet * rows, rows)], half_ref.at[0]),
        (column_hbm.at[pos_ref[0]], column_ref),
        (back_hbm.at[pl.ds(offset, NP)], back_ref),
        (gram_hbm, gram_ref),
        (half_hbm.at[pl.ds((F + facet) * rows, rows)], half_ref.at[1]),
    ]
    loads = copies(moves + [(table_hbm, table_ref)], sems)
    for load in loads[:4]:
        load.start()
    for load in loads[4:]:
        load.start()
    loads[0].wait()

    def half_of(cycle, _, pc):
        return half_ref[cycle, :, pc * PAIR : (pc + 1) * PAIR]

    tables = (column_ref, table_ref, [loads[3], loads[1], loads[4], loads[5], loads[2]])
    keep_ref, send_ref = images if outs == 2 else (images[0], None)
    both_cycles(
        1, coef, base, times, items_ref[2 * times + part], pos_ref[0], devices, items_ref, gram_ref, back_ref, half_of, tables, grid, acc, flip, held, keep_ref, send_ref
    )


def tile_lists(codes, stride):
    total = codes.shape[0]
    ids = jnp.arange(total, dtype=jnp.int32)
    before = ids[None, :] < ids[:, None]
    equal = codes[:, None] == codes[None, :]
    again = jnp.sum((equal & before).astype(jnp.int32), axis=1) > 0
    times = jnp.sum(equal.astype(jnp.int32), axis=1)
    group = jnp.where(again, LISTS * WPLANES, codes >> 6)
    rank = jnp.sum(((group[:, None] == group[None, :]) & before).astype(jnp.int32), axis=1)
    planes = jnp.arange(LISTS * WPLANES, dtype=jnp.int32)
    pairs = (jnp.sum((group[None, :] == planes[:, None]).astype(jnp.int32), axis=1) + 1) >> 1
    which = group >> 4
    earlier = (planes[None, :] < group[:, None]) & ((planes[None, :] >> 4) == which[:, None])
    base = jnp.sum(jnp.where(earlier, pairs[None, :], 0), axis=1)
    where = which * stride + base + (rank >> 1)
    slot, plane = codes & 63, (codes >> 6) & (WPLANES - 1)
    even = (rank & 1) == 0
    delta = jnp.where(even, plane + ((slot - SPARE) << 4), (slot - SPARE) << 10)
    size = LISTS * stride
    places = jnp.arange(2 * size + LISTS, dtype=jnp.int32)[:, None]
    is_item, is_times = places < size, places < 2 * size
    goal = jnp.where(is_item, places, jnp.where(is_times, places - size, places - 2 * size))
    hit = (goal == jnp.where(is_times, where[None, :], which[None, :])) & (which < LISTS)[None, :]
    times = jnp.where(even, times, times << 16)
    value = jnp.where(is_item, delta[None, :], jnp.where(is_times, times[None, :], even.astype(jnp.int32)[None, :]))
    dummy = jnp.where(places[:, 0] < size, (SPARE << 4) + (SPARE << 10), 0)
    return dummy + jnp.sum(jnp.where(hit, value, 0), axis=1)


def exchange(value, bits, devices):
    return lax.ppermute(value, "vis", [(i, i ^ bits) for i in range(devices)])


def split_image(image, position, devices):
    share, far = S // devices, devices // 2
    parts = image.reshape(-1, SIDE, far, 2, share, P_SIZE).transpose(3, 2, 0, 1, 4, 5)
    parts = jnp.take(parts, jnp.arange(far) ^ (position >> 1), axis=1)
    odd = position & 1
    return lax.dynamic_index_in_dim(parts, odd, 0, False), lax.dynamic_index_in_dim(parts, 1 - odd, 0, False)


def merge(arrays, first, last):
    parts = [a[first:last].astype(F32) for a in arrays if a.shape[0] >= last]
    return functools.reduce(jnp.add, parts).astype(BF16)


def final_kernel(groups, *refs):
    out_ref, mixed = refs[-2:]
    f = first = 0
    for parts in groups:
        for k in range(refs[first].shape[1]):
            for q in range(SIDE):
                total = functools.reduce(jnp.add, [ref[0, k, q].astype(F32) for ref in refs[first : first + parts]])
                for c in range(SIDE):
                    mixed[f, c, pl.ds(q, total.shape[0], stride=SIDE), :] = total[:, c * S : (c + 1) * S]
            for c in range(SIDE):
                out_ref[f, :, c * S : (c + 1) * S] = mixed[f, c]
            f += 1
        first += parts


def local(model_input, w_kernels, visibilities, tile_facet, tile_patch, tile_wplane, tile_count):
    devices = lax.axis_size("vis")
    position = lax.axis_index("vis").astype(jnp.int32)
    rows = P_SIZE // devices
    weight = math.sqrt(F * NP / (TILE_CAP * devices))
    total = TILE_CAP * devices
    stride = total // 2 + WPLANES // 2 + UNROLL
    coef = GAIN * weight / 2

    slots = tile_facet * NP + (tile_patch & 3) * SIDE + (tile_patch >> 2)
    live = jnp.arange(TILE_CAP, dtype=jnp.int32) < tile_count[0]
    which = jnp.maximum(tile_facet - (FIRST - 1), 0)
    near = jnp.where(tile_facet < FIRST, slots, slots & (NP - 1))
    codes = jnp.where(live, (which << 10) + (tile_wplane << 6) + near, LISTS << 10)
    bits = 1
    while bits < devices:
        codes = jnp.concatenate([codes, exchange(codes, bits, devices)])
        bits *= 2
    items = tile_lists(codes, stride)

    tables = [jnp.asarray(column_tables(devices)), jnp.asarray(small_tables(weight))]
    here = position.reshape(1)
    smem = pl.BlockSpec(memory_space=pltpu.SMEM)
    vmem = pl.BlockSpec(memory_space=pltpu.VMEM)
    hbm = pl.BlockSpec(memory_space=pl.ANY)
    share, far = S // devices, devices // 2
    split = share % 16 == 0

    def image_shapes(facets):
        if split:
            return [jax.ShapeDtypeStruct((far, facets, SIDE, share, P_SIZE), BF16)] * 2
        return [jax.ShapeDtypeStruct((facets, SIDE, S, P_SIZE), BF16)]

    def halves_of(images):
        return images if split else split_image(images[0], position, devices)

    params = pltpu.CompilerParams(vmem_limit_bytes=FIRST_VMEM)
    outs = 2 if split else 1
    half_shape = (2 * F * rows, 2 * P_SIZE)
    gram_shape = (WPLANES, PAIR, PAIR)
    table_scratch = [pltpu.VMEM((P_SIZE, 2 * rows), BF16), pltpu.VMEM(tables[1].shape, BF16)]

    gram, back, half_rows, *images = pl.pallas_call(
        functools.partial(first_kernel, FIRST, LISTS * stride, rows, coef, devices, outs),
        out_shape=[
            jax.ShapeDtypeStruct(gram_shape, BF16),
            jax.ShapeDtypeStruct(((F - FIRST) * NP, S, PAIR), BF16),
            jax.ShapeDtypeStruct(half_shape, BF16),
            *image_shapes(FIRST),
        ],
        in_specs=[smem] * 4 + [hbm] * 6,
        out_specs=[hbm] * 3 + [vmem] * outs,
        scratch_shapes=[
            pltpu.VMEM(w_kernels.shape, BF16),
            pltpu.VMEM(visibilities.shape, BF16),
            pltpu.VMEM((2 * F * rows, P_SIZE), BF16),
            pltpu.VMEM((2 * SIDE, P_SIZE, S), BF16),
            *table_scratch,
            pltpu.VMEM(gram_shape, BF16),
            pltpu.VMEM(half_shape, BF16),
            pltpu.VMEM((F * NP, S, PAIR), BF16),
            pltpu.VMEM(gram_shape, BF16),
            pltpu.VMEM(gram_shape, BF16),
            pltpu.VMEM((F * NP + 1, S, PAIR), F32),
            pltpu.VMEM((FIRST * NP, S, PAIR), BF16),
            pltpu.VMEM((FIRST * NP, S, PAIR), BF16),
            pltpu.VMEM((max(UNROLL, PREP_UNROLL), PAIR, PAIR), BF16),
            pltpu.SemaphoreType.DMA((12,)),
        ],
        compiler_params=params,
        cost_estimate=pl.CostEstimate(flops=30 * 10**9, bytes_accessed=12 * 2**20, transcendentals=0),
        name="first",
    )(
        here,
        items,
        slots + (tile_wplane << 8),
        tile_count,
        w_kernels,
        visibilities,
        model_input.reshape(2 * F * rows, P_SIZE),
        jnp.asarray(row_table()),
        *tables,
    )

    keep, send = halves_of(images)
    arrays = [[keep, exchange(send, 1, devices)]]

    def halve(group, width):
        sent = merge(arrays[group], width, 2 * width)
        return sent, exchange(sent, 2 * width, devices)

    for facet in range(FIRST, F):
        part = facet - FIRST + 1
        if part == 2:
            width = far // 2
            sent, got = halve(0, width)
            here, _ = lax.optimization_barrier((here, sent))
        images = pl.pallas_call(
            functools.partial(
                later_kernel, facet, (facet - FIRST) * NP, part * stride, LISTS * stride, part, rows, coef, devices, outs
            ),
            out_shape=image_shapes(1),
            in_specs=[smem] * 2 + [hbm] * 5,
            out_specs=[vmem] * outs,
            scratch_shapes=[
                pltpu.VMEM(gram_shape, BF16),
                pltpu.VMEM((NP, S, PAIR), BF16),
                pltpu.VMEM((2, rows, 2 * P_SIZE), BF16),
                *table_scratch,
                pltpu.VMEM((SPARE + 1, S, PAIR), F32),
                pltpu.VMEM((NP, S, PAIR), BF16),
                pltpu.VMEM((NP, S, PAIR), BF16),
                pltpu.VMEM((max(UNROLL, PREP_UNROLL), PAIR, PAIR), BF16),
                pltpu.SemaphoreType.DMA((9,)),
            ],
            compiler_params=pltpu.CompilerParams(vmem_limit_bytes=LATER_VMEM),
            cost_estimate=pl.CostEstimate(flops=14 * 10**9, bytes_accessed=6 * 2**20, transcendentals=0),
            name="facet",
        )(here, items, gram, back, half_rows, *tables)
        keep, send = halves_of(images)
        if part == 2:
            send, got = lax.optimization_barrier((send, got))
            arrays[0].append(got)
        arrays.append([keep, exchange(send, 1, devices)])
    while width > 1:
        width //= 2
        arrays[0].append(halve(0, width)[1])
    for group in range(1, LISTS):
        arrays[group] += [exchange(merge(arrays[group], k, k + 1), 2 * k, devices) for k in range(1, far)]

    def finish(groups, first, facets, before):
        operands = [a for group in groups for a in arrays[group]]
        in_specs = [pl.BlockSpec((1,) + a.shape[1:], lambda i: (0, 0, 0, 0, 0)) for a in operands]
        aliases = {len(operands): 0} if before else {}
        return pl.pallas_call(
            functools.partial(final_kernel, [len(arrays[group]) for group in groups]),
            out_shape=jax.ShapeDtypeStruct((F, rows, P_SIZE), F32),
            grid=(1,),
            in_specs=in_specs + [hbm] * len(before),
            out_specs=pl.BlockSpec((facets, rows, P_SIZE), lambda i: (first // facets, 0, 0)),
            scratch_shapes=[pltpu.VMEM((facets, SIDE, rows, S), F32)],
            input_output_aliases=aliases,
            compiler_params=pltpu.CompilerParams(vmem_limit_bytes=FINAL_VMEM),
            cost_estimate=pl.CostEstimate(flops=10**6, bytes_accessed=2**20, transcendentals=0),
            name="final",
        )(*operands, *before)

    done = finish(range(LISTS - 1), 0, F - 1, [])
    return finish([LISTS - 1], F - 1, 1, [done])


def solution(mesh):
    return jax.shard_map(
        local,
        mesh=mesh,
        in_specs=(
            P(None, "freq", "vis", None),
            P("freq", None, None, None),
            P(("freq", "vis"), None, None, None),
            P(("freq", "vis")),
            P(("freq", "vis")),
            P(("freq", "vis")),
            P(("freq", "vis")),
        ),
        out_specs=P("freq", "vis", None),
        check_vma=False,
    )
```

```python
import functools
import math

import jax
import jax.numpy as jnp
import ml_dtypes
import numpy as np
from jax import lax
from jax.experimental import pallas as pl
from jax.experimental.pallas import tpu as pltpu
from jax.sharding import PartitionSpec as P

P_SIZE = 512
S = 128
F = 4
WPLANES = 16
TILE_CAP = 32
NP = 16
SIDE = P_SIZE // S
PAIR = 2 * S
UNROLL = 8
PREP_UNROLL = 8
FIRST = 2
LISTS = F - FIRST + 1
SPARE = FIRST * NP
GAIN = 0.5
FIRST_VMEM = 53 * 1024 * 1024
LATER_VMEM = 53 * 1024 * 1024
FINAL_VMEM = 6 * 1024 * 1024

BF16 = jnp.bfloat16
F32 = jnp.float32


def angle_tables():
    index = np.arange(P_SIZE)
    angles = (index[:, None] * index[None, :] % P_SIZE) * (2.0 * np.pi / P_SIZE)
    return np.cos(angles) / np.sqrt(P_SIZE), np.sin(angles) / np.sqrt(P_SIZE)


def half(array):
    return np.asarray(array, np.float32).astype(ml_dtypes.bfloat16)


def complex_block(real, imag):
    return np.block([[real, -imag], [imag, real]])


def by_columns(table):
    rows, columns = table.shape
    return table.reshape(rows, columns // S, S).transpose(1, 0, 2)


def wide(ref, chunk):
    return jnp.concatenate([ref[chunk], ref[chunk + 1]], axis=1)


def row_table():
    cosine, sine = angle_tables()
    parts = [cosine.reshape(P_SIZE, SIDE, 1, S), -sine.reshape(P_SIZE, SIDE, 1, S)]
    return half(by_columns(np.concatenate(parts, axis=2).reshape(P_SIZE, 2 * P_SIZE)))


def column_tables(devices):
    cosine, sine = angle_tables()
    rows = P_SIZE // devices
    parts = [t.reshape(P_SIZE, devices, rows).transpose(1, 0, 2) for t in (cosine, sine)]
    return half(np.concatenate(parts, axis=2))


def flip_tables():
    small = np.zeros((S, S))
    for k in range(1, S):
        small[S - k, k] = 1.0
    zero = np.zeros((S, S))
    lanes = np.block([[small, zero], [zero, -small]])
    rows = np.zeros((PAIR, PAIR))
    for i in range(1, PAIR):
        rows[i, PAIR - i] = 1.0
    return half(by_columns(lanes)), half(by_columns(rows))


def inverse_row_tables():
    a, i = np.arange(S)[:, None], np.arange(S)[None, :]
    blocks = []
    for q in range(SIDE):
        angles = ((SIDE * a + q) * i % P_SIZE) * (2.0 * np.pi / P_SIZE)
        blocks.append(by_columns(complex_block(np.cos(angles), np.sin(angles)) / np.sqrt(P_SIZE)))
    return half(np.concatenate(blocks))


def inverse_column_table(weight):
    cosine, sine = angle_tables()
    parts = [cosine.reshape(SIDE, 1, S, P_SIZE), -sine.reshape(SIDE, 1, S, P_SIZE)]
    return half(by_columns(np.concatenate(parts, axis=1).reshape(2 * P_SIZE, P_SIZE) * weight))


def small_tables(weight):
    lanes, rows = flip_tables()
    columns = inverse_column_table(weight).reshape(SIDE * SIDE, PAIR, S)
    return np.concatenate([lanes, rows, inverse_row_tables(), columns])


def inverse_columns(ref, chunk):
    first = 4 + 2 * SIDE
    parts = [ref[first + SIDE * k : first + SIDE * (k + 1)].reshape(2 * P_SIZE, S) for k in (chunk, chunk + 1)]
    return jnp.concatenate(parts, axis=1)


def dot(a, b):
    return jnp.dot(a, b, preferred_element_type=F32)


def restack(pair):
    top = jnp.concatenate([pair[:S, :S], pair[S:, :S]], axis=1)
    bottom = jnp.concatenate([pair[:S, S:], pair[S:, S:]], axis=1)
    return jnp.concatenate([top, bottom], axis=0)


def turn_pair(pair):
    return jnp.concatenate([pair[:, :S], pair[:, S:]], axis=0)


def prepare(spot_ref, count_ref, wk_ref, vis_ref, sky_ref, row_ref, gram_ref, half_ref, kern, kern_t, acc, held, loads, leave):
    acc[...] = jnp.zeros_like(acc)
    loads[0].wait()
    for load in loads[4:]:
        load.start()
    for w in range(WPLANES):
        real, imag = wk_ref[w, 0], wk_ref[w, 1]
        block = jnp.concatenate(
            [jnp.concatenate([real, -imag], axis=1), jnp.concatenate([imag, real], axis=1)], axis=0
        )
        real_t, imag_t = real.T, imag.T
        block_t = jnp.concatenate(
            [jnp.concatenate([real_t, imag_t], axis=1), jnp.concatenate([-imag_t, real_t], axis=1)], axis=0
        )
        kern[w] = block
        kern_t[w] = block_t
        part = dot(block_t, block[:, :S]).astype(BF16)
        turned = jnp.concatenate([-part[S:], part[:S]], axis=0)
        gram_ref[w] = jnp.concatenate([part, turned], axis=1)
    leave[0].start()

    loads[1].wait()
    loads[2].wait()
    for pc in range(SIDE):
        half_ref[:, pc * PAIR : (pc + 1) * PAIR] = dot(sky_ref[...], wide(row_ref, 2 * pc)).astype(BF16)
    leave[1].start()

    loads[3].wait()
    count = count_ref[0]

    def right_product(n, lane):
        t = jnp.minimum(n * PREP_UNROLL + lane, TILE_CAP - 1)
        alive = jnp.where(n * PREP_UNROLL + lane < count, 1.0, 0.0).astype(F32)
        observed = jnp.concatenate([vis_ref[t, 0], vis_ref[t, 1]], axis=1)
        right = (dot(observed, kern[spot_ref[t] >> 8]) * alive).astype(BF16)
        held[lane, :, :S] = turn_pair(right)

    def left_product(n, lane):
        t = jnp.minimum(n * PREP_UNROLL + lane, TILE_CAP - 1)
        slot = spot_ref[t] & 255
        both = dot(kern_t[spot_ref[t] >> 8], held[lane, :, :S])
        acc[slot] = acc[slot] + jnp.concatenate([both[:S], both[S:]], axis=1)

    def step(n, carry):
        for lane in range(PREP_UNROLL):
            left_product(n - 1, lane)
            right_product(n, lane)
        return carry

    batches = jnp.maximum((count + PREP_UNROLL - 1) // PREP_UNROLL, 1)
    for lane in range(PREP_UNROLL):
        right_product(0, lane)
    lax.fori_loop(1, batches, step, 0)
    for lane in range(PREP_UNROLL):
        left_product(batches - 1, lane)


def degrid_grid(items_ref, base, times, count, gram_ref, grid_ref, acc, held):
    def right_product(n, lane):
        code = items_ref[base + n * UNROLL + lane]
        first, second = (code >> 4) & (SPARE - 1), (code >> 10) & (SPARE - 1)
        pair = jnp.concatenate([grid_ref[first], grid_ref[second]], axis=0)
        right = dot(pair, gram_ref[code & (WPLANES - 1)])
        equal = items_ref[times + base + n * UNROLL + lane]
        right = [right[:S] * (equal & 0xFFFF).astype(F32), right[S:] * (equal >> 16).astype(F32)]
        held[lane] = restack(jnp.concatenate(right, axis=0).astype(BF16))

    def left_product(n, lane):
        code = items_ref[base + n * UNROLL + lane]
        both = dot(gram_ref[code & (WPLANES - 1)], held[lane])
        for k, slot in enumerate(((code >> 4) & 63, (code >> 10) & 63)):
            cols = slice(k * S, (k + 1) * S)
            acc[slot] = acc[slot] - jnp.concatenate([both[:S, cols], both[S:, cols]], axis=1)

    def step(n, carry):
        for lane in range(UNROLL):
            left_product(n - 1, lane)
            right_product(n, lane)
        return carry

    batches = jnp.maximum((count + UNROLL - 1) // UNROLL, 1)
    for lane in range(UNROLL):
        right_product(0, lane)
    lax.fori_loop(1, batches, step, 0)
    for lane in range(UNROLL):
        left_product(batches - 1, lane)


def both_cycles(
    facets, coef, base, times, count, pos, devices, items_ref, gram_ref, back_ref, half_of, tables, grid, acc, flip, held, keep_ref, send_ref
):
    column_ref, table_ref, loads = tables

    def block(ref, facet, pc):
        first = facet * NP + pc * SIDE
        return ref[first : first + SIDE].reshape(P_SIZE, PAIR)

    def column_pass(cycle, facet, pc):
        part = half_of(cycle, facet, pc)
        turned = jnp.concatenate([part[:, S:], -part[:, :S]], axis=1)
        return dot(column_ref[...], jnp.concatenate([part, turned], axis=0))

    def place(ref, facet, pc, value):
        first = facet * NP + pc * SIDE
        ref[first : first + SIDE] = value.reshape(SIDE, S, PAIR)

    loads[1].wait()
    for facet in range(facets):
        for pc in range(SIDE):
            place(grid, facet, pc, column_pass(0, facet, pc).astype(BF16))
    if loads[0] is not None:
        loads[4].wait()
        acc[:NP] = back_ref[...].astype(F32)
        loads[0].wait()
    degrid_grid(items_ref, base, times, count, gram_ref, grid, acc, held)

    for load in loads[2:4]:
        if load is not None:
            load.wait()
    lane = lax.broadcasted_iota(jnp.int32, (1, PAIR), 1)
    row = lax.broadcasted_iota(jnp.int32, (PAIR, 1), 0)
    sign = jnp.where(lane < S, 1.0, -1.0).astype(F32)
    for facet in range(facets):
        for pc in range(SIDE):
            place(flip, facet, pc, block(acc, facet, pc).astype(BF16))
        for pc in range(SIDE):
            turned = dot(block(flip, facet, SIDE - 1 - pc), wide(table_ref, 0))
            edge = block(flip, facet, (SIDE - pc) % SIDE).astype(F32) * sign
            mirrored = jnp.where(lane % S == 0, edge, turned)
            mirrored_half = mirrored.astype(BF16)
            fresh = column_pass(1, facet, pc)
            own = block(acc, facet, pc)
            parts = []
            for b in range(2):
                mine = slice(b * PAIR, (b + 1) * PAIR)
                other = slice((1 - b) * PAIR, (2 - b) * PAIR)
                swapped = dot(wide(table_ref, 2), mirrored_half[other])
                swapped = jnp.where(row == 0, mirrored[mine], swapped)
                parts.append((fresh[mine] + coef * (own[mine] + swapped)).astype(BF16))
            place(grid, facet, pc, jnp.concatenate(parts, axis=0))
    for facet in range(facets):
        for pc in range(SIDE):
            place(acc, facet, pc, block(back_ref, facet, pc).astype(F32))
    degrid_grid(items_ref, base, times, count, gram_ref, grid, acc, held)

    share, far = S // devices, devices // 2
    for facet in range(facets):
        mixed = [[] for _ in range(SIDE)]
        for pc in range(SIDE):
            r0, r1, r2, r3 = (acc[facet * NP + pc * SIDE + p] for p in range(SIDE))
            even, odd = r0 + r2, r0 - r2
            even_b, odd_b = r1 + r3, r1 - r3
            turned = jnp.concatenate([-odd_b[:, S:], odd_b[:, :S]], axis=1)
            for q, value in enumerate((even + even_b, odd + turned, even - even_b, odd - turned)):
                mixed[q].append(turn_pair(value.astype(BF16)))
        for q in range(SIDE):
            spec = dot(wide(table_ref, 4 + 2 * q), jnp.concatenate(mixed[q], axis=1)).astype(BF16)
            for pc in range(SIDE):
                cols = slice(pc * S, (pc + 1) * S)
                flip[facet * NP + pc * SIDE + q] = jnp.concatenate([spec[:S, cols], spec[S:, cols]], axis=1)
        spec = jnp.concatenate([block(flip, facet, pc) for pc in range(SIDE)], axis=1)
        image = jnp.concatenate([dot(spec, inverse_columns(table_ref, j)) for j in range(0, SIDE, 2)], axis=1).astype(BF16)
        for q in range(SIDE):
            part = image[q * S : (q + 1) * S]
            if send_ref is None:
                keep_ref[facet, q] = part
                continue
            odd, mine = pos & 1, pos >> 1
            for there in range(far):
                zero = part[2 * there * share : (2 * there + 1) * share]
                one = part[(2 * there + 1) * share : (2 * there + 2) * share]
                offset = there ^ mine
                keep_ref[offset, facet, q] = jnp.where(odd == 0, zero, one)
                send_ref[offset, facet, q] = jnp.where(odd == 0, one, zero)


def copies(moves, sems, first=0):
    return [pltpu.make_async_copy(src, dst, sems.at[first + k]) for k, (src, dst) in enumerate(moves)]


def first_kernel(facets, times, rows, coef, devices, outs, *refs):
    pos_ref, items_ref, spot_ref, live_ref = refs[:4]
    wk_hbm, vis_hbm, sky_hbm, row_hbm, column_hbm, table_hbm = refs[4:10]
    gram_hbm, back_hbm, half_hbm, *images = refs[10 : 13 + outs]
    wk_ref, vis_ref, sky_ref, row_ref, column_ref, table_ref = refs[13 + outs : 19 + outs]
    gram_ref, half_ref, back_ref, kern, kern_t, acc, grid, flip, held, sems = refs[19 + outs :]
    moves = [(wk_hbm, wk_ref), (sky_hbm, sky_ref), (row_hbm, row_ref), (vis_hbm, vis_ref), (column_hbm.at[pos_ref[0]], column_ref)]
    loads = copies(moves + [(table_hbm, table_ref)], sems)
    for load in loads[:4]:
        load.start()
    later = facets * NP
    leave = copies(
        [(gram_ref, gram_hbm), (half_ref, half_hbm), (back_ref.at[pl.ds(later, F * NP - later)], back_hbm)], sems, len(loads)
    )
    prepare(
        spot_ref, live_ref, wk_ref, vis_ref, sky_ref, row_ref, gram_ref, half_ref, kern, kern_t, acc, held, loads, leave
    )
    for slot in range(0, F * NP, NP):
        back_ref[slot : slot + NP] = acc[slot : slot + NP].astype(BF16)
    leave[2].start()

    def half_of(cycle, facet, pc):
        first = (cycle * F + facet) * rows
        return half_ref[first : first + rows, pc * PAIR : (pc + 1) * PAIR]

    tables = (column_ref, table_ref, [None, loads[4], None, loads[5]])
    keep_ref, send_ref = images if outs == 2 else (images[0], None)
    both_cycles(
        facets, coef, 0, times, items_ref[2 * times], pos_ref[0], devices, items_ref, gram_ref, back_ref, half_of, tables, grid, acc, flip, held, keep_ref, send_ref
    )
    for out in leave:
        out.wait()


def later_kernel(facet, offset, base, times, part, rows, coef, devices, outs, *refs):
    pos_ref, items_ref = refs[:2]
    gram_hbm, back_hbm, half_hbm, column_hbm, table_hbm = refs[2:7]
    images = refs[7 : 7 + outs]
    gram_ref, back_ref, half_ref, column_ref, table_ref = refs[7 + outs : 12 + outs]
    acc, grid, flip, held, sems = refs[12 + outs :]
    moves = [
        (half_hbm.at[pl.ds(facet * rows, rows)], half_ref.at[0]),
        (column_hbm.at[pos_ref[0]], column_ref),
        (back_hbm.at[pl.ds(offset, NP)], back_ref),
        (gram_hbm, gram_ref),
        (half_hbm.at[pl.ds((F + facet) * rows, rows)], half_ref.at[1]),
    ]
    loads = copies(moves + [(table_hbm, table_ref)], sems)
    for load in loads[:4]:
        load.start()
    for load in loads[4:]:
        load.start()
    loads[0].wait()

    def half_of(cycle, _, pc):
        return half_ref[cycle, :, pc * PAIR : (pc + 1) * PAIR]

    tables = (column_ref, table_ref, [loads[3], loads[1], loads[4], loads[5], loads[2]])
    keep_ref, send_ref = images if outs == 2 else (images[0], None)
    both_cycles(
        1, coef, base, times, items_ref[2 * times + part], pos_ref[0], devices, items_ref, gram_ref, back_ref, half_of, tables, grid, acc, flip, held, keep_ref, send_ref
    )


def tile_lists(codes, stride):
    total = codes.shape[0]
    ids = jnp.arange(total, dtype=jnp.int32)
    before = ids[None, :] < ids[:, None]
    equal = codes[:, None] == codes[None, :]
    again = jnp.sum((equal & before).astype(jnp.int32), axis=1) > 0
    times = jnp.sum(equal.astype(jnp.int32), axis=1)
    group = jnp.where(again, LISTS * WPLANES, codes >> 6)
    rank = jnp.sum(((group[:, None] == group[None, :]) & before).astype(jnp.int32), axis=1)
    planes = jnp.arange(LISTS * WPLANES, dtype=jnp.int32)
    pairs = (jnp.sum((group[None, :] == planes[:, None]).astype(jnp.int32), axis=1) + 1) >> 1
    which = group >> 4
    earlier = (planes[None, :] < group[:, None]) & ((planes[None, :] >> 4) == which[:, None])
    base = jnp.sum(jnp.where(earlier, pairs[None, :], 0), axis=1)
    where = which * stride + base + (rank >> 1)
    slot, plane = codes & 63, (codes >> 6) & (WPLANES - 1)
    even = (rank & 1) == 0
    delta = jnp.where(even, plane + ((slot - SPARE) << 4), (slot - SPARE) << 10)
    size = LISTS * stride
    places = jnp.arange(2 * size + LISTS, dtype=jnp.int32)[:, None]
    is_item, is_times = places < size, places < 2 * size
    goal = jnp.where(is_item, places, jnp.where(is_times, places - size, places - 2 * size))
    hit = (goal == jnp.where(is_times, where[None, :], which[None, :])) & (which < LISTS)[None, :]
    times = jnp.where(even, times, times << 16)
    value = jnp.where(is_item, delta[None, :], jnp.where(is_times, times[None, :], even.astype(jnp.int32)[None, :]))
    dummy = jnp.where(places[:, 0] < size, (SPARE << 4) + (SPARE << 10), 0)
    return dummy + jnp.sum(jnp.where(hit, value, 0), axis=1)


def exchange(value, bits, devices):
    return lax.ppermute(value, "vis", [(i, i ^ bits) for i in range(devices)])


def split_image(image, position, devices):
    share, far = S // devices, devices // 2
    parts = image.reshape(-1, SIDE, far, 2, share, P_SIZE).transpose(3, 2, 0, 1, 4, 5)
    parts = jnp.take(parts, jnp.arange(far) ^ (position >> 1), axis=1)
    odd = position & 1
    return lax.dynamic_index_in_dim(parts, odd, 0, False), lax.dynamic_index_in_dim(parts, 1 - odd, 0, False)


def merge(arrays, first, last):
    parts = [a[first:last].astype(F32) for a in arrays if a.shape[0] >= last]
    return functools.reduce(jnp.add, parts).astype(BF16)


def final_kernel(groups, *refs):
    out_ref, mixed = refs[-2:]
    f = first = 0
    for parts in groups:
        for k in range(refs[first].shape[1]):
            for q in range(SIDE):
                total = functools.reduce(jnp.add, [ref[0, k, q].astype(F32) for ref in refs[first : first + parts]])
                for c in range(SIDE):
                    mixed[f, c, pl.ds(q, total.shape[0], stride=SIDE), :] = total[:, c * S : (c + 1) * S]
            for c in range(SIDE):
                out_ref[f, :, c * S : (c + 1) * S] = mixed[f, c]
            f += 1
        first += parts


def local(model_input, w_kernels, visibilities, tile_facet, tile_patch, tile_wplane, tile_count):
    devices = lax.axis_size("vis")
    position = lax.axis_index("vis").astype(jnp.int32)
    rows = P_SIZE // devices
    weight = math.sqrt(F * NP / (TILE_CAP * devices))
    total = TILE_CAP * devices
    stride = total // 2 + WPLANES // 2 + UNROLL
    coef = GAIN * weight / 2

    slots = tile_facet * NP + (tile_patch & 3) * SIDE + (tile_patch >> 2)
    live = jnp.arange(TILE_CAP, dtype=jnp.int32) < tile_count[0]
    which = jnp.maximum(tile_facet - (FIRST - 1), 0)
    near = jnp.where(tile_facet < FIRST, slots, slots & (NP - 1))
    codes = jnp.where(live, (which << 10) + (tile_wplane << 6) + near, LISTS << 10)
    bits = 1
    while bits < devices:
        codes = jnp.concatenate([codes, exchange(codes, bits, devices)])
        bits *= 2
    items = tile_lists(codes, stride)

    tables = [jnp.asarray(column_tables(devices)), jnp.asarray(small_tables(weight))]
    here = position.reshape(1)
    smem = pl.BlockSpec(memory_space=pltpu.SMEM)
    vmem = pl.BlockSpec(memory_space=pltpu.VMEM)
    hbm = pl.BlockSpec(memory_space=pl.ANY)
    share, far = S // devices, devices // 2
    split = share % 16 == 0

    def image_shapes(facets):
        if split:
            return [jax.ShapeDtypeStruct((far, facets, SIDE, share, P_SIZE), BF16)] * 2
        return [jax.ShapeDtypeStruct((facets, SIDE, S, P_SIZE), BF16)]

    def halves_of(images):
        return images if split else split_image(images[0], position, devices)

    params = pltpu.CompilerParams(vmem_limit_bytes=FIRST_VMEM)
    outs = 2 if split else 1
    half_shape = (2 * F * rows, 2 * P_SIZE)
    gram_shape = (WPLANES, PAIR, PAIR)
    table_scratch = [pltpu.VMEM((P_SIZE, 2 * rows), BF16), pltpu.VMEM(tables[1].shape, BF16)]

    gram, back, half_rows, *images = pl.pallas_call(
        functools.partial(first_kernel, FIRST, LISTS * stride, rows, coef, devices, outs),
        out_shape=[
            jax.ShapeDtypeStruct(gram_shape, BF16),
            jax.ShapeDtypeStruct(((F - FIRST) * NP, S, PAIR), BF16),
            jax.ShapeDtypeStruct(half_shape, BF16),
            *image_shapes(FIRST),
        ],
        in_specs=[smem] * 4 + [hbm] * 6,
        out_specs=[hbm] * 3 + [vmem] * outs,
        scratch_shapes=[
            pltpu.VMEM(w_kernels.shape, BF16),
            pltpu.VMEM(visibilities.shape, BF16),
            pltpu.VMEM((2 * F * rows, P_SIZE), BF16),
            pltpu.VMEM((2 * SIDE, P_SIZE, S), BF16),
            *table_scratch,
            pltpu.VMEM(gram_shape, BF16),
            pltpu.VMEM(half_shape, BF16),
            pltpu.VMEM((F * NP, S, PAIR), BF16),
            pltpu.VMEM(gram_shape, BF16),
            pltpu.VMEM(gram_shape, BF16),
            pltpu.VMEM((F * NP + 1, S, PAIR), F32),
            pltpu.VMEM((FIRST * NP, S, PAIR), BF16),
            pltpu.VMEM((FIRST * NP, S, PAIR), BF16),
            pltpu.VMEM((max(UNROLL, PREP_UNROLL), PAIR, PAIR), BF16),
            pltpu.SemaphoreType.DMA((12,)),
        ],
        compiler_params=params,
        cost_estimate=pl.CostEstimate(flops=30 * 10**9, bytes_accessed=12 * 2**20, transcendentals=0),
        name="first",
    )(
        here,
        items,
        slots + (tile_wplane << 8),
        tile_count,
        w_kernels,
        visibilities,
        model_input.reshape(2 * F * rows, P_SIZE),
        jnp.asarray(row_table()),
        *tables,
    )

    keep, send = halves_of(images)
    arrays = [[keep, exchange(send, 1, devices)]]

    def halve(group, width):
        sent = merge(arrays[group], width, 2 * width)
        return sent, exchange(sent, 2 * width, devices)

    for facet in range(FIRST, F):
        part = facet - FIRST + 1
        if part == 2:
            width = far // 2
            sent, got = halve(0, width)
            here, _ = lax.optimization_barrier((here, sent))
        images = pl.pallas_call(
            functools.partial(
                later_kernel, facet, (facet - FIRST) * NP, part * stride, LISTS * stride, part, rows, coef, devices, outs
            ),
            out_shape=image_shapes(1),
            in_specs=[smem] * 2 + [hbm] * 5,
            out_specs=[vmem] * outs,
            scratch_shapes=[
                pltpu.VMEM(gram_shape, BF16),
                pltpu.VMEM((NP, S, PAIR), BF16),
                pltpu.VMEM((2, rows, 2 * P_SIZE), BF16),
                *table_scratch,
                pltpu.VMEM((SPARE + 1, S, PAIR), F32),
                pltpu.VMEM((NP, S, PAIR), BF16),
                pltpu.VMEM((NP, S, PAIR), BF16),
                pltpu.VMEM((max(UNROLL, PREP_UNROLL), PAIR, PAIR), BF16),
                pltpu.SemaphoreType.DMA((9,)),
            ],
            compiler_params=pltpu.CompilerParams(vmem_limit_bytes=LATER_VMEM),
            cost_estimate=pl.CostEstimate(flops=14 * 10**9, bytes_accessed=6 * 2**20, transcendentals=0),
            name="facet",
        )(here, items, gram, back, half_rows, *tables)
        keep, send = halves_of(images)
        if part == 2:
            send, got = lax.optimization_barrier((send, got))
            arrays[0].append(got)
        arrays.append([keep, exchange(send, 1, devices)])
    while width > 1:
        width //= 2
        arrays[0].append(halve(0, width)[1])
    for group in range(1, LISTS):
        arrays[group] += [exchange(merge(arrays[group], k, k + 1), 2 * k, devices) for k in range(1, far)]

    def finish(groups, first, facets, before):
        operands = [a for group in groups for a in arrays[group]]
        in_specs = [pl.BlockSpec((1,) + a.shape[1:], lambda i: (0, 0, 0, 0, 0)) for a in operands]
        aliases = {len(operands): 0} if before else {}
        return pl.pallas_call(
            functools.partial(final_kernel, [len(arrays[group]) for group in groups]),
            out_shape=jax.ShapeDtypeStruct((F, rows, P_SIZE), F32),
            grid=(1,),
            in_specs=in_specs + [hbm] * len(before),
            out_specs=pl.BlockSpec((facets, rows, P_SIZE), lambda i: (first // facets, 0, 0)),
            scratch_shapes=[pltpu.VMEM((facets, SIDE, rows, S), F32)],
            input_output_aliases=aliases,
            compiler_params=pltpu.CompilerParams(vmem_limit_bytes=FINAL_VMEM),
            cost_estimate=pl.CostEstimate(flops=10**6, bytes_accessed=2**20, transcendentals=0),
            name="final",
        )(*operands, *before)

    done = finish(range(LISTS - 1), 0, F - 1, [])
    return finish([LISTS - 1], F - 1, 1, [done])


def solution(mesh):
    return jax.shard_map(
        local,
        mesh=mesh,
        in_specs=(
            P(None, "freq", "vis", None),
            P("freq", None, None, None),
            P(("freq", "vis"), None, None, None),
            P(("freq", "vis")),
            P(("freq", "vis")),
            P(("freq", "vis")),
            P(("freq", "vis")),
        ),
        out_specs=P("freq", "vis", None),
        check_vma=False,
    )
```

```python
import functools
import math

import jax
import jax.numpy as jnp
import ml_dtypes
import numpy as np
from jax import lax
from jax.experimental import pallas as pl
from jax.experimental.pallas import tpu as pltpu
from jax.sharding import PartitionSpec as P

P_SIZE = 512
S = 128
F = 4
WPLANES = 16
TILE_CAP = 32
NP = 16
SIDE = P_SIZE // S
PAIR = 2 * S
UNROLL = 7
PREP_UNROLL = 8
FIRST = 2
LISTS = F - FIRST + 1
SPARE = FIRST * NP
GAIN = 0.5
FIRST_VMEM = 53 * 1024 * 1024
LATER_VMEM = 53 * 1024 * 1024
FINAL_VMEM = 6 * 1024 * 1024

BF16 = jnp.bfloat16
F32 = jnp.float32


def angle_tables():
    index = np.arange(P_SIZE)
    angles = (index[:, None] * index[None, :] % P_SIZE) * (2.0 * np.pi / P_SIZE)
    return np.cos(angles) / np.sqrt(P_SIZE), np.sin(angles) / np.sqrt(P_SIZE)


def half(array):
    return np.asarray(array, np.float32).astype(ml_dtypes.bfloat16)


def complex_block(real, imag):
    return np.block([[real, -imag], [imag, real]])


def by_columns(table):
    rows, columns = table.shape
    return table.reshape(rows, columns // S, S).transpose(1, 0, 2)


def wide(ref, chunk):
    return jnp.concatenate([ref[chunk], ref[chunk + 1]], axis=1)


def row_table():
    cosine, sine = angle_tables()
    parts = [cosine.reshape(P_SIZE, SIDE, 1, S), -sine.reshape(P_SIZE, SIDE, 1, S)]
    return half(by_columns(np.concatenate(parts, axis=2).reshape(P_SIZE, 2 * P_SIZE)))


def column_tables(devices):
    cosine, sine = angle_tables()
    rows = P_SIZE // devices
    parts = [t.reshape(P_SIZE, devices, rows).transpose(1, 0, 2) for t in (cosine, sine)]
    return half(np.concatenate(parts, axis=2))


def flip_tables():
    small = np.zeros((S, S))
    for k in range(1, S):
        small[S - k, k] = 1.0
    zero = np.zeros((S, S))
    lanes = np.block([[small, zero], [zero, -small]])
    rows = np.zeros((PAIR, PAIR))
    for i in range(1, PAIR):
        rows[i, PAIR - i] = 1.0
    return half(by_columns(lanes)), half(by_columns(rows))


def inverse_row_tables():
    a, i = np.arange(S)[:, None], np.arange(S)[None, :]
    blocks = []
    for q in range(SIDE):
        angles = ((SIDE * a + q) * i % P_SIZE) * (2.0 * np.pi / P_SIZE)
        blocks.append(by_columns(complex_block(np.cos(angles), np.sin(angles)) / np.sqrt(P_SIZE)))
    return half(np.concatenate(blocks))


def inverse_column_table(weight):
    cosine, sine = angle_tables()
    parts = [cosine.reshape(SIDE, 1, S, P_SIZE), -sine.reshape(SIDE, 1, S, P_SIZE)]
    return half(by_columns(np.concatenate(parts, axis=1).reshape(2 * P_SIZE, P_SIZE) * weight))


def small_tables(weight):
    lanes, rows = flip_tables()
    columns = inverse_column_table(weight).reshape(SIDE * SIDE, PAIR, S)
    return np.concatenate([lanes, rows, inverse_row_tables(), columns])


def inverse_columns(ref, chunk):
    first = 4 + 2 * SIDE
    parts = [ref[first + SIDE * k : first + SIDE * (k + 1)].reshape(2 * P_SIZE, S) for k in (chunk, chunk + 1)]
    return jnp.concatenate(parts, axis=1)


def dot(a, b):
    return jnp.dot(a, b, preferred_element_type=F32)


def restack(pair):
    top = jnp.concatenate([pair[:S, :S], pair[S:, :S]], axis=1)
    bottom = jnp.concatenate([pair[:S, S:], pair[S:, S:]], axis=1)
    return jnp.concatenate([top, bottom], axis=0)


def turn_pair(pair):
    return jnp.concatenate([pair[:, :S], pair[:, S:]], axis=0)


def prepare(spot_ref, count_ref, wk_ref, vis_ref, sky_ref, row_ref, gram_ref, half_ref, kern, kern_t, acc, held, loads, leave):
    acc[...] = jnp.zeros_like(acc)
    loads[0].wait()
    for load in loads[4:]:
        load.start()
    for w in range(WPLANES):
        real, imag = wk_ref[w, 0], wk_ref[w, 1]
        block = jnp.concatenate(
            [jnp.concatenate([real, -imag], axis=1), jnp.concatenate([imag, real], axis=1)], axis=0
        )
        real_t, imag_t = real.T, imag.T
        block_t = jnp.concatenate(
            [jnp.concatenate([real_t, imag_t], axis=1), jnp.concatenate([-imag_t, real_t], axis=1)], axis=0
        )
        kern[w] = block
        kern_t[w] = block_t
        part = dot(block_t, block[:, :S]).astype(BF16)
        turned = jnp.concatenate([-part[S:], part[:S]], axis=0)
        gram_ref[w] = jnp.concatenate([part, turned], axis=1)
    leave[0].start()

    loads[1].wait()
    loads[2].wait()
    for pc in range(SIDE):
        half_ref[:, pc * PAIR : (pc + 1) * PAIR] = dot(sky_ref[...], wide(row_ref, 2 * pc)).astype(BF16)
    leave[1].start()

    loads[3].wait()
    count = count_ref[0]

    def right_product(n, lane):
        t = jnp.minimum(n * PREP_UNROLL + lane, TILE_CAP - 1)
        alive = jnp.where(n * PREP_UNROLL + lane < count, 1.0, 0.0).astype(F32)
        observed = jnp.concatenate([vis_ref[t, 0], vis_ref[t, 1]], axis=1)
        right = (dot(observed, kern[spot_ref[t] >> 8]) * alive).astype(BF16)
        held[lane, :, :S] = turn_pair(right)

    def left_product(n, lane):
        t = jnp.minimum(n * PREP_UNROLL + lane, TILE_CAP - 1)
        slot = spot_ref[t] & 255
        both = dot(kern_t[spot_ref[t] >> 8], held[lane, :, :S])
        acc[slot] = acc[slot] + jnp.concatenate([both[:S], both[S:]], axis=1)

    def step(n, carry):
        for lane in range(PREP_UNROLL):
            left_product(n - 1, lane)
            right_product(n, lane)
        return carry

    batches = jnp.maximum((count + PREP_UNROLL - 1) // PREP_UNROLL, 1)
    for lane in range(PREP_UNROLL):
        right_product(0, lane)
    lax.fori_loop(1, batches, step, 0)
    for lane in range(PREP_UNROLL):
        left_product(batches - 1, lane)


def degrid_grid(items_ref, base, times, count, gram_ref, grid_ref, acc, held):
    def right_product(n, lane):
        code = items_ref[base + n * UNROLL + lane]
        first, second = (code >> 4) & (SPARE - 1), (code >> 10) & (SPARE - 1)
        pair = jnp.concatenate([grid_ref[first], grid_ref[second]], axis=0)
        right = dot(pair, gram_ref[code & (WPLANES - 1)])
        equal = items_ref[times + base + n * UNROLL + lane]
        right = [right[:S] * (equal & 0xFFFF).astype(F32), right[S:] * (equal >> 16).astype(F32)]
        held[lane] = restack(jnp.concatenate(right, axis=0).astype(BF16))

    def left_product(n, lane):
        code = items_ref[base + n * UNROLL + lane]
        both = dot(gram_ref[code & (WPLANES - 1)], held[lane])
        for k, slot in enumerate(((code >> 4) & 63, (code >> 10) & 63)):
            cols = slice(k * S, (k + 1) * S)
            acc[slot] = acc[slot] - jnp.concatenate([both[:S, cols], both[S:, cols]], axis=1)

    def step(n, carry):
        for lane in range(UNROLL):
            left_product(n - 1, lane)
            right_product(n, lane)
        return carry

    batches = jnp.maximum((count + UNROLL - 1) // UNROLL, 1)
    for lane in range(UNROLL):
        right_product(0, lane)
    lax.fori_loop(1, batches, step, 0)
    for lane in range(UNROLL):
        left_product(batches - 1, lane)


def both_cycles(
    facets, coef, base, times, count, pos, devices, items_ref, gram_ref, back_ref, half_of, tables, grid, acc, flip, held, keep_ref, send_ref
):
    column_ref, table_ref, loads = tables

    def block(ref, facet, pc):
        first = facet * NP + pc * SIDE
        return ref[first : first + SIDE].reshape(P_SIZE, PAIR)

    def column_pass(cycle, facet, pc):
        part = half_of(cycle, facet, pc)
        turned = jnp.concatenate([part[:, S:], -part[:, :S]], axis=1)
        return dot(column_ref[...], jnp.concatenate([part, turned], axis=0))

    def place(ref, facet, pc, value):
        first = facet * NP + pc * SIDE
        ref[first : first + SIDE] = value.reshape(SIDE, S, PAIR)

    loads[1].wait()
    for facet in range(facets):
        for pc in range(SIDE):
            place(grid, facet, pc, column_pass(0, facet, pc).astype(BF16))
    if loads[0] is not None:
        loads[4].wait()
        acc[:NP] = back_ref[...].astype(F32)
        loads[0].wait()
    degrid_grid(items_ref, base, times, count, gram_ref, grid, acc, held)

    for load in loads[2:4]:
        if load is not None:
            load.wait()
    lane = lax.broadcasted_iota(jnp.int32, (1, PAIR), 1)
    row = lax.broadcasted_iota(jnp.int32, (PAIR, 1), 0)
    sign = jnp.where(lane < S, 1.0, -1.0).astype(F32)
    for facet in range(facets):
        for pc in range(SIDE):
            place(flip, facet, pc, block(acc, facet, pc).astype(BF16))
        for pc in range(SIDE):
            turned = dot(block(flip, facet, SIDE - 1 - pc), wide(table_ref, 0))
            edge = block(flip, facet, (SIDE - pc) % SIDE).astype(F32) * sign
            mirrored = jnp.where(lane % S == 0, edge, turned)
            mirrored_half = mirrored.astype(BF16)
            fresh = column_pass(1, facet, pc)
            own = block(acc, facet, pc)
            parts = []
            for b in range(2):
                mine = slice(b * PAIR, (b + 1) * PAIR)
                other = slice((1 - b) * PAIR, (2 - b) * PAIR)
                swapped = dot(wide(table_ref, 2), mirrored_half[other])
                swapped = jnp.where(row == 0, mirrored[mine], swapped)
                parts.append((fresh[mine] + coef * (own[mine] + swapped)).astype(BF16))
            place(grid, facet, pc, jnp.concatenate(parts, axis=0))
    for facet in range(facets):
        for pc in range(SIDE):
            place(acc, facet, pc, block(back_ref, facet, pc).astype(F32))
    degrid_grid(items_ref, base, times, count, gram_ref, grid, acc, held)

    share, far = S // devices, devices // 2
    for facet in range(facets):
        mixed = [[] for _ in range(SIDE)]
        for pc in range(SIDE):
            r0, r1, r2, r3 = (acc[facet * NP + pc * SIDE + p] for p in range(SIDE))
            even, odd = r0 + r2, r0 - r2
            even_b, odd_b = r1 + r3, r1 - r3
            turned = jnp.concatenate([-odd_b[:, S:], odd_b[:, :S]], axis=1)
            for q, value in enumerate((even + even_b, odd + turned, even - even_b, odd - turned)):
                mixed[q].append(turn_pair(value.astype(BF16)))
        for q in range(SIDE):
            spec = dot(wide(table_ref, 4 + 2 * q), jnp.concatenate(mixed[q], axis=1)).astype(BF16)
            for pc in range(SIDE):
                cols = slice(pc * S, (pc + 1) * S)
                flip[facet * NP + pc * SIDE + q] = jnp.concatenate([spec[:S, cols], spec[S:, cols]], axis=1)
        spec = jnp.concatenate([block(flip, facet, pc) for pc in range(SIDE)], axis=1)
        image = jnp.concatenate([dot(spec, inverse_columns(table_ref, j)) for j in range(0, SIDE, 2)], axis=1).astype(BF16)
        for q in range(SIDE):
            part = image[q * S : (q + 1) * S]
            if send_ref is None:
                keep_ref[facet, q] = part
                continue
            odd, mine = pos & 1, pos >> 1
            for there in range(far):
                zero = part[2 * there * share : (2 * there + 1) * share]
                one = part[(2 * there + 1) * share : (2 * there + 2) * share]
                offset = there ^ mine
                keep_ref[offset, facet, q] = jnp.where(odd == 0, zero, one)
                send_ref[offset, facet, q] = jnp.where(odd == 0, one, zero)


def copies(moves, sems, first=0):
    return [pltpu.make_async_copy(src, dst, sems.at[first + k]) for k, (src, dst) in enumerate(moves)]


def first_kernel(facets, times, rows, coef, devices, outs, *refs):
    pos_ref, items_ref, spot_ref, live_ref = refs[:4]
    wk_hbm, vis_hbm, sky_hbm, row_hbm, column_hbm, table_hbm = refs[4:10]
    gram_hbm, back_hbm, half_hbm, *images = refs[10 : 13 + outs]
    wk_ref, vis_ref, sky_ref, row_ref, column_ref, table_ref = refs[13 + outs : 19 + outs]
    gram_ref, half_ref, back_ref, kern, kern_t, acc, grid, flip, held, sems = refs[19 + outs :]
    moves = [(wk_hbm, wk_ref), (sky_hbm, sky_ref), (row_hbm, row_ref), (vis_hbm, vis_ref), (column_hbm.at[pos_ref[0]], column_ref)]
    loads = copies(moves + [(table_hbm, table_ref)], sems)
    for load in loads[:4]:
        load.start()
    later = facets * NP
    leave = copies(
        [(gram_ref, gram_hbm), (half_ref, half_hbm), (back_ref.at[pl.ds(later, F * NP - later)], back_hbm)], sems, len(loads)
    )
    prepare(
        spot_ref, live_ref, wk_ref, vis_ref, sky_ref, row_ref, gram_ref, half_ref, kern, kern_t, acc, held, loads, leave
    )
    for slot in range(0, F * NP, NP):
        back_ref[slot : slot + NP] = acc[slot : slot + NP].astype(BF16)
    leave[2].start()

    def half_of(cycle, facet, pc):
        first = (cycle * F + facet) * rows
        return half_ref[first : first + rows, pc * PAIR : (pc + 1) * PAIR]

    tables = (column_ref, table_ref, [None, loads[4], None, loads[5]])
    keep_ref, send_ref = images if outs == 2 else (images[0], None)
    both_cycles(
        facets, coef, 0, times, items_ref[2 * times], pos_ref[0], devices, items_ref, gram_ref, back_ref, half_of, tables, grid, acc, flip, held, keep_ref, send_ref
    )
    for out in leave:
        out.wait()


def later_kernel(facet, offset, base, times, part, rows, coef, devices, outs, *refs):
    pos_ref, items_ref = refs[:2]
    gram_hbm, back_hbm, half_hbm, column_hbm, table_hbm = refs[2:7]
    images = refs[7 : 7 + outs]
    gram_ref, back_ref, half_ref, column_ref, table_ref = refs[7 + outs : 12 + outs]
    acc, grid, flip, held, sems = refs[12 + outs :]
    moves = [
        (half_hbm.at[pl.ds(facet * rows, rows)], half_ref.at[0]),
        (column_hbm.at[pos_ref[0]], column_ref),
        (back_hbm.at[pl.ds(offset, NP)], back_ref),
        (gram_hbm, gram_ref),
        (half_hbm.at[pl.ds((F + facet) * rows, rows)], half_ref.at[1]),
    ]
    loads = copies(moves + [(table_hbm, table_ref)], sems)
    for load in loads[:4]:
        load.start()
    for load in loads[4:]:
        load.start()
    loads[0].wait()

    def half_of(cycle, _, pc):
        return half_ref[cycle, :, pc * PAIR : (pc + 1) * PAIR]

    tables = (column_ref, table_ref, [loads[3], loads[1], loads[4], loads[5], loads[2]])
    keep_ref, send_ref = images if outs == 2 else (images[0], None)
    both_cycles(
        1, coef, base, times, items_ref[2 * times + part], pos_ref[0], devices, items_ref, gram_ref, back_ref, half_of, tables, grid, acc, flip, held, keep_ref, send_ref
    )


def tile_lists(codes, stride):
    total = codes.shape[0]
    ids = jnp.arange(total, dtype=jnp.int32)
    before = ids[None, :] < ids[:, None]
    equal = codes[:, None] == codes[None, :]
    again = jnp.sum((equal & before).astype(jnp.int32), axis=1) > 0
    times = jnp.sum(equal.astype(jnp.int32), axis=1)
    group = jnp.where(again, LISTS * WPLANES, codes >> 6)
    rank = jnp.sum(((group[:, None] == group[None, :]) & before).astype(jnp.int32), axis=1)
    planes = jnp.arange(LISTS * WPLANES, dtype=jnp.int32)
    pairs = (jnp.sum((group[None, :] == planes[:, None]).astype(jnp.int32), axis=1) + 1) >> 1
    which = group >> 4
    earlier = (planes[None, :] < group[:, None]) & ((planes[None, :] >> 4) == which[:, None])
    base = jnp.sum(jnp.where(earlier, pairs[None, :], 0), axis=1)
    where = which * stride + base + (rank >> 1)
    slot, plane = codes & 63, (codes >> 6) & (WPLANES - 1)
    even = (rank & 1) == 0
    delta = jnp.where(even, plane + ((slot - SPARE) << 4), (slot - SPARE) << 10)
    size = LISTS * stride
    places = jnp.arange(2 * size + LISTS, dtype=jnp.int32)[:, None]
    is_item, is_times = places < size, places < 2 * size
    goal = jnp.where(is_item, places, jnp.where(is_times, places - size, places - 2 * size))
    hit = (goal == jnp.where(is_times, where[None, :], which[None, :])) & (which < LISTS)[None, :]
    times = jnp.where(even, times, times << 16)
    value = jnp.where(is_item, delta[None, :], jnp.where(is_times, times[None, :], even.astype(jnp.int32)[None, :]))
    dummy = jnp.where(places[:, 0] < size, (SPARE << 4) + (SPARE << 10), 0)
    return dummy + jnp.sum(jnp.where(hit, value, 0), axis=1)


def exchange(value, bits, devices):
    return lax.ppermute(value, "vis", [(i, i ^ bits) for i in range(devices)])


def split_image(image, position, devices):
    share, far = S // devices, devices // 2
    parts = image.reshape(-1, SIDE, far, 2, share, P_SIZE).transpose(3, 2, 0, 1, 4, 5)
    parts = jnp.take(parts, jnp.arange(far) ^ (position >> 1), axis=1)
    odd = position & 1
    return lax.dynamic_index_in_dim(parts, odd, 0, False), lax.dynamic_index_in_dim(parts, 1 - odd, 0, False)


def merge(arrays, first, last):
    parts = [a[first:last].astype(F32) for a in arrays if a.shape[0] >= last]
    return functools.reduce(jnp.add, parts).astype(BF16)


def final_kernel(groups, *refs):
    out_ref, mixed = refs[-2:]
    f = first = 0
    for parts in groups:
        for k in range(refs[first].shape[1]):
            for q in range(SIDE):
                total = functools.reduce(jnp.add, [ref[0, k, q].astype(F32) for ref in refs[first : first + parts]])
                for c in range(SIDE):
                    mixed[f, c, pl.ds(q, total.shape[0], stride=SIDE), :] = total[:, c * S : (c + 1) * S]
            for c in range(SIDE):
                out_ref[f, :, c * S : (c + 1) * S] = mixed[f, c]
            f += 1
        first += parts


def local(model_input, w_kernels, visibilities, tile_facet, tile_patch, tile_wplane, tile_count):
    devices = lax.axis_size("vis")
    position = lax.axis_index("vis").astype(jnp.int32)
    rows = P_SIZE // devices
    weight = math.sqrt(F * NP / (TILE_CAP * devices))
    total = TILE_CAP * devices
    stride = total // 2 + WPLANES // 2 + UNROLL
    coef = GAIN * weight / 2

    slots = tile_facet * NP + (tile_patch & 3) * SIDE + (tile_patch >> 2)
    live = jnp.arange(TILE_CAP, dtype=jnp.int32) < tile_count[0]
    which = jnp.maximum(tile_facet - (FIRST - 1), 0)
    near = jnp.where(tile_facet < FIRST, slots, slots & (NP - 1))
    codes = jnp.where(live, (which << 10) + (tile_wplane << 6) + near, LISTS << 10)
    bits = 1
    while bits < devices:
        codes = jnp.concatenate([codes, exchange(codes, bits, devices)])
        bits *= 2
    items = tile_lists(codes, stride)

    tables = [jnp.asarray(column_tables(devices)), jnp.asarray(small_tables(weight))]
    here = position.reshape(1)
    smem = pl.BlockSpec(memory_space=pltpu.SMEM)
    vmem = pl.BlockSpec(memory_space=pltpu.VMEM)
    hbm = pl.BlockSpec(memory_space=pl.ANY)
    share, far = S // devices, devices // 2
    split = share % 16 == 0

    def image_shapes(facets):
        if split:
            return [jax.ShapeDtypeStruct((far, facets, SIDE, share, P_SIZE), BF16)] * 2
        return [jax.ShapeDtypeStruct((facets, SIDE, S, P_SIZE), BF16)]

    def halves_of(images):
        return images if split else split_image(images[0], position, devices)

    params = pltpu.CompilerParams(vmem_limit_bytes=FIRST_VMEM)
    outs = 2 if split else 1
    half_shape = (2 * F * rows, 2 * P_SIZE)
    gram_shape = (WPLANES, PAIR, PAIR)
    table_scratch = [pltpu.VMEM((P_SIZE, 2 * rows), BF16), pltpu.VMEM(tables[1].shape, BF16)]

    gram, back, half_rows, *images = pl.pallas_call(
        functools.partial(first_kernel, FIRST, LISTS * stride, rows, coef, devices, outs),
        out_shape=[
            jax.ShapeDtypeStruct(gram_shape, BF16),
            jax.ShapeDtypeStruct(((F - FIRST) * NP, S, PAIR), BF16),
            jax.ShapeDtypeStruct(half_shape, BF16),
            *image_shapes(FIRST),
        ],
        in_specs=[smem] * 4 + [hbm] * 6,
        out_specs=[hbm] * 3 + [vmem] * outs,
        scratch_shapes=[
            pltpu.VMEM(w_kernels.shape, BF16),
            pltpu.VMEM(visibilities.shape, BF16),
            pltpu.VMEM((2 * F * rows, P_SIZE), BF16),
            pltpu.VMEM((2 * SIDE, P_SIZE, S), BF16),
            *table_scratch,
            pltpu.VMEM(gram_shape, BF16),
            pltpu.VMEM(half_shape, BF16),
            pltpu.VMEM((F * NP, S, PAIR), BF16),
            pltpu.VMEM(gram_shape, BF16),
            pltpu.VMEM(gram_shape, BF16),
            pltpu.VMEM((F * NP + 1, S, PAIR), F32),
            pltpu.VMEM((FIRST * NP, S, PAIR), BF16),
            pltpu.VMEM((FIRST * NP, S, PAIR), BF16),
            pltpu.VMEM((max(UNROLL, PREP_UNROLL), PAIR, PAIR), BF16),
            pltpu.SemaphoreType.DMA((12,)),
        ],
        compiler_params=params,
        cost_estimate=pl.CostEstimate(flops=30 * 10**9, bytes_accessed=12 * 2**20, transcendentals=0),
        name="first",
    )(
        here,
        items,
        slots + (tile_wplane << 8),
        tile_count,
        w_kernels,
        visibilities,
        model_input.reshape(2 * F * rows, P_SIZE),
        jnp.asarray(row_table()),
        *tables,
    )

    keep, send = halves_of(images)
    arrays = [[keep, exchange(send, 1, devices)]]

    def halve(group, width):
        sent = merge(arrays[group], width, 2 * width)
        return sent, exchange(sent, 2 * width, devices)

    for facet in range(FIRST, F):
        part = facet - FIRST + 1
        if part == 2:
            width = far // 2
            sent, got = halve(0, width)
            here, _ = lax.optimization_barrier((here, sent))
        images = pl.pallas_call(
            functools.partial(
                later_kernel, facet, (facet - FIRST) * NP, part * stride, LISTS * stride, part, rows, coef, devices, outs
            ),
            out_shape=image_shapes(1),
            in_specs=[smem] * 2 + [hbm] * 5,
            out_specs=[vmem] * outs,
            scratch_shapes=[
                pltpu.VMEM(gram_shape, BF16),
                pltpu.VMEM((NP, S, PAIR), BF16),
                pltpu.VMEM((2, rows, 2 * P_SIZE), BF16),
                *table_scratch,
                pltpu.VMEM((SPARE + 1, S, PAIR), F32),
                pltpu.VMEM((NP, S, PAIR), BF16),
                pltpu.VMEM((NP, S, PAIR), BF16),
                pltpu.VMEM((max(UNROLL, PREP_UNROLL), PAIR, PAIR), BF16),
                pltpu.SemaphoreType.DMA((9,)),
            ],
            compiler_params=pltpu.CompilerParams(vmem_limit_bytes=LATER_VMEM),
            cost_estimate=pl.CostEstimate(flops=14 * 10**9, bytes_accessed=6 * 2**20, transcendentals=0),
            name="facet",
        )(here, items, gram, back, half_rows, *tables)
        keep, send = halves_of(images)
        if part == 2:
            send, got = lax.optimization_barrier((send, got))
            arrays[0].append(got)
        arrays.append([keep, exchange(send, 1, devices)])
    arrays[1].append(halve(1, far // 2)[1])
    while width > 1:
        width //= 2
        arrays[0].append(halve(0, width)[1])
        arrays[1].append(halve(1, width)[1])
    for group in range(2, LISTS):
        arrays[group] += [exchange(merge(arrays[group], k, k + 1), 2 * k, devices) for k in range(1, far)]

    def finish(groups, first, facets, before):
        operands = [a for group in groups for a in arrays[group]]
        in_specs = [pl.BlockSpec((1,) + a.shape[1:], lambda i: (0, 0, 0, 0, 0)) for a in operands]
        aliases = {len(operands): 0} if before else {}
        return pl.pallas_call(
            functools.partial(final_kernel, [len(arrays[group]) for group in groups]),
            out_shape=jax.ShapeDtypeStruct((F, rows, P_SIZE), F32),
            grid=(1,),
            in_specs=in_specs + [hbm] * len(before),
            out_specs=pl.BlockSpec((facets, rows, P_SIZE), lambda i: (first // facets, 0, 0)),
            scratch_shapes=[pltpu.VMEM((facets, SIDE, rows, S), F32)],
            input_output_aliases=aliases,
            compiler_params=pltpu.CompilerParams(vmem_limit_bytes=FINAL_VMEM),
            cost_estimate=pl.CostEstimate(flops=10**6, bytes_accessed=2**20, transcendentals=0),
            name="final",
        )(*operands, *before)

    done = finish(range(LISTS - 1), 0, F - 1, [])
    return finish([LISTS - 1], F - 1, 1, [done])


def solution(mesh):
    return jax.shard_map(
        local,
        mesh=mesh,
        in_specs=(
            P(None, "freq", "vis", None),
            P("freq", None, None, None),
            P(("freq", "vis"), None, None, None),
            P(("freq", "vis")),
            P(("freq", "vis")),
            P(("freq", "vis")),
            P(("freq", "vis")),
        ),
        out_specs=P("freq", "vis", None),
        check_vma=False,
    )
```
